32 devices in a mesh: head: 2 (over x), blk: 16 (over z, y, core).
Axes of the slice: x: 2, y: 2, z: 4, core: 2. Of those that a mesh axis runs over, the one named last changes fastest.
Arguments:
- tokens: bfloat16 [4096, 1280], P(('head', 'blk')), may hold values from -6 to 6
- cotangent: bfloat16 [4096, 1280], P(('head', 'blk')), may hold values from -6 to 6
- permutation: int32 [4096], replicated, may hold values from 0 to 4095, as said below
- seq_lengths: int32 [8], replicated, may hold values from 1 to 2048, 4096 in all
- first_gain: bfloat16 [1280], P(('head', 'blk')), may hold values from 0.5 to 1.5
- first_bias: bfloat16 [1280], P(('head', 'blk')), may hold values from -4 to 4
- query_weight: bfloat16 [1280, 1280], P(('head', 'blk')), may hold values from -0.15625 to 0.15625
- query_bias: bfloat16 [1280], P(('head', 'blk')), may hold values from -6 to 6
- key_weight: bfloat16 [1280, 1280], P(('head', 'blk')), may hold values from -0.15625 to 0.15625
- value_weight: bfloat16 [1280, 1280], P(('head', 'blk')), may hold values from -0.15625 to 0.15625
- value_bias: bfloat16 [1280], P(('head', 'blk')), may hold values from -1.5 to 1.5
- output_weight: bfloat16 [1280, 1280], P(('head', 'blk')), may hold values from -1 to 1
- output_bias: bfloat16 [1280], P(('head', 'blk')), may hold values from -4 to 4
- second_gain: bfloat16 [1280], P(('head', 'blk')), may hold values from 0.5 to 1.5
- second_bias: bfloat16 [1280], P(('head', 'blk')), may hold values from -4 to 4
- expand_weight: bfloat16 [1280, 1280], P(('head', 'blk')), may hold values from -0.15625 to 0.15625
- expand_bias: bfloat16 [1280], P(('head', 'blk')), may hold values from -4 to 4
- contract_weight: bfloat16 [1280, 1280], P(('head', 'blk')), may hold values from -0.15625 to 0.15625
- contract_bias: bfloat16 [1280], P(('head', 'blk')), may hold values from -4 to 4
Outputs:
- mixed: bfloat16 [4096, 1280], P(('head', 'blk'))
- grad_tokens: bfloat16 [4096, 1280], P(('head', 'blk'))
- grad_first_gain: float32 [1280], P(('head', 'blk'))
- grad_first_bias: float32 [1280], P(('head', 'blk'))
- grad_query_weight: float32 [1280, 1280], P(('head', 'blk'))
- grad_query_bias: float32 [1280], P(('head', 'blk'))
- grad_key_weight: float32 [1280, 1280], P(('head', 'blk'))
- grad_value_weight: float32 [1280, 1280], P(('head', 'blk'))
- grad_value_bias: float32 [1280], P(('head', 'blk'))
- grad_output_weight: float32 [1280, 1280], P(('head', 'blk'))
- grad_output_bias: float32 [1280], P(('head', 'blk'))
- grad_second_gain: float32 [1280], P(('head', 'blk'))
- grad_second_bias: float32 [1280], P(('head', 'blk'))
- grad_expand_weight: float32 [1280, 1280], P(('head', 'blk'))
- grad_expand_bias: float32 [1280], P(('head', 'blk'))
- grad_contract_weight: float32 [1280, 1280], P(('head', 'blk'))
- grad_contract_bias: float32 [1280], P(('head', 'blk'))
The draws below stay inside these ranges and needn't reach their ends.
Inputs may be any that keep to these rules, and one draw needn't show every extreme that they name: A permutation of all token indices. Cut the initial order and the positions into runs of 128, numbered from 0: a token never leaves its group of runs (runs r with equal r % 16), and each run of positions holds exactly 64 tokens of every run of initial tokens in its group. `seq_lengths`: sequences lie end to end in the initial order.
All inputs are finite; a program needn't handle non-finite values.
Results may differ from the reference program's by a relative error of at most 0.025.
Values may be sent and summed in bfloat16 or wider, within the bound.
A program may use at most 192 MiB of HBM per device.

```python
import math
import jax
import jax.numpy as jnp
import numpy as np
from jax import lax

D = 1280
HEADS = 8
HEAD_DIM = 160
NSEQ = 8
TOK_DEV = 128
TOKENS = 4096
GROUP = 256
PAIR = 64
MOST = 2048


def draw_permutation(key, part):
    groups = TOKENS // GROUP
    runs = GROUP // TOK_DEV
    keys_source = jax.random.split(jax.random.fold_in(key, 11), groups * runs)
    keys_target = jax.random.split(jax.random.fold_in(key, 23), groups * runs)
    shuffle_source = jax.vmap(lambda item: jax.random.permutation(item, TOK_DEV))(keys_source).reshape(groups, runs, TOK_DEV).astype(jnp.int32)
    shuffle_target = jax.vmap(lambda item: jax.random.permutation(item, TOK_DEV))(keys_target).reshape(groups, runs, TOK_DEV).astype(jnp.int32)
    group_ids = jnp.arange(groups, dtype=jnp.int32)[:, None, None, None]
    target_ids = jnp.arange(runs, dtype=jnp.int32)[None, :, None, None]
    source_ids = jnp.arange(runs, dtype=jnp.int32)[None, None, :, None]
    within = jnp.arange(PAIR, dtype=jnp.int32)[None, None, None, :]
    group_full = jnp.broadcast_to(group_ids, (groups, runs, runs, PAIR))
    target_full = jnp.broadcast_to(target_ids, (groups, runs, runs, PAIR))
    source_full = jnp.broadcast_to(source_ids, (groups, runs, runs, PAIR))
    slot_target = source_full * PAIR + within
    slot_source = target_full * PAIR + within
    position = (target_full * groups + group_full) * TOK_DEV + shuffle_target[group_full, target_full, slot_target]
    anchor = (source_full * groups + group_full) * TOK_DEV + shuffle_source[group_full, source_full, slot_source]
    result = jnp.zeros((TOKENS,), jnp.int32)
    return result.at[position.reshape(-1)].set(anchor.reshape(-1))


def block_scale(rng, dims, pieces, least, top_value):
    level, own = 1.0, jax.random.fold_in(rng, 6)
    for axis_at, shards_of in pieces:
        steps = jnp.exp(jax.random.uniform(jax.random.fold_in(own, axis_at), (shards_of,), jnp.float32, least / len(pieces), top_value / len(pieces)))
        level = level * jnp.repeat(steps, dims[axis_at] // shards_of).reshape([-1 if axis == axis_at else 1 for axis in range(len(dims))])
    return level


def split_up(number_of, total, most, skew):
    loads = [(1 << 20) // math.isqrt(grade ** skew) + 1 for grade in range(2, number_of + 1)]
    surplus, counts = total - most - (number_of - 1), [1] * (number_of - 1)
    while surplus > 0:
        free = [i for i in range(number_of - 1) if counts[i] < most]
        pool, left = sum([loads[i] for i in free]), surplus
        for i in free:
            addition = min(most - counts[i], max(1, left * loads[i] // pool), surplus)
            counts[i] = counts[i] + addition
            surplus = surplus - addition
    return np.array([most] + counts)


def uneven_parts(rng, number_of, total, limit, lean):
    if number_of == 2:
        one = jax.random.randint(rng, (), max(1, total - limit), min(limit, total - 1) + 1)
        return jnp.stack([one, total - one])
    tallies = jnp.asarray(split_up(number_of, total, limit, lean), jnp.int32)
    pairs = (number_of - 1) // 2
    giver, receiver = tallies[1:1 + 2 * pairs:2], tallies[2:2 + 2 * pairs:2]
    slack = jnp.minimum(giver - 1, limit - receiver)
    moved = jax.random.randint(jax.random.fold_in(rng, 1), (pairs,), 0, 1 << 20) % (slack + 1)
    tallies = tallies.at[1:1 + 2 * pairs:2].set(giver - moved).at[2:2 + 2 * pairs:2].set(receiver + moved)
    return tallies[jax.random.permutation(jax.random.fold_in(rng, 2), number_of)]


def centred(own_key, dims, width, reach, cuts=(), kind=jnp.bfloat16):
    level = block_scale(own_key, dims, cuts, -0.22, 0.18) if cuts else 1.0
    values = jax.random.normal(own_key, dims, jnp.float32) * width * level
    return jnp.minimum(jnp.maximum(values, -reach), reach).astype(kind)


def setup_inputs(seed: int = 0) -> dict:
    splits = jax.random.split(jax.random.key(seed), 20)
    tokens = centred(splits[0], (TOKENS, D), 1.0, 6.0, ((0, 32),))
    cotangent = centred(splits[1], (TOKENS, D), 1.0, 6.0, ((0, 32),))
    permutation = draw_permutation(jax.random.fold_in(splits[19], 71), 0)
    seq_lengths = uneven_parts(splits[3], NSEQ, TOKENS, MOST, 2).astype(jnp.int32)
    first_gain = jnp.clip(1.0 + 0.1 * jax.random.normal(splits[4], (D,), jnp.float32), 0.5, 1.5).astype(jnp.bfloat16)
    first_bias = centred(splits[5], (D,), 0.3, 4.0, ((0, 32),))
    query_weight = centred(splits[6], (D, D), D ** -0.5, 0.15625, ((0, 32),))
    query_bias = centred(splits[7], (D,), 0.5, 6.0, ((0, 32),))
    key_weight = centred(splits[8], (D, D), D ** -0.5, 0.15625, ((0, 32),))
    value_weight = centred(splits[9], (D, D), D ** -0.5, 0.15625, ((0, 32),))
    value_bias = centred(splits[10], (D,), 0.1, 1.5, ((0, 32),))
    output_weight = centred(splits[11], (D, D), (D // 32) ** -0.5, 1.0, ((0, 32),))
    output_bias = centred(splits[12], (D,), 0.3, 4.0, ((0, 32),))
    second_gain = jnp.clip(1.0 + 0.1 * jax.random.normal(splits[13], (D,), jnp.float32), 0.5, 1.5).astype(jnp.bfloat16)
    second_bias = centred(splits[14], (D,), 0.3, 4.0, ((0, 32),))
    expand_weight = centred(splits[15], (D, D), D ** -0.5, 0.15625, ((0, 32),))
    expand_bias = centred(splits[16], (D,), 0.3, 4.0, ((0, 32),))
    contract_weight = centred(splits[17], (D, D), D ** -0.5, 0.15625, ((0, 32),))
    contract_bias = centred(splits[18], (D,), 0.3, 4.0, ((0, 32),))
    return dict(tokens=tokens, cotangent=cotangent, permutation=permutation, seq_lengths=seq_lengths, first_gain=first_gain, first_bias=first_bias, query_weight=query_weight, query_bias=query_bias, key_weight=key_weight, value_weight=value_weight, value_bias=value_bias, output_weight=output_weight, output_bias=output_bias, second_gain=second_gain, second_bias=second_bias, expand_weight=expand_weight, expand_bias=expand_bias, contract_weight=contract_weight, contract_bias=contract_bias)


@jax.custom_vjp
def low(v):
    return lax.optimization_barrier(v.astype(jnp.bfloat16)).astype(jnp.float32)

@jax.custom_vjp
def low_back(v):
    return v

def low_keep(v):
    return (low(v), None)

def low_pass(kept, grad):
    return (grad,)

def back_keep(v):
    return (v, None)

def back_low(kept, grad):
    return (low(grad),)
low.defvjp(low_keep, low_pass)
low_back.defvjp(back_keep, back_low)

def matmul(left, right):
    return jnp.dot(left, right, precision=lax.Precision.HIGHEST, preferred_element_type=jnp.float32)

def normalize(values, gain, shift):
    centre = lax.optimization_barrier(jnp.mean(values, axis=-1, keepdims=True))
    spread = lax.optimization_barrier(jnp.mean((values - centre) ** 2, axis=-1, keepdims=True))
    return (values - centre) * lax.rsqrt(spread + 1e-05) * gain + shift

def attention(queries, keys, values, segment, initial):
    block = min(512, TOKENS)
    count = TOKENS // block
    keys_heads = keys.reshape(TOKENS, HEADS, HEAD_DIM)
    values_heads = values.reshape(TOKENS, HEADS, HEAD_DIM)

    def one_block(items):
        query_block, segment_block, place_block = items
        query_heads = query_block.reshape(block, HEADS, HEAD_DIM)
        scores = jnp.einsum('qhd,khd->hqk', query_heads, keys_heads, precision=lax.Precision.HIGHEST) * HEAD_DIM ** (-0.5)
        scores = low_back(scores)
        allowed = (segment_block[:, None] == segment[None, :]) & (initial[None, :] <= place_block[:, None])
        scores = jnp.where(allowed[None], scores, -1e+30)
        weights = low(jax.nn.softmax(scores, axis=-1))
        mixed = jnp.einsum('hqk,khd->qhd', weights, values_heads, precision=lax.Precision.HIGHEST)
        return mixed.reshape(block, D)
    outputs = lax.map(jax.checkpoint(one_block), (queries.reshape(count, block, D), segment.reshape(count, block), initial.reshape(count, block)))
    return outputs.reshape(TOKENS, D)

def reference(tokens, cotangent, permutation, seq_lengths, first_gain, first_bias, query_weight, query_bias, key_weight, value_weight, value_bias, output_weight, output_bias, second_gain, second_bias, expand_weight, expand_bias, contract_weight, contract_bias):
    ends = jnp.cumsum(seq_lengths).astype(jnp.int32)
    initial = jnp.arange(TOKENS, dtype=jnp.int32)
    segment = lax.optimization_barrier(jnp.sum((initial[:, None] >= ends[None, :]).astype(jnp.int32), axis=1))

    def forward(inputs, params):
        gain_one, shift_one, weight_query, shift_query, weight_key, weight_value, shift_value, weight_output, shift_output, gain_two, shift_two, weight_expand, shift_expand, weight_contract, shift_contract = params
        hidden = low(normalize(inputs, gain_one, shift_one))
        queries = low_back(low(matmul(hidden, weight_query) + shift_query))
        keys = low_back(low(matmul(hidden, weight_key)))
        values = low_back(low(matmul(hidden, weight_value) + shift_value))
        mixed = low_back(low(attention(queries, keys, values, segment, initial)))
        branch = low_back(matmul(mixed, weight_output) + shift_output)
        middle = inputs + branch
        second = low(normalize(middle, gain_two, shift_two))
        expanded = low_back(matmul(second, weight_expand) + shift_expand)
        activated = low(jax.nn.gelu(expanded, approximate=False))
        result = middle + matmul(activated, weight_contract) + shift_contract
        return result[permutation]
    params = tuple((item.astype(jnp.float32) for item in (first_gain, first_bias, query_weight, query_bias, key_weight, value_weight, value_bias, output_weight, output_bias, second_gain, second_bias, expand_weight, expand_bias, contract_weight, contract_bias)))
    inputs = tokens.astype(jnp.float32)
    outputs, pull = jax.vjp(forward, inputs, params)
    grad_inputs, grads = pull(cotangent.astype(jnp.float32))
    return (outputs.astype(jnp.bfloat16), grad_inputs.astype(jnp.bfloat16), grads[0], grads[1], grads[2], grads[3], grads[4], grads[5], grads[6], grads[7], grads[8], grads[9], grads[10], grads[11], grads[12], grads[13], grads[14])
```

```python
import functools
import jax
import jax.numpy as jnp
from jax import lax
from jax.experimental import pallas as pl
from jax.experimental.pallas import tpu as pltpu
from jax.sharding import PartitionSpec as P

HEAD_DIM = 160
MESH = pl.DeviceIdType.MESH
BF = jnp.bfloat16
F32 = jnp.float32
MB = 1 << 20


def nn(a, b):
    return lax.dot_general(a, b, (((1,), (0,)), ((), ())), preferred_element_type=F32)


def nt(a, b):
    return lax.dot_general(a, b, (((1,), (1,)), ((), ())), preferred_element_type=F32)


def tn(a, b):
    return lax.dot_general(a, b, (((0,), (0,)), ((), ())), preferred_element_type=F32)


def stats(v):
    centre = jnp.mean(v, axis=-1, keepdims=True)
    off = v - centre
    spread = jnp.mean(off * off, axis=-1, keepdims=True)
    r = lax.rsqrt(spread + 1e-05)
    return off * r, r


def block_kernel(
    tok, cot, perm2, lens, wpre, fpre,
    mixed_out, gtok_out, fout, wout,
    T, H, W, KV, Q, O, F, G, R0, R1, R2, R3, FA, FR,
    wr, wasm, fr, colb, vec, bias,
    LS, ST, A, As, C, RES, MID, N2, RR, EX, H2, ACT, CI, DE, GB, DOs, DOr,
    DK, DV, DQ, DKVr, DKVQ, U, UR, UZ, VR, VS, DW, DWr, DWz, DWh, WOr,
    ss, rs,
):
    h = lax.axis_index("head")
    b = lax.axis_index("blk")
    z = lax.div(b, 4)
    y = lax.rem(lax.div(b, 2), 2)
    c = lax.rem(b, 2)
    sib = 1 - c
    hx = 1 - h
    yx = 1 - y
    t = z * 2 + c
    first = c == 0
    p1h = jnp.where(first, hx, h)
    p1y = jnp.where(first, y, yx)
    p2h = jnp.where(first, h, hx)
    p2y = jnp.where(first, yx, y)

    def dev(hh, zz, yy, cc):
        return (hh, zz * 4 + yy * 2 + cc)

    zs = [lax.rem(z + k, 4) for k in range(4)]
    zr = [lax.rem(z + 4 - k, 4) for k in range(4)]
    SIB = dev(h, z, y, sib)
    P1 = dev(p1h, z, p1y, c)
    P2 = dev(p2h, z, p2y, c)
    XP = dev(hx, z, y, c)
    YP = dev(h, z, yx, c)
    DP = dev(hx, z, yx, c)
    plane = [(h, yx, YP), (hx, y, XP), (hx, yx, DP)]

    count = [0]

    def desc(src, dst, device):
        i = count[0]
        count[0] += 1
        return pltpu.make_async_remote_copy(
            src_ref=src, dst_ref=dst, send_sem=ss.at[i], recv_sem=rs.at[i],
            device_id=device, device_id_type=MESH,
        )

    pending = []

    def send(src, dst, device):
        cp = desc(src, dst, device)
        cp.start()
        pending.append(cp)
        return cp

    def left(cps):
        for cp in cps:
            cp.wait_send()
        keep = [cp for cp in pending if not any(cp is one for one in cps)]
        pending[:] = keep

    bar = pltpu.get_barrier_semaphore()
    for k in range(1, 4):
        pl.semaphore_signal(bar, inc=1, device_id=dev(h, zs[k], y, c), device_id_type=MESH)
        pl.semaphore_signal(bar, inc=1, device_id=dev(h, zs[k], y, sib), device_id_type=MESH)
    for peer in (SIB, XP, YP, DP):
        pl.semaphore_signal(bar, inc=1, device_id=peer, device_id_type=MESH)
    pl.semaphore_wait(bar, 10)

    wa = send(wpre.at[sib], wr, SIB)
    fa = send(fpre.at[sib], fr, SIB)
    tz = [send(tok, T.at[z, c], dev(h, zs[k], y, c)) for k in range(1, 4)]
    ts = [send(tok, T.at[z, c], SIB)]
    cx = send(cot, C.at[h], XP)
    T[z, c] = tok[...]
    C[h] = cot[...]

    wa.wait_recv()
    wasm[:, pl.ds(pl.multiple_of(c * 40, 8), 40), :] = wpre[c]
    wasm[:, pl.ds(pl.multiple_of(sib * 40, 8), 40), :] = wr[...]
    for k in range(4):
        DWz[k] = wasm[k].astype(BF)
    W[h, z, y] = DWz[z]
    wz = [send(DWz.at[zs[k]], W.at[h, z, y], dev(h, zs[k], y, c)) for k in range(1, 4)]
    fa.wait_recv()
    FA[:, pl.ds(pl.multiple_of(c * 40, 8), 40), :] = fpre[c]
    FA[:, pl.ds(pl.multiple_of(sib * 40, 8), 40), :] = fr[...]
    for w in range(3):
        F[w, c, h, z, y] = FA[w].astype(BF)
    for cp in wz:
        cp.wait_recv()
    wp = [send(W.at[h, :, y], W.at[h, :, y], d) for (_, _, d) in plane]
    fz = [
        [send(F.at[w, c, h, z, y], F.at[w, c, h, z, y], dev(h, zs[k], y, c)) for k in range(1, 4)]
        for w in range(3)
    ]
    for k in range(1, 4):
        tz[k - 1].wait_recv()
        ts.append(send(T.at[zr[k], c], T.at[zr[k], c], SIB))
    for cp in wp:
        cp.wait_recv()

    def tcol(hh, _):
        colb[pl.ds(pl.multiple_of(hh * 640, 128), 640), :] = (
            W[hh, :, :, :, 384:512].reshape(640, 128).astype(F32)
        )
        return 0

    lax.fori_loop(0, 2, tcol, 0)
    colb[1280:1408, :] = jnp.zeros((128, 128), F32)
    vec[...] = jnp.transpose(colb[0:1280, :])[96:112, :]
    mine = jnp.transpose(colb[pl.ds(pl.multiple_of(t * 160, 8), 256), :])
    bias[...] = jnp.zeros((8, 512), F32)
    bias[0:1, 160:320] = mine[99:100, 0:160]
    bias[0:1, 320:480] = mine[98:99, 0:160]

    lane256 = lax.broadcasted_iota(jnp.int32, (256, 256), 1)

    kv_y, kv_x, kv_d = [], [], []
    for k in range(4):
        zt = zr[k]
        ts[k].wait_recv()

        def norm(i, _):
            rows = pl.ds(pl.multiple_of(lax.rem(i, 2) * 64, 64), 64)
            n, _ = stats(T[zt, lax.div(i, 2), rows].astype(F32))
            H[zt, pl.ds(pl.multiple_of(i * 64, 64), 64)] = (n * vec[0:1, :] + vec[1:2, :]).astype(BF)
            return 0

        lax.fori_loop(0, 4, norm, 0)
        kvq = nn(H[zt], W[...].reshape(1280, 512)) + bias[0:1, :]
        KV[h, zt, y] = kvq[:, 0:384].astype(BF)
        qr = pltpu.roll(kvq[:, 256:512], 192, 1)
        Q[zt] = jnp.where(lane256 < 160, qr, 0.0).astype(BF)
        src = KV.at[h, zt, y]
        kv_y.append(send(src, KV.at[h, zt, y], YP))
        cpx = desc(src, KV.at[h, zt, y], XP)
        cpd = desc(src, KV.at[h, zt, y], DP)
        kv_x.append(cpx)
        kv_d.append(cpd)

        @pl.when(h == 0)
        def _():
            cpx.start()
            cpd.start()

    f1, f2a, fs = [], [], []
    for w in range(3):
        for cp in fz[w]:
            cp.wait_recv()
        own = F.at[w, c, h, :, y]
        f1.append(send(own, own, P1))
        f2a.append(send(own, own, P2))
        fs.append(send(own, own, SIB))

    for cp in kv_y:
        cp.wait_recv()

    @pl.when(h == 1)
    def _():
        for cp in kv_x + kv_d:
            cp.wait_recv()

    f2b = []
    for w in range(3):
        f1[w].wait_recv()
        got = F.at[w, c, p1h, :, p1y]
        f2b.append(send(got, got, P2))
        fs.append(send(got, got, SIB))

    scale = HEAD_DIM ** -0.5
    ends = []
    run = 0
    for e in range(8):
        run = run + lens[e]
        ends.append(run)

    def seg_of(pos):
        s = jnp.zeros_like(pos)
        for e in range(7):
            s = jnp.where(pos >= ends[e], ends[e], s)
        return s

    def rowpos(zt):
        return (h * 8 + zt * 2 + y) * 256

    def fwd_tile(zt, _):
        qt = h * 8 + zt * 2 + y
        lo = jnp.maximum(qt - 8, 0)
        num = qt + 1 - lo
        qpos = qt * 256 + lax.broadcasted_iota(jnp.int32, (256, 1), 0)
        seg = seg_of(qpos)
        q = Q[zt]

        def score(j, ml):
            m, l = ml
            kt = lo + j
            kh, kz, ky = lax.div(kt, 8), lax.rem(lax.div(kt, 2), 4), lax.rem(kt, 2)
            s = nt(q, KV[kh, kz, ky, :, 0:256]) * scale
            kpos = kt * 256 + lax.broadcasted_iota(jnp.int32, (256, 256), 1)
            ok = (kpos >= seg) & (kpos <= qpos)
            s = jnp.where(ok, s, -1e30)
            mn = jnp.maximum(m, jnp.max(s, axis=-1, keepdims=True))
            f = jnp.exp(m - mn)
            p = jnp.where(ok, jnp.exp(s - mn), 0.0)
            O[zt] = O[zt] * f + nn(p.astype(BF), KV[kh, kz, ky, :, 128:384])
            return mn, l * f + jnp.sum(p, axis=-1, keepdims=True)

        O[zt] = jnp.zeros((256, 256), F32)
        start = (jnp.full((256, 1), -1e30, F32), jnp.zeros((256, 1), F32))
        m, l = lax.fori_loop(0, num, score, start)
        o = O[zt] / l
        O[zt] = o
        LS[zt] = jnp.broadcast_to(m + jnp.log(l), (256, 128))
        a = pltpu.roll(o, 224, 1).astype(BF)
        As[zt] = a.reshape(2, 128, 256)
        return 0

    asend = []
    for k in (1, 2, 3, 0):
        zt = zs[k]
        fwd_tile(zt, 0)
        for cc in (c, sib):
            if k == 0 and cc is c:
                continue
            asend.append(send(As.at[zt, cc], A.at[t], dev(h, zt, y, cc)))
    A[t] = As[z, c]

    for w in range(3):
        f2a[w].wait_recv()
        got = F.at[w, c, p2h, :, p2y]
        fs.append(send(got, got, SIB))
        f2b[w].wait_recv()
        got = F.at[w, c, hx, :, yx]
        fs.append(send(got, got, SIB))
    for cp in asend:
        cp.wait_recv()
    for cp in fs:
        cp.wait_recv()

    VR[...] = jnp.zeros((128, 1280), F32)

    def halves(fn):
        def run_half(i, _):
            fn(i, pl.ds(pl.multiple_of(i * 640, 128), 640))
            return 0

        lax.fori_loop(0, 2, run_half, 0)

    def out_half(i, cols):
        acc = tok[:, cols].astype(F32) + vec[4:5, cols]
        for e in range(8):
            acc += nn(A[e, :, 0:160], F[0, i, e // 4, e % 4].reshape(160, 640))
        MID[:, cols] = acc

    halves(out_half)

    def norm2(i, _):
        rows = pl.ds(pl.multiple_of(i * 32, 32), 32)
        n2, r2 = stats(MID[rows, :])
        N2[rows, :] = n2
        RR[rows, :] = jnp.broadcast_to(r2, (32, 128))
        H2[rows, :] = (n2 * vec[5:6, :] + vec[6:7, :]).astype(BF)
        return 0

    lax.fori_loop(0, 4, norm2, 0)

    def exp_half(i, cols):
        ex = nn(H2[...], F[1, i].reshape(1280, 640)) + vec[7:8, cols]
        phi = 0.5 * (1.0 + lax.erf(ex * (0.5**0.5)))
        ACT[:, cols] = (ex * phi).astype(BF)
        EX[:, cols] = phi + ex * jnp.exp(-0.5 * ex * ex) * 0.3989422804014327

    halves(exp_half)

    def con_half(i, cols):
        res = MID[:, cols] + nn(ACT[...], F[2, i].reshape(1280, 640)) + vec[8:9, cols]
        RES[h, :, cols] = res.astype(BF)

    halves(con_half)
    rx = send(RES.at[h], RES.at[h], XP)

    cx.wait_recv()
    i_sub = lax.broadcasted_iota(jnp.int32, (128, 128), 0)
    mine0 = (h * 16 + b) * 128
    oh0 = jnp.where(perm2[0:1, :] == mine0 + i_sub, 1.0, 0.0).astype(BF)
    oh1 = jnp.where(perm2[1:2, :] == mine0 + i_sub, 1.0, 0.0).astype(BF)

    def cot_half(i, cols):
        ci = nn(oh0, C[0, :, cols]) + nn(oh1, C[1, :, cols])
        CI[:, cols] = ci.astype(BF)
        VR[104:105, cols] = jnp.sum(ci, axis=0, keepdims=True)

    halves(cot_half)

    def act_half(i, cols):
        f0, f1w = F[2, 0, i].reshape(640, 640), F[2, 1, i].reshape(640, 640)
        dact = nt(CI[:, 0:640], f0) + nt(CI[:, 640:1280], f1w)
        de = (dact * EX[:, cols]).astype(BF)
        DE[:, cols] = de
        VR[103:104, cols] = jnp.sum(de.astype(F32), axis=0, keepdims=True)

    halves(act_half)

    def outer(left, right, dst):
        def one(i, _):
            hh, half = lax.div(i, 2), lax.rem(i, 2)
            g = tn(
                left[:, pl.ds(pl.multiple_of(hh * 640, 128), 640)],
                right[:, pl.ds(pl.multiple_of(half * 640, 128), 640)],
            )
            dst[half, hh] = g.astype(BF).reshape(4, 2, 80, 640)
            return 0

        lax.fori_loop(0, 4, one, 0)

    Gw = [F.at[1], F.at[2], G]
    ra = [None] * 3

    def rs_a(w):
        ra[w] = send(Gw[w].at[sib], R0.at[w], SIB)

    outer(ACT, CI, G)
    rs_a(2)

    def back_half(i, cols):
        f0, f1w = F[1, 0, i].reshape(640, 640), F[1, 1, i].reshape(640, 640)
        EX[:, cols] = nt(DE[:, 0:640], f0) + nt(DE[:, 640:1280], f1w)

    halves(back_half)

    def norm2_back(i, _):
        rows = pl.ds(pl.multiple_of(i * 32, 32), 32)
        dh2, n2 = EX[rows, :], N2[rows, :]
        VR[101:102, :] += jnp.sum(dh2 * n2, axis=0, keepdims=True)
        VR[102:103, :] += jnp.sum(dh2, axis=0, keepdims=True)
        wv = dh2 * vec[5:6, :]
        dmid = CI[rows, :].astype(F32) + RR[rows, 0:1] * (
            wv - jnp.mean(wv, axis=-1, keepdims=True) - n2 * jnp.mean(wv * n2, axis=-1, keepdims=True)
        )
        MID[rows, :] = dmid
        gb = dmid.astype(BF)
        GB[rows, :] = gb
        VR[100:101, :] += jnp.sum(gb.astype(F32), axis=0, keepdims=True)
        return 0

    lax.fori_loop(0, 4, norm2_back, 0)
    left(asend)
    As[...] = jnp.zeros((4, 2, 128, 256), BF)

    def dattn(e, _):
        eh, ez = lax.div(e, 4), lax.rem(e, 4)
        da = nt(GB[:, 0:640], F[0, 0, eh, ez].reshape(160, 640)) + nt(
            GB[:, 640:1280], F[0, 1, eh, ez].reshape(160, 640)
        )
        As[lax.div(e, 2), lax.rem(e, 2), :, 0:160] = da.astype(BF)
        return 0

    lax.fori_loop(0, 8, dattn, 0)
    dos = []
    for k in range(4):
        for cc in (c, sib):
            if k == 0 and cc is c:
                continue
            dos.append(send(As.at[zs[k], cc], DOr.at[z, c], dev(h, zs[k], y, cc)))
    DOr[z, c] = As[z, c]

    left([cp for row in fz for cp in row] + f1 + f2a + f2b + fs)
    outer(H2, DE, F.at[2])
    rs_a(1)

    def outo(e, _):
        def one(half, _):
            g = tn(A[e, :, 0:160], GB[:, pl.ds(pl.multiple_of(half * 640, 128), 640)])
            F[1, half, lax.div(e, 4), lax.rem(e, 4)] = g.astype(BF).reshape(2, 80, 640)
            return 0

        lax.fori_loop(0, 2, one, 0)
        return 0

    lax.fori_loop(0, 8, outo, 0)
    rs_a(0)

    rx.wait_recv()
    pm = jnp.where(h == 0, perm2[0:1, :], perm2[1:2, :])
    om0 = jnp.where(pm == b * 128 + i_sub, 1.0, 0.0).astype(BF)
    om1 = jnp.where(pm == (16 + b) * 128 + i_sub, 1.0, 0.0).astype(BF)

    def mix_half(i, cols):
        mixed_out[:, cols] = (tn(om0, RES[0, :, cols]) + tn(om1, RES[1, :, cols])).astype(BF)

    halves(mix_half)

    def add_into(dst_at, others):
        def one(i, _):
            ref, idx = dst_at(i)
            total = ref[idx].astype(F32)
            for other in others:
                total += other(i).astype(F32)
            ref[idx] = total.astype(BF)
            return 0

        return one

    r1, r2s, r3, r4 = [None] * 3, [None] * 3, [None] * 3, [None] * 3

    def rs_b(w):
        ra[w].wait_recv()
        gw = Gw[w]

        def one(i, _):
            ih, iz = lax.div(i, 4), lax.rem(i, 4)
            gw[c, ih, iz] = (gw[c, ih, iz].astype(F32) + R0[w, ih, iz].astype(F32)).astype(BF)
            return 0

        lax.fori_loop(0, 8, one, 0)
        r1[w] = [
            send(gw.at[c, hx, :, yx], R1.at[w, 1], P2),
            send(gw.at[c, p2h, :, p2y], R1.at[w, 0], P2),
        ]

    def rs_c(w):
        gw = Gw[w]
        for cp in r1[w]:
            cp.wait_recv()

        def one(i, _):
            gw[c, p1h, i, p1y] = (gw[c, p1h, i, p1y].astype(F32) + R1[w, 1, i].astype(F32)).astype(BF)
            return 0

        lax.fori_loop(0, 4, one, 0)
        r2s[w] = send(gw.at[c, p1h, :, p1y], R2.at[w], P1)

    def rs_d(w):
        gw = Gw[w]
        r2s[w].wait_recv()

        def two(i, _):
            gw[c, h, i, y] = (
                gw[c, h, i, y].astype(F32) + R1[w, 0, i].astype(F32) + R2[w, i].astype(F32)
            ).astype(BF)
            return 0

        lax.fori_loop(0, 4, two, 0)
        r3[w] = [send(gw.at[c, h, zs[k], y], R3.at[w, k - 1], dev(h, zs[k], y, c)) for k in range(1, 4)]

    def rs_e(w):
        gw = Gw[w]
        total = gw[c, h, z, y].astype(F32)
        for k in range(1, 4):
            r3[w][k - 1].wait_recv()
            total += R3[w, k - 1].astype(F32)
        FA[w] = total
        r4[w] = send(FA.at[w, pl.ds(pl.multiple_of(sib * 40, 8), 40)], FR.at[w], SIB)

    def rs_f(w):
        r4[w].wait_recv()
        fout[w, :, pl.ds(pl.multiple_of(c * 640, 128), 640)] = FA[w, pl.ds(pl.multiple_of(c * 40, 8), 40)]
        fout[w, :, pl.ds(pl.multiple_of(sib * 640, 128), 640)] = FR[w]

    for w in (2, 1, 0):
        rs_b(w)

    for cp in dos:
        cp.wait_recv()
    left(kv_y)

    @pl.when(h == 0)
    def _():
        for cp in kv_x + kv_d:
            cp.wait_send()

    lane128 = lax.broadcasted_iota(jnp.int32, (256, 128), 1)

    def prep(zt, _):
        do = pltpu.roll(DOr[zt].reshape(256, 256).astype(F32), 32, 1)
        DOs[zt] = do.astype(BF)
        agree = jnp.sum(do * O[zt], axis=-1, keepdims=True)
        both = jnp.where(lane128 == 0, LS[zt], jnp.where(lane128 == 1, agree, 0.0))
        ST[zt] = jnp.transpose(both)[0:8, :]
        DQ[zt] = jnp.zeros((256, 256), F32)
        return 0

    lax.fori_loop(0, 4, prep, 0)

    def key_tile(kh, kz, ky):
        kt = kh * 8 + kz * 2 + ky
        base = kt - h * 8 - y
        zlo = jnp.maximum(lax.div(base + 33, 2) - 16, 0)
        zhi = jnp.minimum(lax.div(base + 40, 2) - 16, 3) + 1
        DK[...] = jnp.zeros((256, 256), F32)
        DV[...] = jnp.zeros((256, 256), F32)
        kk = KV[kh, kz, ky, :, 0:256]
        vv = KV[kh, kz, ky, :, 128:384]
        kpos = kt * 256 + lax.broadcasted_iota(jnp.int32, (256, 1), 0)

        def one(zq, _):
            q = Q[zq]
            do = DOs[zq]
            qpos = (h * 8 + zq * 2 + y) * 256 + lax.broadcasted_iota(jnp.int32, (1, 256), 1)
            seg = seg_of(qpos)
            st = ST[zq]
            s = nt(kk, q) * scale
            ok = (kpos >= seg) & (kpos <= qpos)
            p = jnp.where(ok, jnp.exp(jnp.where(ok, s - st[0:1, :], 0.0)), 0.0)
            dp = nt(vv, do)
            ds = (p * (dp - st[1:2, :])).astype(BF)
            DK[...] += nn(ds, q)
            DV[...] += nn(p.astype(BF), do)
            DQ[zq] += tn(ds, kk)
            return 0

        lax.fori_loop(zlo, zhi, one, 0)
        dk = DK[...] * scale
        dv = DV[...]
        KV[kh, kz, ky, :, 0:128] = dk[:, 0:128].astype(BF)
        KV[kh, kz, ky, :, 128:256] = (dk[:, 128:256] + dv[:, 0:128]).astype(BF)
        KV[kh, kz, ky, :, 256:384] = dv[:, 128:256].astype(BF)

    dkx, dkd, dky = [], [], []
    for kz in range(4):
        dkd.append(desc(KV.at[0, kz, yx], DKVr.at[2, kz], dev(0, z, yx, c)))
        dkx.append(desc(KV.at[0, kz, y], DKVr.at[1, kz], dev(0, z, y, c)))

    @pl.when(h == 1)
    def _():
        for kz in range(4):
            key_tile(0, kz, yx)
            dkd[kz].start()
            key_tile(0, kz, y)
            dkx[kz].start()

    for w in (2, 1, 0):
        rs_c(w)
    for kz in range(4):
        key_tile(h, kz, yx)
        dky.append(send(KV.at[h, kz, yx], DKVr.at[0, kz], YP))
    for w in (2, 1, 0):
        rs_d(w)

    def own_tile(kz, _):
        key_tile(h, kz, y)
        return 0

    lax.fori_loop(0, 4, own_tile, 0)
    for w in (2, 1, 0):
        rs_e(w)

    for cp in dky:
        cp.wait_recv()

    @pl.when(h == 0)
    def _():
        for cp in dkx + dkd:
            cp.wait_recv()

    def join(zt, _):
        dkv = KV[h, zt, y].astype(F32) + DKVr[0, zt].astype(F32)
        dkv = jnp.where(h == 0, dkv + (DKVr[1, zt].astype(F32) + DKVr[2, zt].astype(F32)), dkv)
        dq = pltpu.roll(jnp.where(lane256 < 160, DQ[zt] * scale, 0.0), 64, 1)
        DKVQ[zt, :, 0:256] = dkv[:, 0:256].astype(BF)
        DKVQ[zt, :, 256:384] = (dkv[:, 256:384] + dq[:, 0:128]).astype(BF)
        DKVQ[zt, :, 384:512] = dq[:, 128:256].astype(BF)
        return 0

    lax.fori_loop(0, 4, join, 0)

    VS[...] = jnp.zeros((128, 512), F32)

    def first_grad(zt, _):
        d = DKVQ[zt]
        VS[98:99, :] += jnp.sum(d.astype(F32), axis=0, keepdims=True)

        def u_half(i, cols):
            u = nt(d, W[i].reshape(640, 512))
            VR[97:98, cols] += jnp.sum(u, axis=0, keepdims=True)
            U[zt, :, :, cols] = u.astype(BF).reshape(2, 128, 640)

        halves(u_half)

        def gain(i, _):
            rows = pl.ds(pl.multiple_of(lax.rem(i, 2) * 64, 64), 64)
            n, _ = stats(T[zt, lax.div(i, 2), rows].astype(F32))
            VR[96:97, :] += jnp.sum(U[zt, lax.div(i, 2), rows].astype(F32) * n, axis=0, keepdims=True)
            return 0

        lax.fori_loop(0, 4, gain, 0)
        return 0

    us = []
    for k in range(4):
        first_grad(zs[k], 0)
        us.append(send(U.at[zs[k], sib], UR.at[zs[k]], SIB))

    VS[99:100, :] = VS[98:99, :]
    vst = jnp.transpose(VS[...])
    vlane = lax.broadcasted_iota(jnp.int32, (160, 128), 1)
    colb[0:1280, :] = jnp.transpose(VR[...])
    rows = pl.ds(pl.multiple_of(t * 160, 8), 160)
    colb[rows, :] += jnp.where(vlane == 98, vst[320:480, :], 0.0) + jnp.where(
        vlane == 99, vst[160:320, :], 0.0
    )

    uz = []
    for k in (1, 2, 3, 0):
        us[k].wait_recv()
        zt = zs[k]
        U[zt, c] = (U[zt, c].astype(F32) + UR[zt].astype(F32)).astype(BF)
        if k:
            uz.append(send(U.at[zt, c], UZ.at[k - 1], dev(h, zt, y, c)))

    def head_grad(hh, _):
        g = tn(
            H[:, :, pl.ds(pl.multiple_of(hh * 640, 128), 640)].reshape(1024, 640),
            DKVQ[...].reshape(1024, 512),
        )
        DW[hh, :, :, :, 0:384] = g[:, 0:384].astype(BF).reshape(4, 2, 80, 384)
        last = g[:, 384:512] + colb[pl.ds(pl.multiple_of(hh * 640, 128), 640), :]
        DW[hh, :, :, :, 384:512] = last.astype(BF).reshape(4, 2, 80, 128)
        return 0

    lax.fori_loop(0, 2, head_grad, 0)
    dwp = [send(DW.at[ph, :, py], DWr.at[i], d) for i, (ph, py, d) in enumerate(plane)]
    for cp in dwp:
        cp.wait_recv()
    left(wz)
    for k in range(4):
        DWz[k] = (
            DW[h, k, y].astype(F32) + DWr[0, k].astype(F32) + DWr[1, k].astype(F32) + DWr[2, k].astype(F32)
        ).astype(BF)
    dwz = [send(DWz.at[zs[k]], DWh.at[z], dev(h, zs[k], y, c)) for k in range(1, 4)]
    DWh[z] = DWz[z]

    for cp in uz:
        cp.wait_recv()

    def last_rows(i, _):
        rows = pl.ds(pl.multiple_of(i * 32, 32), 32)
        u = U[z, c, rows].astype(F32)
        for k in range(3):
            u += UZ[k, rows].astype(F32)
        n, r = stats(tok[rows, :].astype(F32))
        wv = u * vec[0:1, :]
        gt = MID[rows, :] + r * (
            wv - jnp.mean(wv, axis=-1, keepdims=True) - n * jnp.mean(wv * n, axis=-1, keepdims=True)
        )
        gtok_out[rows, :] = gt.astype(BF)
        return 0

    lax.fori_loop(0, 4, last_rows, 0)

    for cp in dwz:
        cp.wait_recv()
    for k in range(4):
        wasm[k] = DWh[k].astype(F32)
    wr[...] = wasm[:, pl.ds(pl.multiple_of(sib * 40, 8), 40), :]
    wo = send(wr, WOr, SIB)
    wout[c] = wasm[:, pl.ds(pl.multiple_of(c * 40, 8), 40), :]
    for w in (2, 1, 0):
        rs_f(w)
    wo.wait_recv()
    wout[sib] = WOr[...]

    for cp in pending:
        cp.wait_send()

    @pl.when(h == 1)
    def _():
        for cp in dkx + dkd:
            cp.wait_send()

    assert count[0] <= NSEM, count[0]


NSEM = 192


def fast_local(
    tokens, cotangent, permutation, seq_lengths, first_gain, first_bias, query_weight, query_bias,
    key_weight, value_weight, value_bias, output_weight, output_bias, second_gain, second_bias,
    expand_weight, expand_bias, contract_weight, contract_bias,
):
    b = lax.axis_index("blk")
    perm2 = lax.dynamic_index_in_dim(permutation.reshape(2, 16, 128), b, 1, keepdims=False)
    vectors = [first_gain, first_bias, query_bias, value_bias, output_bias, second_gain, second_bias,
               expand_bias, contract_bias]
    vcol = jnp.stack(vectors, axis=1)
    vcol = jnp.pad(vcol, ((0, 0), (0, 23)))
    wpre = jnp.concatenate(
        [key_weight.reshape(40, 8, 160), value_weight.reshape(40, 8, 160), query_weight.reshape(40, 8, 160),
         jnp.broadcast_to(vcol[:, None, :], (40, 8, 32))], axis=2,
    )
    wpre = wpre.reshape(40, 4, 2, 512).transpose(2, 1, 0, 3).astype(F32)
    fpre = jnp.stack([output_weight, expand_weight, contract_weight]).reshape(3, 40, 2, 640)
    fpre = fpre.transpose(2, 0, 1, 3).astype(F32)

    vm = pltpu.VMEM
    fshape = (2, 2, 4, 2, 80, 640)
    scratch = dict(
        T=vm((4, 2, 128, 1280), BF), H=vm((4, 256, 1280), BF), W=vm((2, 4, 2, 80, 512), BF),
        KV=vm((2, 4, 2, 256, 384), BF), Q=vm((4, 256, 256), BF), O=vm((4, 256, 256), F32),
        F=vm((3,) + fshape, BF), G=vm(fshape, BF), R0=vm((3, 2, 4, 2, 80, 640), BF),
        R1=vm((3, 2, 4, 80, 640), BF), R2=vm((3, 4, 80, 640), BF), R3=vm((3, 3, 80, 640), BF),
        FA=vm((3, 80, 640), F32), FR=vm((3, 40, 640), F32),
        wr=vm((4, 40, 512), F32), wasm=vm((4, 80, 512), F32),
        fr=vm((3, 40, 640), F32),
        colb=vm((1408, 128), F32), vec=vm((16, 1280), F32), bias=vm((8, 512), F32),
        LS=vm((4, 256, 128), F32), ST=vm((4, 8, 256), F32),
        A=vm((8, 128, 256), BF), As=vm((4, 2, 128, 256), BF), C=vm((2, 128, 1280), BF),
        RES=vm((2, 128, 1280), BF), MID=vm((128, 1280), F32), N2=vm((128, 1280), F32), RR=vm((128, 128), F32),
        EX=vm((128, 1280), F32), H2=vm((128, 1280), BF), ACT=vm((128, 1280), BF),
        CI=vm((128, 1280), BF), DE=vm((128, 1280), BF), GB=vm((128, 1280), BF),
        DOs=vm((4, 256, 256), BF), DOr=vm((4, 2, 128, 256), BF),
        DK=vm((256, 256), F32), DV=vm((256, 256), F32), DQ=vm((4, 256, 256), F32),
        DKVr=vm((3, 4, 256, 384), BF), DKVQ=vm((4, 256, 512), BF), U=vm((4, 2, 128, 1280), BF),
        UR=vm((4, 128, 1280), BF), UZ=vm((3, 128, 1280), BF), VR=vm((128, 1280), F32),
        VS=vm((128, 512), F32), DW=vm((2, 4, 2, 80, 512), BF),
        DWr=vm((3, 4, 80, 512), BF), DWz=vm((4, 80, 512), BF), DWh=vm((4, 80, 512), BF),
        WOr=vm((4, 40, 512), F32),
        ss=pltpu.SemaphoreType.DMA((NSEM,)), rs=pltpu.SemaphoreType.DMA((NSEM,)),
    )
    vspec = pl.BlockSpec(memory_space=pltpu.VMEM)
    mixed, gtok, fout, wout = pl.pallas_call(
        block_kernel,
        out_shape=(
            jax.ShapeDtypeStruct((128, 1280), BF), jax.ShapeDtypeStruct((128, 1280), BF),
            jax.ShapeDtypeStruct((3, 40, 1280), F32), jax.ShapeDtypeStruct((2, 4, 40, 512), F32),
        ),
        in_specs=[vspec, vspec, vspec, pl.BlockSpec(memory_space=pltpu.SMEM), vspec, vspec],
        out_specs=(vspec,) * 4,
        scratch_shapes=list(scratch.values()),
        compiler_params=pltpu.CompilerParams(
            collective_id=0, has_side_effects=True, vmem_limit_bytes=63 * MB,
        ),
        cost_estimate=pl.CostEstimate(flops=12_000_000_000, bytes_accessed=6_000_000, transcendentals=5_000_000),
        name="block",
    )(tokens, cotangent, perm2, seq_lengths, wpre, fpre)
    heads = wout.transpose(2, 1, 0, 3).reshape(40, 8, 512)
    gk = heads[:, :, 0:160].reshape(40, 1280)
    gv = heads[:, :, 160:320].reshape(40, 1280)
    gq = heads[:, :, 320:480].reshape(40, 1280)
    vg = jnp.sum(heads[:, :, 480:489], axis=1)
    return (
        mixed, gtok, vg[:, 0], vg[:, 1], gq, vg[:, 2], gk, gv, vg[:, 3], fout[0], vg[:, 4], vg[:, 5],
        vg[:, 6], fout[1], vg[:, 7], fout[2], vg[:, 8],
    )


def shifted(array, axis, by):
    length = lax.axis_size(axis)
    return lax.ppermute(array, axis, [(i, (i + by) % length) for i in range(length)])


def normalize(values, gain, shift):
    centre = jnp.mean(values, axis=-1, keepdims=True)
    spread = jnp.mean((values - centre) ** 2, axis=-1, keepdims=True)
    return (values - centre) * lax.rsqrt(spread + 1e-05) * gain + shift


def exact_gelu(values):
    return jax.nn.gelu(values, approximate=False)


def layout_initial(permutation, blk_source, width, blk_count, head_count):
    rows = jnp.arange(width * head_count, dtype=jnp.int32)
    places = (rows // width * blk_count + blk_source) * width + rows % width
    return jnp.take(permutation, places)


def segment_of(initial, ends):
    return jnp.sum((initial[:, None] >= ends[None, :]).astype(jnp.int32), axis=1)


def permitted(query_orig, key_orig, ends):
    same = segment_of(query_orig, ends)[:, None] == segment_of(key_orig, ends)[None, :]
    return same & (key_orig[None, :] <= query_orig[:, None])


def outer_sum(left, right):
    return lax.dot_general(
        left, right, (((0,), (0,)), ((), ())), preferred_element_type=jnp.float32
    )


def back_product(left, right):
    return lax.dot_general(
        left, right, (((1,), (1,)), ((), ())), preferred_element_type=jnp.float32
    )


def block_terms(
    query_block,
    grad_block,
    log_block,
    agree_block,
    query_orig,
    key_block,
    value_block,
    key_orig,
    ends,
    scale,
):
    allowed = permitted(query_orig, key_orig, ends)
    scores = (
        jnp.einsum("qhd,khd->hqk", query_block, key_block, preferred_element_type=jnp.float32)
        * scale
    )
    weights = jnp.exp(jnp.where(allowed[None], scores - log_block[..., None], -1e30))
    value_term = jnp.einsum(
        "hqk,qhd->khd", weights.astype(jnp.bfloat16), grad_block, preferred_element_type=jnp.float32
    )
    product = jnp.einsum(
        "qhd,khd->hqk", grad_block, value_block, preferred_element_type=jnp.float32
    )
    score_grad = (weights * (product - agree_block[..., None])).astype(jnp.bfloat16)
    query_term = jnp.einsum(
        "hqk,khd->qhd", score_grad, key_block, preferred_element_type=jnp.float32
    )
    key_term = jnp.einsum(
        "hqk,qhd->khd", score_grad, query_block, preferred_element_type=jnp.float32
    )
    return (query_term, key_term, value_term)


def local(
    tokens,
    cotangent,
    permutation,
    seq_lengths,
    first_gain,
    first_bias,
    query_weight,
    query_bias,
    key_weight,
    value_weight,
    value_bias,
    output_weight,
    output_bias,
    second_gain,
    second_bias,
    expand_weight,
    expand_bias,
    contract_weight,
    contract_bias,
):
    width = tokens.shape[0]
    blk_count = lax.axis_size("blk")
    head_count = lax.axis_size("head")
    blk_index = lax.axis_index("blk")
    flat_index = lax.axis_index("head") * blk_count + blk_index
    count = seq_lengths.shape[0]
    before = jnp.arange(count)[None, :] <= jnp.arange(count)[:, None]
    ends = jnp.sum(jnp.where(before, seq_lengths[None, :], 0), axis=1)
    total = permutation.shape[0]
    numbers = jnp.arange(total, dtype=jnp.int32)
    inverse = jnp.zeros((total,), jnp.int32).at[permutation].set(numbers)
    local_rows = jnp.arange(width, dtype=jnp.int32)
    first_row = flat_index * width
    going = lax.dynamic_slice_in_dim(inverse, first_row, width)
    order_source = jnp.argsort(going)
    arriving = lax.dynamic_slice_in_dim(permutation, first_row, width)
    order_target = jnp.argsort(arriving // width // blk_count * width + local_rows)
    undo_target = jnp.argsort(order_target)
    undo_source = jnp.argsort(order_source)
    received = lax.all_to_all(
        jnp.take(tokens, order_source, axis=0), "head", split_axis=0, concat_axis=0, tiled=True
    )
    inputs = jnp.take(received, undo_target, axis=0).astype(jnp.float32)
    vectors = jnp.stack(
        [
            first_gain,
            first_bias,
            query_bias,
            value_bias,
            output_bias,
            second_gain,
            second_bias,
            expand_bias,
            contract_bias,
        ]
    )
    query_full, key_full, value_full, output_full, expand_full, contract_full, vector_stack = (
        lax.all_gather(query_weight, ("head", "blk"), axis=0, tiled=True),
        lax.all_gather(key_weight, ("head", "blk"), axis=0, tiled=True),
        lax.all_gather(value_weight, ("head", "blk"), axis=0, tiled=True),
        lax.all_gather(output_weight, ("head", "blk"), axis=0, tiled=True),
        lax.all_gather(expand_weight, ("head", "blk"), axis=0, tiled=True),
        lax.all_gather(contract_weight, ("head", "blk"), axis=0, tiled=True),
        lax.all_gather(vectors, ("head", "blk"), axis=1, tiled=True),
    )
    vector_full = vector_stack.astype(jnp.float32)
    first_hidden = normalize(inputs, vector_full[0], vector_full[1]).astype(jnp.bfloat16)
    queries = (
        jnp.dot(first_hidden, query_full, preferred_element_type=jnp.float32) + vector_full[2]
    ).astype(jnp.bfloat16)
    keys = jnp.dot(first_hidden, key_full, preferred_element_type=jnp.float32).astype(jnp.bfloat16)
    values = (
        jnp.dot(first_hidden, value_full, preferred_element_type=jnp.float32) + vector_full[3]
    ).astype(jnp.bfloat16)
    head_queries, head_keys, head_values = (
        lax.all_to_all(queries, "head", split_axis=1, concat_axis=0, tiled=True),
        lax.all_to_all(keys, "head", split_axis=1, concat_axis=0, tiled=True),
        lax.all_to_all(values, "head", split_axis=1, concat_axis=0, tiled=True),
    )
    rows_here = width * head_count
    feature_here = head_queries.shape[1]
    heads_here = feature_here // HEAD_DIM
    scale = HEAD_DIM ** (-0.5)
    query_initial = layout_initial(permutation, blk_index, width, blk_count, head_count)
    shaped_queries = head_queries.reshape(rows_here, heads_here, HEAD_DIM)
    shaped_keys = head_keys.reshape(rows_here, heads_here, HEAD_DIM)
    shaped_values = head_values.reshape(rows_here, heads_here, HEAD_DIM)
    start_state = (
        jnp.full((heads_here, rows_here), -1e30, jnp.float32),
        jnp.zeros((heads_here, rows_here), jnp.float32),
        jnp.zeros((heads_here, rows_here, HEAD_DIM), jnp.float32),
    )
    carry = start_state
    key_piece = lax.all_gather(head_keys, "blk", axis=0, tiled=True)
    value_piece = lax.all_gather(head_values, "blk", axis=0, tiled=True)
    pieces = key_piece.shape[0] // rows_here
    key_blocks = key_piece.reshape(pieces, rows_here, heads_here, HEAD_DIM)
    value_blocks = value_piece.reshape(pieces, rows_here, heads_here, HEAD_DIM)

    def visit(state, item):
        key_block, value_block, offset = item
        running, total_sum, gathered = state
        key_initial = layout_initial(permutation, offset, width, blk_count, head_count)
        allowed = permitted(query_initial, key_initial, ends)
        scores = (
            jnp.einsum(
                "qhd,khd->hqk", shaped_queries, key_block, preferred_element_type=jnp.float32
            )
            * scale
        )
        scores = jnp.where(allowed[None], scores, -1e30)
        newest = jnp.maximum(running, jnp.max(scores, axis=-1))
        factor = jnp.exp(running - newest)
        exponent = jnp.where(allowed[None], jnp.exp(scores - newest[..., None]), 0.0)
        total_sum = factor * total_sum + jnp.sum(exponent, axis=-1)
        gathered = factor[..., None] * gathered + jnp.einsum(
            "hqk,khd->hqd",
            exponent.astype(jnp.bfloat16),
            value_block,
            preferred_element_type=jnp.float32,
        )
        return ((newest, total_sum, gathered), None)

    carry, unused = lax.scan(
        visit, carry, (key_blocks, value_blocks, jnp.arange(pieces, dtype=jnp.int32))
    )
    running, total_sum, gathered = carry
    attended = gathered / total_sum[..., None]
    log_total = running + jnp.log(total_sum)
    attended_rows = jnp.transpose(attended, (1, 0, 2)).reshape(rows_here, feature_here)
    merged = lax.all_to_all(
        attended_rows.astype(jnp.bfloat16), "head", split_axis=0, concat_axis=1, tiled=True
    )
    middle = (
        inputs + jnp.dot(merged, output_full, preferred_element_type=jnp.float32) + vector_full[4]
    )
    second_hidden = normalize(middle, vector_full[5], vector_full[6]).astype(jnp.bfloat16)
    expanded = (
        jnp.dot(second_hidden, expand_full, preferred_element_type=jnp.float32) + vector_full[7]
    )
    activated = exact_gelu(expanded).astype(jnp.bfloat16)
    result = (
        middle
        + jnp.dot(activated, contract_full, preferred_element_type=jnp.float32)
        + vector_full[8]
    )
    grad_contract = outer_sum(activated, cotangent)
    grad_contract_bias = jnp.sum(cotangent.astype(jnp.float32), axis=0)
    grad_activated = back_product(cotangent, contract_full)
    unused_value, gelu_pull = jax.vjp(exact_gelu, expanded)
    grad_expanded = gelu_pull(grad_activated)[0].astype(jnp.bfloat16)
    grad_expand = outer_sum(second_hidden, grad_expanded)
    grad_expand_bias = jnp.sum(grad_expanded.astype(jnp.float32), axis=0)
    grad_second = back_product(grad_expanded, expand_full)
    unused_second, second_pull = jax.vjp(normalize, middle, vector_full[5], vector_full[6])
    grad_middle_norm, grad_second_gain, grad_second_bias = second_pull(grad_second)
    grad_middle = cotangent.astype(jnp.float32) + grad_middle_norm
    grad_branch = grad_middle.astype(jnp.bfloat16)
    grad_output = outer_sum(merged, grad_branch)
    grad_output_bias = jnp.sum(grad_branch.astype(jnp.float32), axis=0)
    grad_merged = back_product(grad_branch, output_full).astype(jnp.bfloat16)
    head_grad = lax.all_to_all(grad_merged, "head", split_axis=1, concat_axis=0, tiled=True)
    shaped_grad = head_grad.reshape(rows_here, heads_here, HEAD_DIM)
    agreement = jnp.einsum("qhd,hqd->hq", shaped_grad.astype(jnp.float32), attended)
    zero_rows = jnp.zeros((rows_here, heads_here, HEAD_DIM), jnp.float32)

    def key_turn(turn, state):
        moving_keys, moving_values, key_total, value_total, query_total = state
        source = (blk_index - turn) % blk_count
        key_orig = layout_initial(permutation, source, width, blk_count, head_count)
        query_term, key_term, value_term = block_terms(
            shaped_queries,
            shaped_grad,
            log_total,
            agreement,
            query_initial,
            moving_keys,
            moving_values,
            key_orig,
            ends,
            scale,
        )
        moving_keys, moving_values = shifted((moving_keys, moving_values), "blk", 1)
        key_total, value_total = (
            shifted((key_total + key_term).astype(jnp.bfloat16), "blk", 1).astype(jnp.float32),
            shifted((value_total + value_term).astype(jnp.bfloat16), "blk", 1).astype(jnp.float32),
        )
        return (moving_keys, moving_values, key_total, value_total, query_total + query_term)

    final_state = lax.fori_loop(
        0, blk_count, key_turn, (shaped_keys, shaped_values, zero_rows, zero_rows, zero_rows)
    )
    key_grad_heads = final_state[2]
    value_grad_heads = final_state[3]
    query_grad_heads = final_state[4]
    query_grad_rows = (
        (query_grad_heads * scale).astype(jnp.bfloat16).reshape(rows_here, feature_here)
    )
    key_grad_rows = (key_grad_heads * scale).astype(jnp.bfloat16).reshape(rows_here, feature_here)
    value_grad_rows = value_grad_heads.astype(jnp.bfloat16).reshape(rows_here, feature_here)
    grad_queries, grad_keys, grad_values = (
        lax.all_to_all(query_grad_rows, "head", split_axis=0, concat_axis=1, tiled=True),
        lax.all_to_all(key_grad_rows, "head", split_axis=0, concat_axis=1, tiled=True),
        lax.all_to_all(value_grad_rows, "head", split_axis=0, concat_axis=1, tiled=True),
    )
    grad_query = outer_sum(first_hidden, grad_queries)
    grad_key = outer_sum(first_hidden, grad_keys)
    grad_value = outer_sum(first_hidden, grad_values)
    grad_query_bias = jnp.sum(grad_queries.astype(jnp.float32), axis=0)
    grad_value_bias = jnp.sum(grad_values.astype(jnp.float32), axis=0)
    grad_first = (
        back_product(grad_queries, query_full)
        + back_product(grad_keys, key_full)
        + back_product(grad_values, value_full)
    )
    unused_first, first_pull = jax.vjp(normalize, inputs, vector_full[0], vector_full[1])
    grad_inputs_norm, grad_first_gain, grad_first_bias = first_pull(grad_first)
    grad_inputs = (grad_middle + grad_inputs_norm).astype(jnp.bfloat16)
    vector_grads = jnp.stack(
        [
            grad_first_gain,
            grad_first_bias,
            grad_query_bias,
            grad_value_bias,
            grad_output_bias,
            grad_second_gain,
            grad_second_bias,
            grad_expand_bias,
            grad_contract_bias,
        ]
    )
    summed = (
        lax.psum_scatter(grad_query, ("head", "blk"), scatter_dimension=0, tiled=True),
        lax.psum_scatter(grad_key, ("head", "blk"), scatter_dimension=0, tiled=True),
        lax.psum_scatter(grad_value, ("head", "blk"), scatter_dimension=0, tiled=True),
        lax.psum_scatter(grad_output, ("head", "blk"), scatter_dimension=0, tiled=True),
        lax.psum_scatter(grad_expand, ("head", "blk"), scatter_dimension=0, tiled=True),
        lax.psum_scatter(grad_contract, ("head", "blk"), scatter_dimension=0, tiled=True),
        lax.psum_scatter(vector_grads, ("head", "blk"), scatter_dimension=1, tiled=True),
    )
    vector_shares = summed[6]
    returned = lax.all_to_all(
        jnp.take(grad_inputs, order_target, axis=0), "head", split_axis=0, concat_axis=0, tiled=True
    )
    grad_tokens = jnp.take(returned, undo_source, axis=0)
    return (
        result.astype(jnp.bfloat16),
        grad_tokens,
        vector_shares[0],
        vector_shares[1],
        summed[0],
        vector_shares[2],
        summed[1],
        summed[2],
        vector_shares[3],
        summed[3],
        vector_shares[4],
        vector_shares[5],
        vector_shares[6],
        summed[4],
        vector_shares[7],
        summed[5],
        vector_shares[8],
    )


def solution(mesh):
    return jax.shard_map(
        fast_local if mesh.shape["head"] == 2 and mesh.shape["blk"] == 16 else local,
        mesh=mesh,
        in_specs=(
            P(("head", "blk"), None),
            P(("head", "blk"), None),
            P(),
            P(),
            P(("head", "blk")),
            P(("head", "blk")),
            P(("head", "blk"), None),
            P(("head", "blk")),
            P(("head", "blk"), None),
            P(("head", "blk"), None),
            P(("head", "blk")),
            P(("head", "blk"), None),
            P(("head", "blk")),
            P(("head", "blk")),
            P(("head", "blk")),
            P(("head", "blk"), None),
            P(("head", "blk")),
            P(("head", "blk"), None),
            P(("head", "blk")),
        ),
        out_specs=(
            P(("head", "blk"), None),
            P(("head", "blk"), None),
            P(("head", "blk")),
            P(("head", "blk")),
            P(("head", "blk"), None),
            P(("head", "blk")),
            P(("head", "blk"), None),
            P(("head", "blk"), None),
            P(("head", "blk")),
            P(("head", "blk"), None),
            P(("head", "blk")),
            P(("head", "blk")),
            P(("head", "blk")),
            P(("head", "blk"), None),
            P(("head", "blk")),
            P(("head", "blk"), None),
            P(("head", "blk")),
        ),
        check_vma=False,
    )
```

```python
import functools
import jax
import jax.numpy as jnp
from jax import lax
from jax.experimental import pallas as pl
from jax.experimental.pallas import tpu as pltpu
from jax.sharding import PartitionSpec as P

HEAD_DIM = 160
MESH = pl.DeviceIdType.MESH
BF = jnp.bfloat16
F32 = jnp.float32
MB = 1 << 20


def nn(a, b):
    return lax.dot_general(a, b, (((1,), (0,)), ((), ())), preferred_element_type=F32)


def nt(a, b):
    return lax.dot_general(a, b, (((1,), (1,)), ((), ())), preferred_element_type=F32)


def tn(a, b):
    return lax.dot_general(a, b, (((0,), (0,)), ((), ())), preferred_element_type=F32)


def stats(v):
    centre = jnp.mean(v, axis=-1, keepdims=True)
    off = v - centre
    spread = jnp.mean(off * off, axis=-1, keepdims=True)
    r = lax.rsqrt(spread + 1e-05)
    return off * r, r


def block_kernel(
    tok, cot, perm, lens, vcol, wq, wk, wv, wts0, wts1, wts2,
    mixed_out, gtok_out, gq, gk, gv, fo0, fo1, fo2, vgo,
    WP, FP, T, H, W, KV, Q, O, F, G, R0, R1, R2, R3, FA, FR,
    wr, wasm, fr, colb, vec, bias,
    LS, ST, A, As, C, RES, MID, N2, RR, EX, H2, ACT, CI, DE, GB, DOs, DOr,
    DK, DV, DQ, DKVr, DKVQ, U, UR, UZ, VR, VS, DW, DWr, DWz, DWh, WOr,
    ss, rs, lss, lrs,
):
    h = lax.axis_index("head")
    b = lax.axis_index("blk")
    z = lax.div(b, 4)
    y = lax.rem(lax.div(b, 2), 2)
    c = lax.rem(b, 2)
    sib = 1 - c
    hx = 1 - h
    yx = 1 - y
    t = z * 2 + c
    first = c == 0
    p1h = jnp.where(first, hx, h)
    p1y = jnp.where(first, y, yx)
    p2h = jnp.where(first, h, hx)
    p2y = jnp.where(first, yx, y)

    def dev(hh, zz, yy, cc):
        return (hh, zz * 4 + yy * 2 + cc)

    zs = [lax.rem(z + k, 4) for k in range(4)]
    zr = [lax.rem(z + 4 - k, 4) for k in range(4)]
    SIB = dev(h, z, y, sib)
    P1 = dev(p1h, z, p1y, c)
    P2 = dev(p2h, z, p2y, c)
    XP = dev(hx, z, y, c)
    YP = dev(h, z, yx, c)

    count = [0]

    def desc(src, dst, device):
        i = count[0]
        count[0] += 1
        return pltpu.make_async_remote_copy(
            src_ref=src, dst_ref=dst, send_sem=ss.at[i], recv_sem=rs.at[i],
            device_id=device, device_id_type=MESH,
        )

    pending = []

    def send(src, dst, device):
        cp = desc(src, dst, device)
        cp.start()
        pending.append(cp)
        return cp

    def left(cps):
        for cp in cps:
            cp.wait_send()
        keep = [cp for cp in pending if not any(cp is one for one in cps)]
        pending[:] = keep

    fout = (fo0, fo1, fo2)
    for e in range(8):
        for i, src in enumerate((wk, wv, wq)):
            WP[e % 2, e // 2, :, i * 160:(i + 1) * 160] = src[:, e * 160:(e + 1) * 160].astype(F32)
        WP[e % 2, e // 2, :, 480:512] = vcol[...]
    for w, src in enumerate((wts0, wts1, wts2)):
        for half in range(2):
            FP[half, w] = src[:, half * 640:(half + 1) * 640].astype(F32)

    bar = pltpu.get_barrier_semaphore()
    for k in range(1, 4):
        pl.semaphore_signal(bar, inc=1, device_id=dev(h, zs[k], y, c), device_id_type=MESH)
        pl.semaphore_signal(bar, inc=1, device_id=dev(h, zs[k], y, sib), device_id_type=MESH)
    for peer in (SIB, XP, YP):
        pl.semaphore_signal(bar, inc=1, device_id=peer, device_id_type=MESH)
    pl.semaphore_wait(bar, 9)

    up, down = z < 3, z > 0
    UP = dev(h, jnp.minimum(z + 1, 3), y, c)
    DOWN = dev(h, jnp.maximum(z - 1, 0), y, c)
    order = [
        z,
        jnp.where(z == 0, 1, jnp.where(z == 3, 2, jnp.where(z == 1, 0, 3))),
        jnp.where(z == 0, 2, jnp.where(z == 3, 1, jnp.where(z == 1, 2, 1))),
        jnp.where(z == 0, 3, jnp.where(z == 3, 0, jnp.where(z == 1, 3, 0))),
    ]

    def tcopy(src, zt, si, device):
        return pltpu.make_async_remote_copy(
            src_ref=src, dst_ref=T.at[zt, c], send_sem=lss.at[si], recv_sem=lrs.at[zt],
            device_id=device, device_id_type=MESH,
        )

    ts = []

    def token_start():
        pl.when(up)(tcopy(tok, z, 0, UP).start)
        pl.when(down)(tcopy(tok, z, 1, DOWN).start)
        ts.append(send(tok, T.at[z, c], SIB))

    def token_step(k):
        zt = order[k]
        here = T.at[zt, c]
        tcopy(here, zt, 0, UP).wait_recv()
        pl.when((zt < z) & up)(tcopy(here, zt, 1 + k, UP).start)
        pl.when((zt > z) & down)(tcopy(here, zt, 1 + k, DOWN).start)
        ts.append(send(here, here, SIB))

    def token_end():
        pl.when(up)(tcopy(tok, z, 0, UP).wait_send)
        pl.when(down)(tcopy(tok, z, 1, DOWN).wait_send)
        for k in range(1, 4):
            zt = order[k]
            here = T.at[zt, c]
            pl.when((zt < z) & up)(tcopy(here, zt, 1 + k, UP).wait_send)
            pl.when((zt > z) & down)(tcopy(here, zt, 1 + k, DOWN).wait_send)

    wa = send(WP.at[sib], wr, SIB)
    fa = send(FP.at[sib], fr, SIB)
    T[z, c] = tok[...]
    C[h] = cot[...]

    wa.wait_recv()
    wasm[:, pl.ds(pl.multiple_of(c * 40, 8), 40), :] = WP[c]
    wasm[:, pl.ds(pl.multiple_of(sib * 40, 8), 40), :] = wr[...]
    for k in range(4):
        DWz[k] = wasm[k].astype(BF)
    W[h, z, y] = DWz[z]
    wz = [send(DWz.at[zs[k]], W.at[h, z, y], dev(h, zs[k], y, c)) for k in range(1, 4)]
    cx = send(cot, C.at[h], XP)
    fa.wait_recv()
    FA[:, pl.ds(pl.multiple_of(c * 40, 8), 40), :] = FP[c]
    FA[:, pl.ds(pl.multiple_of(sib * 40, 8), 40), :] = fr[...]
    for w in range(3):
        F[w, c, h, z, y] = FA[w].astype(BF)

    fz = [None] * 3

    def f_line(w):
        own = F.at[w, c, h, z, y]
        fz[w] = [send(own, own, dev(h, zs[k], y, c)) for k in range(1, 4)]

    f1, f2a, f2b, fs = [None] * 3, [None] * 3, [None] * 3, []

    def f_plane(w):
        for cp in fz[w]:
            cp.wait_recv()
        own = F.at[w, c, h, :, y]
        f1[w] = send(own, own, P1)
        f2a[w] = send(own, own, P2)
        one = send(own, own, SIB)
        fs.append(one)
        fs_w[id(one)] = w

    def f_forward(w):
        f1[w].wait_recv()
        got = F.at[w, c, p1h, :, p1y]
        f2b[w] = send(got, got, P2)
        one = send(got, got, SIB)
        fs.append(one)
        fs_w[id(one)] = w

    flast = [None] * 3
    fs_w = {}

    def f_last(w):
        f2a[w].wait_recv()
        got = F.at[w, c, p2h, :, p2y]
        one = send(got, got, SIB)
        f2b[w].wait_recv()
        got = F.at[w, c, hx, :, yx]
        flast[w] = [one, send(got, got, SIB)]

    f_line(0)
    token_start()
    for cp in wz:
        cp.wait_recv()
    own = W.at[h, :, y]
    w1 = send(own, own, P1)
    w2 = send(own, own, P2)
    w1.wait_recv()
    got = W.at[p1h, :, p1y]
    w3 = send(got, got, P2)
    f_plane(0)
    w2.wait_recv()
    w3.wait_recv()

    def tcol(hh, _):
        colb[pl.ds(pl.multiple_of(hh * 640, 128), 640), :] = (
            W[hh, :, :, :, 384:512].reshape(640, 128).astype(F32)
        )
        return 0

    lax.fori_loop(0, 2, tcol, 0)
    colb[1280:1408, :] = jnp.zeros((128, 128), F32)
    vec[...] = jnp.transpose(colb[0:1280, :])[96:112, :]
    mine = jnp.transpose(colb[pl.ds(pl.multiple_of(t * 160, 8), 256), :])
    bias[...] = jnp.zeros((8, 512), F32)
    bias[0:1, 160:320] = mine[99:100, 0:160]
    bias[0:1, 320:480] = mine[98:99, 0:160]

    lane256 = lax.broadcasted_iota(jnp.int32, (256, 256), 1)

    kv1, kv2, kv3 = [], [], []

    def project(k):
        zt = order[k]
        ts[k].wait_recv()

        def norm(i, _):
            rows = pl.ds(pl.multiple_of(lax.rem(i, 2) * 64, 64), 64)
            n, _ = stats(T[zt, lax.div(i, 2), rows].astype(F32))
            H[zt, pl.ds(pl.multiple_of(i * 64, 64), 64)] = (n * vec[0:1, :] + vec[1:2, :]).astype(BF)
            return 0

        lax.fori_loop(0, 4, norm, 0)
        kvq = nn(H[zt], W[...].reshape(1280, 512)) + bias[0:1, :]
        KV[h, zt, y] = kvq[:, 0:384].astype(BF)
        qr = pltpu.roll(kvq[:, 256:512], 192, 1)
        Q[zt] = jnp.where(lane256 < 160, qr, 0.0).astype(BF)
        src = KV.at[h, zt, y]
        kv1.append(send(src, src, P1))
        kv2.append(send(src, src, P2))

    def kv_forward(k):
        kv1[k].wait_recv()
        got = KV.at[p1h, order[k], p1y]
        kv3.append(send(got, got, P2))

    project(0)
    token_step(1)
    f_forward(0)
    project(1)
    kv_forward(0)
    token_step(2)
    project(2)
    kv_forward(1)
    token_step(3)
    f_line(1)
    project(3)
    kv_forward(2)
    kv_forward(3)
    f_line(2)
    f_plane(1)
    for cp in kv2 + kv3:
        cp.wait_recv()

    scale = HEAD_DIM ** -0.5
    ends = []
    run = 0
    for e in range(8):
        run = run + lens[e]
        ends.append(run)

    def seg_of(pos):
        s = jnp.zeros_like(pos)
        for e in range(7):
            s = jnp.where(pos >= ends[e], ends[e], s)
        return s

    def rowpos(zt):
        return (h * 8 + zt * 2 + y) * 256

    def fwd_tile(zt, _):
        qt = h * 8 + zt * 2 + y
        lo = jnp.maximum(qt - 8, 0)
        num = qt + 1 - lo
        qpos = qt * 256 + lax.broadcasted_iota(jnp.int32, (256, 1), 0)
        seg = seg_of(qpos)
        q = Q[zt]

        def score(j, ml):
            m, l = ml
            kt = lo + j
            kh, kz, ky = lax.div(kt, 8), lax.rem(lax.div(kt, 2), 4), lax.rem(kt, 2)
            s = nt(q, KV[kh, kz, ky, :, 0:256]) * scale
            kpos = kt * 256 + lax.broadcasted_iota(jnp.int32, (256, 256), 1)
            ok = (kpos >= seg) & (kpos <= qpos)
            s = jnp.where(ok, s, -1e30)
            mn = jnp.maximum(m, jnp.max(s, axis=-1, keepdims=True))
            f = jnp.exp(m - mn)
            p = jnp.where(ok, jnp.exp(s - mn), 0.0)
            O[zt] = O[zt] * f + nn(p.astype(BF), KV[kh, kz, ky, :, 128:384])
            return mn, l * f + jnp.sum(p, axis=-1, keepdims=True)

        O[zt] = jnp.zeros((256, 256), F32)
        start = (jnp.full((256, 1), -1e30, F32), jnp.zeros((256, 1), F32))
        m, l = lax.fori_loop(0, num, score, start)
        o = O[zt] / l
        O[zt] = o
        LS[zt] = jnp.broadcast_to(m + jnp.log(l), (256, 128))
        a = pltpu.roll(o, 224, 1).astype(BF)
        As[zt] = a.reshape(2, 128, 256)
        return 0

    asend = []
    for k in (1, 2, 3, 0):
        zt = zs[k]
        fwd_tile(zt, 0)
        for cc in (c, sib):
            if k == 0 and cc is c:
                continue
            asend.append(send(As.at[zt, cc], A.at[t], dev(h, zt, y, cc)))
        if k == 1:
            f_plane(2)
        if k == 2:
            f_forward(1)
        if k == 3:
            f_forward(2)
    A[t] = As[z, c]

    f_last(0)
    for cp in asend:
        cp.wait_recv()

    def f_done(w):
        for cp in flast[w] + fs[2 * w:2 * w + 2]:
            cp.wait_recv()

    fs.sort(key=lambda cp: fs_w[id(cp)])
    f_done(0)
    f_last(1)

    VR[...] = jnp.zeros((128, 1280), F32)

    def halves(fn):
        def run_half(i, _):
            fn(i, pl.ds(pl.multiple_of(i * 640, 128), 640))
            return 0

        lax.fori_loop(0, 2, run_half, 0)

    def out_half(i, cols):
        acc = tok[:, cols].astype(F32) + vec[4:5, cols]
        for e in range(8):
            acc += nn(A[e, :, 0:160], F[0, i, e // 4, e % 4].reshape(160, 640))
        MID[:, cols] = acc

    halves(out_half)

    def norm2(i, _):
        rows = pl.ds(pl.multiple_of(i * 32, 32), 32)
        n2, r2 = stats(MID[rows, :])
        N2[rows, :] = n2
        RR[rows, :] = jnp.broadcast_to(r2, (32, 128))
        H2[rows, :] = (n2 * vec[5:6, :] + vec[6:7, :]).astype(BF)
        return 0

    lax.fori_loop(0, 4, norm2, 0)

    def exp_half(i, cols):
        ex = nn(H2[...], F[1, i].reshape(1280, 640)) + vec[7:8, cols]
        phi = 0.5 * (1.0 + lax.erf(ex * (0.5**0.5)))
        ACT[:, cols] = (ex * phi).astype(BF)
        EX[:, cols] = phi + ex * jnp.exp(-0.5 * ex * ex) * 0.3989422804014327

    f_done(1)
    f_last(2)
    halves(exp_half)

    cx.wait_recv()
    i_sub = lax.broadcasted_iota(jnp.int32, (128, 128), 0)
    mine0 = (h * 16 + b) * 128
    pr0, pr1 = perm[pl.ds(b, 1), :], perm[pl.ds(16 + b, 1), :]
    oh0 = jnp.where(pr0 == mine0 + i_sub, 1.0, 0.0).astype(BF)
    oh1 = jnp.where(pr1 == mine0 + i_sub, 1.0, 0.0).astype(BF)

    def cot_half(i, cols):
        ci = nn(oh0, C[0, :, cols]) + nn(oh1, C[1, :, cols])
        CI[:, cols] = ci.astype(BF)
        VR[104:105, cols] = jnp.sum(ci, axis=0, keepdims=True)

    halves(cot_half)

    def outer(left, right, dst):
        def one(i, _):
            hh, half = lax.div(i, 2), lax.rem(i, 2)
            g = tn(
                left[:, pl.ds(pl.multiple_of(hh * 640, 128), 640)],
                right[:, pl.ds(pl.multiple_of(half * 640, 128), 640)],
            )
            dst[half, hh] = g.astype(BF).reshape(4, 2, 80, 640)
            return 0

        lax.fori_loop(0, 4, one, 0)

    Gw = [F.at[1], F.at[2], G]
    ra = [None] * 3

    def rs_a(w):
        ra[w] = send(Gw[w].at[sib], R0.at[w], SIB)

    r1, r2s, r3, r4 = [None] * 3, [None] * 3, [None] * 3, [None] * 3

    def rs_b(w):
        ra[w].wait_recv()
        gw = Gw[w]

        def one(i, _):
            ih, iz = lax.div(i, 4), lax.rem(i, 4)
            gw[c, ih, iz] = (gw[c, ih, iz].astype(F32) + R0[w, ih, iz].astype(F32)).astype(BF)
            return 0

        lax.fori_loop(0, 8, one, 0)
        r1[w] = [
            send(gw.at[c, hx, :, yx], R1.at[w, 1], P2),
            send(gw.at[c, p2h, :, p2y], R1.at[w, 0], P2),
        ]

    def rs_c(w):
        gw = Gw[w]
        for cp in r1[w]:
            cp.wait_recv()

        def one(i, _):
            gw[c, p1h, i, p1y] = (gw[c, p1h, i, p1y].astype(F32) + R1[w, 1, i].astype(F32)).astype(BF)
            return 0

        lax.fori_loop(0, 4, one, 0)
        r2s[w] = send(gw.at[c, p1h, :, p1y], R2.at[w], P1)

    def rs_d(w):
        gw = Gw[w]
        r2s[w].wait_recv()

        def two(i, _):
            gw[c, h, i, y] = (
                gw[c, h, i, y].astype(F32) + R1[w, 0, i].astype(F32) + R2[w, i].astype(F32)
            ).astype(BF)
            return 0

        lax.fori_loop(0, 4, two, 0)
        r3[w] = [send(gw.at[c, h, zs[k], y], R3.at[w, k - 1], dev(h, zs[k], y, c)) for k in range(1, 4)]

    def rs_e(w):
        gw = Gw[w]
        total = gw[c, h, z, y].astype(F32)
        for k in range(1, 4):
            r3[w][k - 1].wait_recv()
            total += R3[w, k - 1].astype(F32)
        FA[w] = total
        r4[w] = send(FA.at[w, pl.ds(pl.multiple_of(sib * 40, 8), 40)], FR.at[w], SIB)

    def rs_f(w):
        r4[w].wait_recv()
        fout[w][:, pl.ds(pl.multiple_of(c * 640, 128), 640)] = FA[w, pl.ds(pl.multiple_of(c * 40, 8), 40)]
        fout[w][:, pl.ds(pl.multiple_of(sib * 640, 128), 640)] = FR[w]

    outer(ACT, CI, G)
    rs_a(2)
    f_done(2)
    def con_half(i, cols):
        res = MID[:, cols] + nn(ACT[...], F[2, i].reshape(1280, 640)) + vec[8:9, cols]
        RES[h, :, cols] = res.astype(BF)

    halves(con_half)
    rx = send(RES.at[h], RES.at[h], XP)

    def act_half(i, cols):
        f0, f1w = F[2, 0, i].reshape(640, 640), F[2, 1, i].reshape(640, 640)
        dact = nt(CI[:, 0:640], f0) + nt(CI[:, 640:1280], f1w)
        de = (dact * EX[:, cols]).astype(BF)
        DE[:, cols] = de
        VR[103:104, cols] = jnp.sum(de.astype(F32), axis=0, keepdims=True)

    halves(act_half)
    left([cp for row in fz + flast for cp in row] + f1 + f2a + f2b + fs)
    outer(H2, DE, F.at[2])
    rs_a(1)


    def back_half(i, cols):
        f0, f1w = F[1, 0, i].reshape(640, 640), F[1, 1, i].reshape(640, 640)
        EX[:, cols] = nt(DE[:, 0:640], f0) + nt(DE[:, 640:1280], f1w)

    rs_b(2)
    halves(back_half)

    def norm2_back(i, _):
        rows = pl.ds(pl.multiple_of(i * 32, 32), 32)
        dh2, n2 = EX[rows, :], N2[rows, :]
        VR[101:102, :] += jnp.sum(dh2 * n2, axis=0, keepdims=True)
        VR[102:103, :] += jnp.sum(dh2, axis=0, keepdims=True)
        wv = dh2 * vec[5:6, :]
        dmid = CI[rows, :].astype(F32) + RR[rows, 0:1] * (
            wv - jnp.mean(wv, axis=-1, keepdims=True) - n2 * jnp.mean(wv * n2, axis=-1, keepdims=True)
        )
        MID[rows, :] = dmid
        gb = dmid.astype(BF)
        GB[rows, :] = gb
        VR[100:101, :] += jnp.sum(gb.astype(F32), axis=0, keepdims=True)
        return 0

    lax.fori_loop(0, 4, norm2_back, 0)
    left(asend)
    As[...] = jnp.zeros((4, 2, 128, 256), BF)

    def dattn(e, _):
        eh, ez = lax.div(e, 4), lax.rem(e, 4)
        da = nt(GB[:, 0:640], F[0, 0, eh, ez].reshape(160, 640)) + nt(
            GB[:, 640:1280], F[0, 1, eh, ez].reshape(160, 640)
        )
        As[lax.div(e, 2), lax.rem(e, 2), :, 0:160] = da.astype(BF)
        return 0

    lax.fori_loop(0, 8, dattn, 0)
    dos = []
    for k in range(4):
        for cc in (c, sib):
            if k == 0 and cc is c:
                continue
            dos.append(send(As.at[zs[k], cc], DOr.at[z, c], dev(h, zs[k], y, cc)))
    DOr[z, c] = As[z, c]


    def outo(e, _):
        def one(half, _):
            g = tn(A[e, :, 0:160], GB[:, pl.ds(pl.multiple_of(half * 640, 128), 640)])
            F[1, half, lax.div(e, 4), lax.rem(e, 4)] = g.astype(BF).reshape(2, 80, 640)
            return 0

        lax.fori_loop(0, 2, one, 0)
        return 0

    rs_b(1)
    lax.fori_loop(0, 8, outo, 0)
    rs_a(0)

    rx.wait_recv()
    pm = perm[pl.ds(h * 16 + b, 1), :]
    om0 = jnp.where(pm == b * 128 + i_sub, 1.0, 0.0).astype(BF)
    om1 = jnp.where(pm == (16 + b) * 128 + i_sub, 1.0, 0.0).astype(BF)

    def mix_half(i, cols):
        mixed_out[:, cols] = (tn(om0, RES[0, :, cols]) + tn(om1, RES[1, :, cols])).astype(BF)

    halves(mix_half)
    rs_b(0)


    for cp in dos:
        cp.wait_recv()
    left(kv1 + kv2 + kv3)

    lane128 = lax.broadcasted_iota(jnp.int32, (256, 128), 1)

    def prep(zt, _):
        do = pltpu.roll(DOr[zt].reshape(256, 256).astype(F32), 32, 1)
        DOs[zt] = do.astype(BF)
        agree = jnp.sum(do * O[zt], axis=-1, keepdims=True)
        both = jnp.where(lane128 == 0, LS[zt], jnp.where(lane128 == 1, agree, 0.0))
        ST[zt] = jnp.transpose(both)[0:8, :]
        DQ[zt] = jnp.zeros((256, 256), F32)
        return 0

    lax.fori_loop(0, 4, prep, 0)

    def key_tile(kh, kz, ky):
        kt = kh * 8 + kz * 2 + ky
        base = kt - h * 8 - y
        zlo = jnp.maximum(lax.div(base + 33, 2) - 16, 0)
        zhi = jnp.minimum(lax.div(base + 40, 2) - 16, 3) + 1
        DK[...] = jnp.zeros((256, 256), F32)
        DV[...] = jnp.zeros((256, 256), F32)
        kk = KV[kh, kz, ky, :, 0:256]
        vv = KV[kh, kz, ky, :, 128:384]
        kpos = kt * 256 + lax.broadcasted_iota(jnp.int32, (256, 1), 0)

        def one(zq, _):
            q = Q[zq]
            do = DOs[zq]
            qpos = (h * 8 + zq * 2 + y) * 256 + lax.broadcasted_iota(jnp.int32, (1, 256), 1)
            seg = seg_of(qpos)
            st = ST[zq]
            s = nt(kk, q) * scale
            ok = (kpos >= seg) & (kpos <= qpos)
            p = jnp.where(ok, jnp.exp(jnp.where(ok, s - st[0:1, :], 0.0)), 0.0)
            dp = nt(vv, do)
            ds = (p * (dp - st[1:2, :])).astype(BF)
            DK[...] += nn(ds, q)
            DV[...] += nn(p.astype(BF), do)
            DQ[zq] += tn(ds, kk)
            return 0

        lax.fori_loop(zlo, zhi, one, 0)
        dk = DK[...] * scale
        dv = DV[...]
        KV[kh, kz, ky, :, 0:128] = dk[:, 0:128].astype(BF)
        KV[kh, kz, ky, :, 128:256] = (dk[:, 128:256] + dv[:, 0:128]).astype(BF)
        KV[kh, kz, ky, :, 256:384] = dv[:, 128:256].astype(BF)

    dk0, dk1, dk2 = {}, {}, {}
    turn = (1, 2, 3, 0)
    for k in turn:
        kz = zs[k]
        key_tile(hx, kz, yx)
        dk1[k] = send(KV.at[hx, kz, yx], DKVr.at[1, kz], P2)
        key_tile(p2h, kz, p2y)
        dk0[k] = send(KV.at[p2h, kz, p2y], DKVr.at[0, kz], P2)
    rs_c(2)
    for k in turn:
        kz = zs[k]
        key_tile(p1h, kz, p1y)
        dk1[k].wait_recv()
        KV[p1h, kz, p1y] = (KV[p1h, kz, p1y].astype(F32) + DKVr[1, kz].astype(F32)).astype(BF)
        dk2[k] = send(KV.at[p1h, kz, p1y], DKVr.at[2, kz], P1)
    rs_d(2)
    rs_c(1)

    def own_tile(kz, _):
        key_tile(h, kz, y)
        return 0

    lax.fori_loop(0, 4, own_tile, 0)
    rs_c(0)
    rs_e(2)
    rs_d(1)

    def join(zt, _):
        dkv = KV[h, zt, y].astype(F32) + DKVr[0, zt].astype(F32) + DKVr[2, zt].astype(F32)
        dq = pltpu.roll(jnp.where(lane256 < 160, DQ[zt] * scale, 0.0), 64, 1)
        DKVQ[zt, :, 0:256] = dkv[:, 0:256].astype(BF)
        DKVQ[zt, :, 256:384] = (dkv[:, 256:384] + dq[:, 0:128]).astype(BF)
        DKVQ[zt, :, 384:512] = dq[:, 128:256].astype(BF)
        return 0


    VS[...] = jnp.zeros((128, 512), F32)

    def first_grad(zt, _):
        d = DKVQ[zt]
        VS[98:99, :] += jnp.sum(d.astype(F32), axis=0, keepdims=True)

        def u_half(i, cols):
            u = nt(d, W[i].reshape(640, 512))
            VR[97:98, cols] += jnp.sum(u, axis=0, keepdims=True)
            U[zt, :, :, cols] = u.astype(BF).reshape(2, 128, 640)

        halves(u_half)

        def gain(i, _):
            rows = pl.ds(pl.multiple_of(lax.rem(i, 2) * 64, 64), 64)
            n, _ = stats(T[zt, lax.div(i, 2), rows].astype(F32))
            VR[96:97, :] += jnp.sum(U[zt, lax.div(i, 2), rows].astype(F32) * n, axis=0, keepdims=True)
            return 0

        lax.fori_loop(0, 4, gain, 0)
        return 0

    us = []
    for k in turn:
        dk0[k].wait_recv()
        dk2[k].wait_recv()
        join(zs[k], 0)
        first_grad(zs[k], 0)
        us.append(send(U.at[zs[k], sib], UR.at[zs[k]], SIB))

    rs_d(0)
    VS[99:100, :] = VS[98:99, :]
    vst = jnp.transpose(VS[...])
    vlane = lax.broadcasted_iota(jnp.int32, (160, 128), 1)
    colb[0:1280, :] = jnp.transpose(VR[...])
    rows = pl.ds(pl.multiple_of(t * 160, 8), 160)
    colb[rows, :] += jnp.where(vlane == 98, vst[320:480, :], 0.0) + jnp.where(
        vlane == 99, vst[160:320, :], 0.0
    )

    uz = []
    for i, k in enumerate((1, 2, 3, 0)):
        us[i].wait_recv()
        zt = zs[k]
        U[zt, c] = (U[zt, c].astype(F32) + UR[zt].astype(F32)).astype(BF)
        if k:
            uz.append(send(U.at[zt, c], UZ.at[k - 1], dev(h, zt, y, c)))

    def head_grad(hh, _):
        g = tn(
            H[:, :, pl.ds(pl.multiple_of(hh * 640, 128), 640)].reshape(1024, 640),
            DKVQ[...].reshape(1024, 512),
        )
        DW[hh, :, :, :, 0:384] = g[:, 0:384].astype(BF).reshape(4, 2, 80, 384)
        last = g[:, 384:512] + colb[pl.ds(pl.multiple_of(hh * 640, 128), 640), :]
        DW[hh, :, :, :, 384:512] = last.astype(BF).reshape(4, 2, 80, 128)
        return 0

    lax.fori_loop(0, 2, head_grad, 0)
    dw1 = send(DW.at[hx, :, yx], DWr.at[1], P2)
    rs_e(1)
    rs_e(0)
    dw0 = send(DW.at[p2h, :, p2y], DWr.at[0], P2)
    dw1.wait_recv()
    DW[p1h, :, p1y] = (DW[p1h, :, p1y].astype(F32) + DWr[1].astype(F32)).astype(BF)
    dw2 = send(DW.at[p1h, :, p1y], DWr.at[2], P1)
    dw0.wait_recv()
    dw2.wait_recv()
    left(wz)
    for k in range(4):
        DWz[k] = (
            DW[h, k, y].astype(F32) + DWr[0, k].astype(F32) + DWr[2, k].astype(F32)
        ).astype(BF)
    dwz = [send(DWz.at[zs[k]], DWh.at[z], dev(h, zs[k], y, c)) for k in range(1, 4)]
    DWh[z] = DWz[z]

    for cp in uz:
        cp.wait_recv()

    def last_rows(i, _):
        rows = pl.ds(pl.multiple_of(i * 32, 32), 32)
        u = U[z, c, rows].astype(F32)
        for k in range(3):
            u += UZ[k, rows].astype(F32)
        n, r = stats(tok[rows, :].astype(F32))
        wv = u * vec[0:1, :]
        gt = MID[rows, :] + r * (
            wv - jnp.mean(wv, axis=-1, keepdims=True) - n * jnp.mean(wv * n, axis=-1, keepdims=True)
        )
        gtok_out[rows, :] = gt.astype(BF)
        return 0

    lax.fori_loop(0, 4, last_rows, 0)

    for cp in dwz:
        cp.wait_recv()
    for k in range(4):
        wasm[k] = DWh[k].astype(F32)
    wr[...] = wasm[:, pl.ds(pl.multiple_of(sib * 40, 8), 40), :]
    wo = send(wr, WOr, SIB)
    left([wa])
    WP[c] = wasm[:, pl.ds(pl.multiple_of(c * 40, 8), 40), :]
    for w in (2, 1, 0):
        rs_f(w)
    wo.wait_recv()
    WP[sib] = WOr[...]
    total = jnp.zeros((40, 128), F32)
    for e in range(8):
        for i, dst in enumerate((gk, gv, gq)):
            dst[:, e * 160:(e + 1) * 160] = WP[e % 2, e // 2, :, i * 160:(i + 1) * 160]
        total += WP[e % 2, e // 2, :, 384:512]
    colb[0:40, :] = total
    vgo[...] = jnp.transpose(colb[0:128, :])[96:112, :]

    token_end()
    for cp in pending:
        cp.wait_send()

    assert count[0] <= NSEM, count[0]


NSEM = 192


def hand_over(*refs):
    n = len(refs) // 2
    sems = refs[-1]
    copies = [pltpu.make_async_copy(refs[i], refs[n + i], sems.at[i]) for i in range(n)]
    for cp in copies:
        cp.start()
    for cp in copies:
        cp.wait()


def fast_local(
    tokens, cotangent, permutation, seq_lengths, first_gain, first_bias, query_weight, query_bias,
    key_weight, value_weight, value_bias, output_weight, output_bias, second_gain, second_bias,
    expand_weight, expand_bias, contract_weight, contract_bias,
):
    vectors = [first_gain, first_bias, query_bias, value_bias, output_bias, second_gain, second_bias,
               expand_bias, contract_bias]
    vcol = jnp.pad(jnp.stack(vectors, axis=1).astype(F32), ((0, 0), (0, 23)))
    perm = permutation.reshape(32, 128)

    vm = pltpu.VMEM
    fshape = (2, 2, 4, 2, 80, 640)
    scratch = dict(
        WP=vm((2, 4, 40, 512), F32), FP=vm((2, 3, 40, 640), F32),
        T=vm((4, 2, 128, 1280), BF), H=vm((4, 256, 1280), BF), W=vm((2, 4, 2, 80, 512), BF),
        KV=vm((2, 4, 2, 256, 384), BF), Q=vm((4, 256, 256), BF), O=vm((4, 256, 256), F32),
        F=vm((3,) + fshape, BF), G=vm(fshape, BF), R0=vm((3, 2, 4, 2, 80, 640), BF),
        R1=vm((3, 2, 4, 80, 640), BF), R2=vm((3, 4, 80, 640), BF), R3=vm((3, 3, 80, 640), BF),
        FA=vm((3, 80, 640), F32), FR=vm((3, 40, 640), F32),
        wr=vm((4, 40, 512), F32), wasm=vm((4, 80, 512), F32),
        fr=vm((3, 40, 640), F32),
        colb=vm((1408, 128), F32), vec=vm((16, 1280), F32), bias=vm((8, 512), F32),
        LS=vm((4, 256, 128), F32), ST=vm((4, 8, 256), F32),
        A=vm((8, 128, 256), BF), As=vm((4, 2, 128, 256), BF), C=vm((2, 128, 1280), BF),
        RES=vm((2, 128, 1280), BF), MID=vm((128, 1280), F32), N2=vm((128, 1280), F32), RR=vm((128, 128), F32),
        EX=vm((128, 1280), F32), H2=vm((128, 1280), BF), ACT=vm((128, 1280), BF),
        CI=vm((128, 1280), BF), DE=vm((128, 1280), BF), GB=vm((128, 1280), BF),
        DOs=vm((4, 256, 256), BF), DOr=vm((4, 2, 128, 256), BF),
        DK=vm((256, 256), F32), DV=vm((256, 256), F32), DQ=vm((4, 256, 256), F32),
        DKVr=vm((3, 4, 256, 384), BF), DKVQ=vm((4, 256, 512), BF), U=vm((4, 2, 128, 1280), BF),
        UR=vm((4, 128, 1280), BF), UZ=vm((3, 128, 1280), BF), VR=vm((128, 1280), F32),
        VS=vm((128, 512), F32), DW=vm((2, 4, 2, 80, 512), BF),
        DWr=vm((3, 4, 80, 512), BF), DWz=vm((4, 80, 512), BF), DWh=vm((4, 80, 512), BF),
        WOr=vm((4, 40, 512), F32),
        ss=pltpu.SemaphoreType.DMA((NSEM,)), rs=pltpu.SemaphoreType.DMA((NSEM,)),
        lss=pltpu.SemaphoreType.DMA((5,)), lrs=pltpu.SemaphoreType.DMA((4,)),
    )
    vspec = pl.BlockSpec(memory_space=pltpu.VMEM)
    rows = jax.ShapeDtypeStruct((40, 1280), F32)
    tokens_out = jax.ShapeDtypeStruct((128, 1280), BF)
    mixed, gtok, gq, gk, gv, go, ge, gc, vg = pl.pallas_call(
        block_kernel,
        out_shape=(tokens_out, tokens_out) + (rows,) * 6 + (jax.ShapeDtypeStruct((16, 128), F32),),
        in_specs=[vspec, vspec, vspec, pl.BlockSpec(memory_space=pltpu.SMEM)] + [vspec] * 7,
        out_specs=(vspec,) * 9,
        scratch_shapes=list(scratch.values()),
        compiler_params=pltpu.CompilerParams(
            collective_id=0, has_side_effects=True, vmem_limit_bytes=63 * MB,
        ),
        cost_estimate=pl.CostEstimate(flops=12_000_000_000, bytes_accessed=6_000_000, transcendentals=5_000_000),
        name="block",
    )(tokens, cotangent, perm, seq_lengths, vcol, query_weight, key_weight, value_weight, output_weight,
      expand_weight, contract_weight)
    any_spec = pl.BlockSpec(memory_space=pl.ANY)
    mixed, gtok, gq, gk, gv, go, ge, gc = pl.pallas_call(
        hand_over,
        out_shape=(tokens_out, tokens_out) + (rows,) * 6,
        in_specs=[vspec] * 8,
        out_specs=(any_spec,) * 8,
        scratch_shapes=[pltpu.SemaphoreType.DMA((8,))],
        name="hand_over",
    )(mixed, gtok, gq, gk, gv, go, ge, gc)
    v = [vg[j, 0:40] for j in range(9)]
    return mixed, gtok, v[0], v[1], gq, v[2], gk, gv, v[3], go, v[4], v[5], v[6], ge, v[7], gc, v[8]


def shifted(array, axis, by):
    length = lax.axis_size(axis)
    return lax.ppermute(array, axis, [(i, (i + by) % length) for i in range(length)])


def normalize(values, gain, shift):
    centre = jnp.mean(values, axis=-1, keepdims=True)
    spread = jnp.mean((values - centre) ** 2, axis=-1, keepdims=True)
    return (values - centre) * lax.rsqrt(spread + 1e-05) * gain + shift


def exact_gelu(values):
    return jax.nn.gelu(values, approximate=False)


def layout_initial(permutation, blk_source, width, blk_count, head_count):
    rows = jnp.arange(width * head_count, dtype=jnp.int32)
    places = (rows // width * blk_count + blk_source) * width + rows % width
    return jnp.take(permutation, places)


def segment_of(initial, ends):
    return jnp.sum((initial[:, None] >= ends[None, :]).astype(jnp.int32), axis=1)


def permitted(query_orig, key_orig, ends):
    same = segment_of(query_orig, ends)[:, None] == segment_of(key_orig, ends)[None, :]
    return same & (key_orig[None, :] <= query_orig[:, None])


def outer_sum(left, right):
    return lax.dot_general(
        left, right, (((0,), (0,)), ((), ())), preferred_element_type=jnp.float32
    )


def back_product(left, right):
    return lax.dot_general(
        left, right, (((1,), (1,)), ((), ())), preferred_element_type=jnp.float32
    )


def block_terms(
    query_block,
    grad_block,
    log_block,
    agree_block,
    query_orig,
    key_block,
    value_block,
    key_orig,
    ends,
    scale,
):
    allowed = permitted(query_orig, key_orig, ends)
    scores = (
        jnp.einsum("qhd,khd->hqk", query_block, key_block, preferred_element_type=jnp.float32)
        * scale
    )
    weights = jnp.exp(jnp.where(allowed[None], scores - log_block[..., None], -1e30))
    value_term = jnp.einsum(
        "hqk,qhd->khd", weights.astype(jnp.bfloat16), grad_block, preferred_element_type=jnp.float32
    )
    product = jnp.einsum(
        "qhd,khd->hqk", grad_block, value_block, preferred_element_type=jnp.float32
    )
    score_grad = (weights * (product - agree_block[..., None])).astype(jnp.bfloat16)
    query_term = jnp.einsum(
        "hqk,khd->qhd", score_grad, key_block, preferred_element_type=jnp.float32
    )
    key_term = jnp.einsum(
        "hqk,qhd->khd", score_grad, query_block, preferred_element_type=jnp.float32
    )
    return (query_term, key_term, value_term)


def local(
    tokens,
    cotangent,
    permutation,
    seq_lengths,
    first_gain,
    first_bias,
    query_weight,
    query_bias,
    key_weight,
    value_weight,
    value_bias,
    output_weight,
    output_bias,
    second_gain,
    second_bias,
    expand_weight,
    expand_bias,
    contract_weight,
    contract_bias,
):
    width = tokens.shape[0]
    blk_count = lax.axis_size("blk")
    head_count = lax.axis_size("head")
    blk_index = lax.axis_index("blk")
    flat_index = lax.axis_index("head") * blk_count + blk_index
    count = seq_lengths.shape[0]
    before = jnp.arange(count)[None, :] <= jnp.arange(count)[:, None]
    ends = jnp.sum(jnp.where(before, seq_lengths[None, :], 0), axis=1)
    total = permutation.shape[0]
    numbers = jnp.arange(total, dtype=jnp.int32)
    inverse = jnp.zeros((total,), jnp.int32).at[permutation].set(numbers)
    local_rows = jnp.arange(width, dtype=jnp.int32)
    first_row = flat_index * width
    going = lax.dynamic_slice_in_dim(inverse, first_row, width)
    order_source = jnp.argsort(going)
    arriving = lax.dynamic_slice_in_dim(permutation, first_row, width)
    order_target = jnp.argsort(arriving // width // blk_count * width + local_rows)
    undo_target = jnp.argsort(order_target)
    undo_source = jnp.argsort(order_source)
    received = lax.all_to_all(
        jnp.take(tokens, order_source, axis=0), "head", split_axis=0, concat_axis=0, tiled=True
    )
    inputs = jnp.take(received, undo_target, axis=0).astype(jnp.float32)
    vectors = jnp.stack(
        [
            first_gain,
            first_bias,
            query_bias,
            value_bias,
            output_bias,
            second_gain,
            second_bias,
            expand_bias,
            contract_bias,
        ]
    )
    query_full, key_full, value_full, output_full, expand_full, contract_full, vector_stack = (
        lax.all_gather(query_weight, ("head", "blk"), axis=0, tiled=True),
        lax.all_gather(key_weight, ("head", "blk"), axis=0, tiled=True),
        lax.all_gather(value_weight, ("head", "blk"), axis=0, tiled=True),
        lax.all_gather(output_weight, ("head", "blk"), axis=0, tiled=True),
        lax.all_gather(expand_weight, ("head", "blk"), axis=0, tiled=True),
        lax.all_gather(contract_weight, ("head", "blk"), axis=0, tiled=True),
        lax.all_gather(vectors, ("head", "blk"), axis=1, tiled=True),
    )
    vector_full = vector_stack.astype(jnp.float32)
    first_hidden = normalize(inputs, vector_full[0], vector_full[1]).astype(jnp.bfloat16)
    queries = (
        jnp.dot(first_hidden, query_full, preferred_element_type=jnp.float32) + vector_full[2]
    ).astype(jnp.bfloat16)
    keys = jnp.dot(first_hidden, key_full, preferred_element_type=jnp.float32).astype(jnp.bfloat16)
    values = (
        jnp.dot(first_hidden, value_full, preferred_element_type=jnp.float32) + vector_full[3]
    ).astype(jnp.bfloat16)
    head_queries, head_keys, head_values = (
        lax.all_to_all(queries, "head", split_axis=1, concat_axis=0, tiled=True),
        lax.all_to_all(keys, "head", split_axis=1, concat_axis=0, tiled=True),
        lax.all_to_all(values, "head", split_axis=1, concat_axis=0, tiled=True),
    )
    rows_here = width * head_count
    feature_here = head_queries.shape[1]
    heads_here = feature_here // HEAD_DIM
    scale = HEAD_DIM ** (-0.5)
    query_initial = layout_initial(permutation, blk_index, width, blk_count, head_count)
    shaped_queries = head_queries.reshape(rows_here, heads_here, HEAD_DIM)
    shaped_keys = head_keys.reshape(rows_here, heads_here, HEAD_DIM)
    shaped_values = head_values.reshape(rows_here, heads_here, HEAD_DIM)
    start_state = (
        jnp.full((heads_here, rows_here), -1e30, jnp.float32),
        jnp.zeros((heads_here, rows_here), jnp.float32),
        jnp.zeros((heads_here, rows_here, HEAD_DIM), jnp.float32),
    )
    carry = start_state
    key_piece = lax.all_gather(head_keys, "blk", axis=0, tiled=True)
    value_piece = lax.all_gather(head_values, "blk", axis=0, tiled=True)
    pieces = key_piece.shape[0] // rows_here
    key_blocks = key_piece.reshape(pieces, rows_here, heads_here, HEAD_DIM)
    value_blocks = value_piece.reshape(pieces, rows_here, heads_here, HEAD_DIM)

    def visit(state, item):
        key_block, value_block, offset = item
        running, total_sum, gathered = state
        key_initial = layout_initial(permutation, offset, width, blk_count, head_count)
        allowed = permitted(query_initial, key_initial, ends)
        scores = (
            jnp.einsum(
                "qhd,khd->hqk", shaped_queries, key_block, preferred_element_type=jnp.float32
            )
            * scale
        )
        scores = jnp.where(allowed[None], scores, -1e30)
        newest = jnp.maximum(running, jnp.max(scores, axis=-1))
        factor = jnp.exp(running - newest)
        exponent = jnp.where(allowed[None], jnp.exp(scores - newest[..., None]), 0.0)
        total_sum = factor * total_sum + jnp.sum(exponent, axis=-1)
        gathered = factor[..., None] * gathered + jnp.einsum(
            "hqk,khd->hqd",
            exponent.astype(jnp.bfloat16),
            value_block,
            preferred_element_type=jnp.float32,
        )
        return ((newest, total_sum, gathered), None)

    carry, unused = lax.scan(
        visit, carry, (key_blocks, value_blocks, jnp.arange(pieces, dtype=jnp.int32))
    )
    running, total_sum, gathered = carry
    attended = gathered / total_sum[..., None]
    log_total = running + jnp.log(total_sum)
    attended_rows = jnp.transpose(attended, (1, 0, 2)).reshape(rows_here, feature_here)
    merged = lax.all_to_all(
        attended_rows.astype(jnp.bfloat16), "head", split_axis=0, concat_axis=1, tiled=True
    )
    middle = (
        inputs + jnp.dot(merged, output_full, preferred_element_type=jnp.float32) + vector_full[4]
    )
    second_hidden = normalize(middle, vector_full[5], vector_full[6]).astype(jnp.bfloat16)
    expanded = (
        jnp.dot(second_hidden, expand_full, preferred_element_type=jnp.float32) + vector_full[7]
    )
    activated = exact_gelu(expanded).astype(jnp.bfloat16)
    result = (
        middle
        + jnp.dot(activated, contract_full, preferred_element_type=jnp.float32)
        + vector_full[8]
    )
    grad_contract = outer_sum(activated, cotangent)
    grad_contract_bias = jnp.sum(cotangent.astype(jnp.float32), axis=0)
    grad_activated = back_product(cotangent, contract_full)
    unused_value, gelu_pull = jax.vjp(exact_gelu, expanded)
    grad_expanded = gelu_pull(grad_activated)[0].astype(jnp.bfloat16)
    grad_expand = outer_sum(second_hidden, grad_expanded)
    grad_expand_bias = jnp.sum(grad_expanded.astype(jnp.float32), axis=0)
    grad_second = back_product(grad_expanded, expand_full)
    unused_second, second_pull = jax.vjp(normalize, middle, vector_full[5], vector_full[6])
    grad_middle_norm, grad_second_gain, grad_second_bias = second_pull(grad_second)
    grad_middle = cotangent.astype(jnp.float32) + grad_middle_norm
    grad_branch = grad_middle.astype(jnp.bfloat16)
    grad_output = outer_sum(merged, grad_branch)
    grad_output_bias = jnp.sum(grad_branch.astype(jnp.float32), axis=0)
    grad_merged = back_product(grad_branch, output_full).astype(jnp.bfloat16)
    head_grad = lax.all_to_all(grad_merged, "head", split_axis=1, concat_axis=0, tiled=True)
    shaped_grad = head_grad.reshape(rows_here, heads_here, HEAD_DIM)
    agreement = jnp.einsum("qhd,hqd->hq", shaped_grad.astype(jnp.float32), attended)
    zero_rows = jnp.zeros((rows_here, heads_here, HEAD_DIM), jnp.float32)

    def key_turn(turn, state):
        moving_keys, moving_values, key_total, value_total, query_total = state
        source = (blk_index - turn) % blk_count
        key_orig = layout_initial(permutation, source, width, blk_count, head_count)
        query_term, key_term, value_term = block_terms(
            shaped_queries,
            shaped_grad,
            log_total,
            agreement,
            query_initial,
            moving_keys,
            moving_values,
            key_orig,
            ends,
            scale,
        )
        moving_keys, moving_values = shifted((moving_keys, moving_values), "blk", 1)
        key_total, value_total = (
            shifted((key_total + key_term).astype(jnp.bfloat16), "blk", 1).astype(jnp.float32),
            shifted((value_total + value_term).astype(jnp.bfloat16), "blk", 1).astype(jnp.float32),
        )
        return (moving_keys, moving_values, key_total, value_total, query_total + query_term)

    final_state = lax.fori_loop(
        0, blk_count, key_turn, (shaped_keys, shaped_values, zero_rows, zero_rows, zero_rows)
    )
    key_grad_heads = final_state[2]
    value_grad_heads = final_state[3]
    query_grad_heads = final_state[4]
    query_grad_rows = (
        (query_grad_heads * scale).astype(jnp.bfloat16).reshape(rows_here, feature_here)
    )
    key_grad_rows = (key_grad_heads * scale).astype(jnp.bfloat16).reshape(rows_here, feature_here)
    value_grad_rows = value_grad_heads.astype(jnp.bfloat16).reshape(rows_here, feature_here)
    grad_queries, grad_keys, grad_values = (
        lax.all_to_all(query_grad_rows, "head", split_axis=0, concat_axis=1, tiled=True),
        lax.all_to_all(key_grad_rows, "head", split_axis=0, concat_axis=1, tiled=True),
        lax.all_to_all(value_grad_rows, "head", split_axis=0, concat_axis=1, tiled=True),
    )
    grad_query = outer_sum(first_hidden, grad_queries)
    grad_key = outer_sum(first_hidden, grad_keys)
    grad_value = outer_sum(first_hidden, grad_values)
    grad_query_bias = jnp.sum(grad_queries.astype(jnp.float32), axis=0)
    grad_value_bias = jnp.sum(grad_values.astype(jnp.float32), axis=0)
    grad_first = (
        back_product(grad_queries, query_full)
        + back_product(grad_keys, key_full)
        + back_product(grad_values, value_full)
    )
    unused_first, first_pull = jax.vjp(normalize, inputs, vector_full[0], vector_full[1])
    grad_inputs_norm, grad_first_gain, grad_first_bias = first_pull(grad_first)
    grad_inputs = (grad_middle + grad_inputs_norm).astype(jnp.bfloat16)
    vector_grads = jnp.stack(
        [
            grad_first_gain,
            grad_first_bias,
            grad_query_bias,
            grad_value_bias,
            grad_output_bias,
            grad_second_gain,
            grad_second_bias,
            grad_expand_bias,
            grad_contract_bias,
        ]
    )
    summed = (
        lax.psum_scatter(grad_query, ("head", "blk"), scatter_dimension=0, tiled=True),
        lax.psum_scatter(grad_key, ("head", "blk"), scatter_dimension=0, tiled=True),
        lax.psum_scatter(grad_value, ("head", "blk"), scatter_dimension=0, tiled=True),
        lax.psum_scatter(grad_output, ("head", "blk"), scatter_dimension=0, tiled=True),
        lax.psum_scatter(grad_expand, ("head", "blk"), scatter_dimension=0, tiled=True),
        lax.psum_scatter(grad_contract, ("head", "blk"), scatter_dimension=0, tiled=True),
        lax.psum_scatter(vector_grads, ("head", "blk"), scatter_dimension=1, tiled=True),
    )
    vector_shares = summed[6]
    returned = lax.all_to_all(
        jnp.take(grad_inputs, order_target, axis=0), "head", split_axis=0, concat_axis=0, tiled=True
    )
    grad_tokens = jnp.take(returned, undo_source, axis=0)
    return (
        result.astype(jnp.bfloat16),
        grad_tokens,
        vector_shares[0],
        vector_shares[1],
        summed[0],
        vector_shares[2],
        summed[1],
        summed[2],
        vector_shares[3],
        summed[3],
        vector_shares[4],
        vector_shares[5],
        vector_shares[6],
        summed[4],
        vector_shares[7],
        summed[5],
        vector_shares[8],
    )


def solution(mesh):
    return jax.shard_map(
        fast_local if mesh.shape["head"] == 2 and mesh.shape["blk"] == 16 else local,
        mesh=mesh,
        in_specs=(
            P(("head", "blk"), None),
            P(("head", "blk"), None),
            P(),
            P(),
            P(("head", "blk")),
            P(("head", "blk")),
            P(("head", "blk"), None),
            P(("head", "blk")),
            P(("head", "blk"), None),
            P(("head", "blk"), None),
            P(("head", "blk")),
            P(("head", "blk"), None),
            P(("head", "blk")),
            P(("head", "blk")),
            P(("head", "blk")),
            P(("head", "blk"), None),
            P(("head", "blk")),
            P(("head", "blk"), None),
            P(("head", "blk")),
        ),
        out_specs=(
            P(("head", "blk"), None),
            P(("head", "blk"), None),
            P(("head", "blk")),
            P(("head", "blk")),
            P(("head", "blk"), None),
            P(("head", "blk")),
            P(("head", "blk"), None),
            P(("head", "blk"), None),
            P(("head", "blk")),
            P(("head", "blk"), None),
            P(("head", "blk")),
            P(("head", "blk")),
            P(("head", "blk")),
            P(("head", "blk"), None),
            P(("head", "blk")),
            P(("head", "blk"), None),
            P(("head", "blk")),
        ),
        check_vma=False,
    )
```

```python
import functools
import jax
import jax.numpy as jnp
from jax import lax
from jax.experimental import pallas as pl
from jax.experimental.pallas import tpu as pltpu
from jax.sharding import PartitionSpec as P

HEAD_DIM = 160
MESH = pl.DeviceIdType.MESH
BF = jnp.bfloat16
F32 = jnp.float32
MB = 1 << 20


def nn(a, b):
    return lax.dot_general(a, b, (((1,), (0,)), ((), ())), preferred_element_type=F32)


def nt(a, b):
    return lax.dot_general(a, b, (((1,), (1,)), ((), ())), preferred_element_type=F32)


def tn(a, b):
    return lax.dot_general(a, b, (((0,), (0,)), ((), ())), preferred_element_type=F32)


def stats(v):
    centre = jnp.mean(v, axis=-1, keepdims=True)
    off = v - centre
    spread = jnp.mean(off * off, axis=-1, keepdims=True)
    r = lax.rsqrt(spread + 1e-05)
    return off * r, r


def block_kernel(
    tok, cot, perm, lens, vcol, wq, wk, wv, wts0, wts1, wts2,
    mixed_out, gtok_out, gq, gk, gv, fo0, fo1, fo2, vgo,
    WP, FP, T, H, W, KV, Q, QT, OT, F, G, R0, R1, R2, R3, FA, FR,
    wr, wasm, fr, colb, vec, bias,
    MS, TS, A, As, C, RES, MID, EX, H2, ACT, CI, DE, GB, DOs, DOT, DOr,
    DK, DV, DQ, DKVr, DKVQ, U, UR, UZ, VR, VS, DW, DWr, DWz, DWh, WOr,
    ss, rs, lss, lrs,
):
    h = lax.axis_index("head")
    b = lax.axis_index("blk")
    z = lax.div(b, 4)
    y = lax.rem(lax.div(b, 2), 2)
    c = lax.rem(b, 2)
    sib = 1 - c
    hx = 1 - h
    yx = 1 - y
    t = z * 2 + c
    first = c == 0
    p1h = jnp.where(first, hx, h)
    p1y = jnp.where(first, y, yx)
    p2h = jnp.where(first, h, hx)
    p2y = jnp.where(first, yx, y)

    def dev(hh, zz, yy, cc):
        return (hh, zz * 4 + yy * 2 + cc)

    zs = [lax.rem(z + k, 4) for k in range(4)]
    zr = [lax.rem(z + 4 - k, 4) for k in range(4)]
    SIB = dev(h, z, y, sib)
    P1 = dev(p1h, z, p1y, c)
    P2 = dev(p2h, z, p2y, c)
    XP = dev(hx, z, y, c)
    YP = dev(h, z, yx, c)

    count = [0]

    def desc(src, dst, device):
        i = count[0]
        count[0] += 1
        return pltpu.make_async_remote_copy(
            src_ref=src, dst_ref=dst, send_sem=ss.at[i], recv_sem=rs.at[i],
            device_id=device, device_id_type=MESH,
        )

    pending = []

    def send(src, dst, device):
        cp = desc(src, dst, device)
        cp.start()
        pending.append(cp)
        return cp

    def left(cps):
        for cp in cps:
            cp.wait_send()
        keep = [cp for cp in pending if not any(cp is one for one in cps)]
        pending[:] = keep

    bar = pltpu.get_barrier_semaphore()
    for k in range(1, 4):
        pl.semaphore_signal(bar, inc=1, device_id=dev(h, zs[k], y, c), device_id_type=MESH)
        pl.semaphore_signal(bar, inc=1, device_id=dev(h, zs[k], y, sib), device_id_type=MESH)
    for peer in (SIB, XP, YP):
        pl.semaphore_signal(bar, inc=1, device_id=peer, device_id_type=MESH)

    fout = (fo0, fo1, fo2)
    for e in range(8):
        for i, src in enumerate((wk, wv, wq)):
            WP[e % 2, e // 2, :, i * 160:(i + 1) * 160] = src[:, e * 160:(e + 1) * 160].astype(F32)
        WP[e % 2, e // 2, :, 480:512] = vcol[...]
    for w, src in enumerate((wts0, wts1, wts2)):
        for half in range(2):
            FP[half, w] = src[:, half * 640:(half + 1) * 640].astype(F32)

    pl.semaphore_wait(bar, 9)

    up, down = z < 3, z > 0
    UP = dev(h, jnp.minimum(z + 1, 3), y, c)
    DOWN = dev(h, jnp.maximum(z - 1, 0), y, c)
    order = [
        z,
        jnp.where(z == 0, 1, jnp.where(z == 3, 2, jnp.where(z == 1, 0, 3))),
        jnp.where(z == 0, 2, jnp.where(z == 3, 1, jnp.where(z == 1, 2, 1))),
        jnp.where(z == 0, 3, jnp.where(z == 3, 0, jnp.where(z == 1, 3, 0))),
    ]

    def tcopy(src, zt, si, device):
        return pltpu.make_async_remote_copy(
            src_ref=src, dst_ref=T.at[zt, c], send_sem=lss.at[si], recv_sem=lrs.at[zt],
            device_id=device, device_id_type=MESH,
        )

    ts = []

    def token_start():
        pl.when(up)(tcopy(tok, z, 0, UP).start)
        pl.when(down)(tcopy(tok, z, 1, DOWN).start)
        ts.append(send(tok, T.at[z, c], SIB))

    def token_step(k):
        zt = order[k]
        here = T.at[zt, c]
        tcopy(here, zt, 0, UP).wait_recv()
        pl.when((zt < z) & up)(tcopy(here, zt, 1 + k, UP).start)
        pl.when((zt > z) & down)(tcopy(here, zt, 1 + k, DOWN).start)
        ts.append(send(here, here, SIB))

    def token_end():
        pl.when(up)(tcopy(tok, z, 0, UP).wait_send)
        pl.when(down)(tcopy(tok, z, 1, DOWN).wait_send)
        for k in range(1, 4):
            zt = order[k]
            here = T.at[zt, c]
            pl.when((zt < z) & up)(tcopy(here, zt, 1 + k, UP).wait_send)
            pl.when((zt > z) & down)(tcopy(here, zt, 1 + k, DOWN).wait_send)

    wa = send(WP.at[sib], wr, SIB)
    fa = send(FP.at[sib], fr, SIB)
    T[z, c] = tok[...]
    C[h] = cot[...]

    wa.wait_recv()
    wasm[:, pl.ds(pl.multiple_of(c * 40, 8), 40), :] = WP[c]
    wasm[:, pl.ds(pl.multiple_of(sib * 40, 8), 40), :] = wr[...]
    for k in range(4):
        DWz[k] = wasm[k].astype(BF)
    W[h, z, y] = DWz[z]
    wz = [send(DWz.at[zs[k]], W.at[h, z, y], dev(h, zs[k], y, c)) for k in range(1, 4)]
    cx = send(cot, C.at[h], XP)
    fa.wait_recv()
    FA[:, pl.ds(pl.multiple_of(c * 40, 8), 40), :] = FP[c]
    FA[:, pl.ds(pl.multiple_of(sib * 40, 8), 40), :] = fr[...]
    for w in range(3):
        F[w, c, h, z, y] = FA[w].astype(BF)

    fz = [None] * 3

    def f_line(w):
        own = F.at[w, c, h, z, y]
        fz[w] = [send(own, own, dev(h, zs[k], y, c)) for k in range(1, 4)]

    f1, f2a, f2b, fs = [None] * 3, [None] * 3, [None] * 3, []

    def f_plane(w):
        for cp in fz[w]:
            cp.wait_recv()
        own = F.at[w, c, h, :, y]
        f1[w] = send(own, own, P1)
        f2a[w] = send(own, own, P2)
        one = send(own, own, SIB)
        fs.append(one)
        fs_w[id(one)] = w

    def f_forward(w):
        f1[w].wait_recv()
        got = F.at[w, c, p1h, :, p1y]
        f2b[w] = send(got, got, P2)
        one = send(got, got, SIB)
        fs.append(one)
        fs_w[id(one)] = w

    flast = [None] * 3
    fs_w = {}

    def f_last(w):
        f2a[w].wait_recv()
        got = F.at[w, c, p2h, :, p2y]
        one = send(got, got, SIB)
        f2b[w].wait_recv()
        got = F.at[w, c, hx, :, yx]
        flast[w] = [one, send(got, got, SIB)]

    f_line(0)
    token_start()
    for cp in wz:
        cp.wait_recv()
    own = W.at[h, :, y]
    w1 = send(own, own, P1)
    w2 = send(own, own, P2)
    w1.wait_recv()
    got = W.at[p1h, :, p1y]
    w3 = send(got, got, P2)
    f_plane(0)
    w2.wait_recv()
    w3.wait_recv()

    def tcol(hh, _):
        colb[pl.ds(pl.multiple_of(hh * 640, 128), 640), :] = (
            W[hh, :, :, :, 384:512].reshape(640, 128).astype(F32)
        )
        return 0

    lax.fori_loop(0, 2, tcol, 0)
    colb[1280:1408, :] = jnp.zeros((128, 128), F32)
    vec[...] = jnp.transpose(colb[0:1280, :])[96:112, :]
    mine = jnp.transpose(colb[pl.ds(pl.multiple_of(t * 160, 8), 256), :])
    bias[...] = jnp.zeros((8, 512), F32)
    bias[0:1, 160:320] = mine[99:100, 0:160]
    bias[0:1, 320:480] = mine[98:99, 0:160]

    lane256 = lax.broadcasted_iota(jnp.int32, (256, 256), 1)

    kv1, kv2, kv3 = [], [], []

    def project(k):
        zt = order[k]
        ts[k].wait_recv()

        def norm(i, _):
            rows = pl.ds(pl.multiple_of(lax.rem(i, 2) * 64, 64), 64)
            n, _ = stats(T[zt, lax.div(i, 2), rows].astype(F32))
            H[zt, pl.ds(pl.multiple_of(i * 64, 64), 64)] = (n * vec[0:1, :] + vec[1:2, :]).astype(BF)
            return 0

        lax.fori_loop(0, 4, norm, 0)
        kvq = nn(H[zt], W[...].reshape(1280, 512)) + bias[0:1, :]
        KV[h, zt, y] = kvq[:, 0:384].astype(BF)
        qr = pltpu.roll(kvq[:, 256:512], 192, 1)
        qr = jnp.where(lane256 < 160, qr, 0.0)
        Q[zt] = qr.astype(BF)
        QT[zt] = jnp.transpose(qr).astype(BF)
        src = KV.at[h, zt, y]
        kv1.append(send(src, src, P1))
        kv2.append(send(src, src, P2))

    def kv_forward(k):
        kv1[k].wait_recv()
        got = KV.at[p1h, order[k], p1y]
        kv3.append(send(got, got, P2))

    scale = HEAD_DIM ** -0.5
    ends = []
    run = 0
    for e in range(8):
        run = run + lens[e]
        ends.append(run)

    def seg_of(pos):
        s = jnp.zeros_like(pos)
        for e in range(7):
            s = jnp.where(pos >= ends[e], ends[e], s)
        return s

    def rowpos(zt):
        return (h * 8 + zt * 2 + y) * 256

    def pair_range(kt):
        base = kt - h * 8 - y
        zlo = jnp.maximum(lax.div(base + 33, 2) - 16, 0)
        zhi = jnp.minimum(lax.div(base + 40, 2) - 16, 3) + 1
        return zlo, zhi

    def allowed(kt, zq):
        kpos = kt * 256 + lax.broadcasted_iota(jnp.int32, (256, 1), 0)
        qpos = (h * 8 + zq * 2 + y) * 256 + lax.broadcasted_iota(jnp.int32, (1, 256), 1)
        return (kpos >= seg_of(qpos)) & (kpos <= qpos)

    def absorb(gh, kz, gy):
        kt = gh * 8 + kz * 2 + gy
        zlo, zhi = pair_range(kt)
        TS[...] = jnp.transpose(KV[gh, kz, gy, :, 128:384].astype(F32)).astype(BF)
        kk = KV.at[gh, kz, gy]

        def one(zq, _):
            s = jnp.where(allowed(kt, zq), nn(kk[:, 0:256], QT[zq]) * scale, -1e30)
            m = MS[zq, 0:1, :]
            mn = jnp.maximum(m, jnp.max(s, axis=0, keepdims=True))
            f = jnp.exp(m - mn)
            p = jnp.exp(s - mn)
            MS[zq, 0:1, :] = mn
            MS[zq, 1:2, :] = MS[zq, 1:2, :] * f + jnp.sum(p, axis=0, keepdims=True)
            OT[zq] = OT[zq] * f + nn(TS[...], p.astype(BF))
            return 0

        lax.fori_loop(zlo, zhi, one, 0)
        return 0

    def group(gh, gy):
        lax.fori_loop(0, 4, lambda kz, _: absorb(gh, kz, gy), 0)

    OT[...] = jnp.zeros((4, 256, 256), F32)
    MS[:, 0:1, :] = jnp.full((4, 1, 256), -1e30, F32)
    MS[:, 1:2, :] = jnp.zeros((4, 1, 256), F32)

    def finish(zt):
        m, l = MS[zt, 0:1, :], MS[zt, 1:2, :]
        o = OT[zt] / l
        OT[zt] = o
        MS[zt, 0:1, :] = m + jnp.log(l)
        turned = jnp.concatenate([o[32:256, :], o[0:32, :]], axis=0)
        As[zt] = jnp.transpose(turned).astype(BF).reshape(2, 128, 256)

    project(0)
    token_step(1)
    f_forward(0)
    project(1)
    token_step(2)
    f_line(1)
    project(2)
    kv_forward(0)
    token_step(3)
    f_line(2)
    project(3)
    kv_forward(1)
    kv_forward(2)
    kv_forward(3)
    f_plane(1)
    group(h, y)
    f_plane(2)
    group(p1h, p1y)
    f_forward(1)
    for cp in kv2:
        cp.wait_recv()
    group(p2h, p2y)
    for cp in kv3:
        cp.wait_recv()
    group(hx, yx)
    f_forward(2)
    asend = []
    for k in (1, 2, 3, 0):
        zt = zs[k]
        finish(zt)
        for cc in (c, sib):
            if k == 0 and cc is c:
                continue
            asend.append(send(As.at[zt, cc], A.at[t], dev(h, zt, y, cc)))
    A[t] = As[z, c]

    f_last(0)
    for cp in asend:
        cp.wait_recv()

    def f_done(w):
        for cp in flast[w] + fs[2 * w:2 * w + 2]:
            cp.wait_recv()

    fs.sort(key=lambda cp: fs_w[id(cp)])
    f_done(0)
    f_last(1)

    VR[...] = jnp.zeros((128, 1280), F32)

    def halves(fn):
        def run_half(i, _):
            fn(i, pl.ds(pl.multiple_of(i * 640, 128), 640))
            return 0

        lax.fori_loop(0, 2, run_half, 0)

    def out_half(i, cols):
        acc = tok[:, cols].astype(F32) + vec[4:5, cols]
        for e in range(8):
            acc += nn(A[e, :, 0:160], F[0, i, e // 4, e % 4].reshape(160, 640))
        MID[:, cols] = acc

    halves(out_half)

    def norm2(i, _):
        rows = pl.ds(pl.multiple_of(i * 32, 32), 32)
        n2, _ = stats(MID[rows, :])
        H2[rows, :] = (n2 * vec[5:6, :] + vec[6:7, :]).astype(BF)
        return 0

    lax.fori_loop(0, 4, norm2, 0)

    def exp_half(i, cols):
        ex = nn(H2[...], F[1, i].reshape(1280, 640)) + vec[7:8, cols]
        phi = 0.5 * (1.0 + lax.erf(ex * (0.5**0.5)))
        ACT[:, cols] = (ex * phi).astype(BF)
        EX[:, cols] = phi + ex * jnp.exp(-0.5 * ex * ex) * 0.3989422804014327

    f_done(1)
    f_last(2)
    halves(exp_half)

    cx.wait_recv()
    i_sub = lax.broadcasted_iota(jnp.int32, (128, 128), 0)
    mine0 = (h * 16 + b) * 128
    pr0, pr1 = perm[pl.ds(b, 1), :], perm[pl.ds(16 + b, 1), :]
    oh0 = jnp.where(pr0 == mine0 + i_sub, 1.0, 0.0).astype(BF)
    oh1 = jnp.where(pr1 == mine0 + i_sub, 1.0, 0.0).astype(BF)

    def cot_half(i, cols):
        ci = nn(oh0, C[0, :, cols]) + nn(oh1, C[1, :, cols])
        CI[:, cols] = ci.astype(BF)
        VR[104:105, cols] = jnp.sum(ci, axis=0, keepdims=True)

    halves(cot_half)

    def outer(left, right, dst):
        def one(i, _):
            hh, half = lax.div(i, 2), lax.rem(i, 2)
            g = tn(
                left[:, pl.ds(pl.multiple_of(hh * 640, 128), 640)],
                right[:, pl.ds(pl.multiple_of(half * 640, 128), 640)],
            )
            dst[half, hh] = g.astype(BF).reshape(4, 2, 80, 640)
            return 0

        lax.fori_loop(0, 4, one, 0)

    Gw = [F.at[1], F.at[2], G]
    ra = [None] * 3

    def rs_a(w):
        ra[w] = send(Gw[w].at[sib], R0.at[w], SIB)

    r1, r2s, r3, r4 = [None] * 3, [None] * 3, [None] * 3, [None] * 3

    def rs_b(w):
        ra[w].wait_recv()
        gw = Gw[w]

        def one(i, _):
            ih, iz = lax.div(i, 4), lax.rem(i, 4)
            gw[c, ih, iz] = (gw[c, ih, iz].astype(F32) + R0[w, ih, iz].astype(F32)).astype(BF)
            return 0

        lax.fori_loop(0, 8, one, 0)
        r1[w] = [
            send(gw.at[c, hx, :, yx], R1.at[w, 1], P2),
            send(gw.at[c, p2h, :, p2y], R1.at[w, 0], P2),
        ]

    def rs_c(w):
        gw = Gw[w]
        for cp in r1[w]:
            cp.wait_recv()

        def one(i, _):
            gw[c, p1h, i, p1y] = (gw[c, p1h, i, p1y].astype(F32) + R1[w, 1, i].astype(F32)).astype(BF)
            return 0

        lax.fori_loop(0, 4, one, 0)
        r2s[w] = send(gw.at[c, p1h, :, p1y], R2.at[w], P1)

    def rs_d(w):
        gw = Gw[w]
        r2s[w].wait_recv()

        def two(i, _):
            gw[c, h, i, y] = (
                gw[c, h, i, y].astype(F32) + R1[w, 0, i].astype(F32) + R2[w, i].astype(F32)
            ).astype(BF)
            return 0

        lax.fori_loop(0, 4, two, 0)
        r3[w] = [send(gw.at[c, h, zs[k], y], R3.at[w, k - 1], dev(h, zs[k], y, c)) for k in range(1, 4)]

    def rs_e(w):
        gw = Gw[w]
        total = gw[c, h, z, y].astype(F32)
        for k in range(1, 4):
            r3[w][k - 1].wait_recv()
            total += R3[w, k - 1].astype(F32)
        FA[w] = total
        r4[w] = send(FA.at[w, pl.ds(pl.multiple_of(sib * 40, 8), 40)], FR.at[w], SIB)

    def rs_f(w):
        r4[w].wait_recv()
        fout[w][:, pl.ds(pl.multiple_of(c * 640, 128), 640)] = FA[w, pl.ds(pl.multiple_of(c * 40, 8), 40)]
        fout[w][:, pl.ds(pl.multiple_of(sib * 640, 128), 640)] = FR[w]

    outer(ACT, CI, G)
    rs_a(2)
    f_done(2)
    def con_half(i, cols):
        res = MID[:, cols] + nn(ACT[...], F[2, i].reshape(1280, 640)) + vec[8:9, cols]
        RES[h, :, cols] = res.astype(BF)

    halves(con_half)
    rx = send(RES.at[h], RES.at[h], XP)

    def act_half(i, cols):
        f0, f1w = F[2, 0, i].reshape(640, 640), F[2, 1, i].reshape(640, 640)
        dact = nt(CI[:, 0:640], f0) + nt(CI[:, 640:1280], f1w)
        de = (dact * EX[:, cols]).astype(BF)
        DE[:, cols] = de
        VR[103:104, cols] = jnp.sum(de.astype(F32), axis=0, keepdims=True)

    halves(act_half)
    def back_half(i, cols):
        f0, f1w = F[1, 0, i].reshape(640, 640), F[1, 1, i].reshape(640, 640)
        EX[:, cols] = nt(DE[:, 0:640], f0) + nt(DE[:, 640:1280], f1w)

    left([cp for row in fz + flast for cp in row] + f1 + f2a + f2b + fs)
    outer(H2, DE, F.at[2])
    rs_a(1)
    rs_b(2)
    halves(back_half)

    def norm2_back(i, _):
        rows = pl.ds(pl.multiple_of(i * 32, 32), 32)
        dh2 = EX[rows, :]
        n2, r2 = stats(MID[rows, :])
        VR[101:102, :] += jnp.sum(dh2 * n2, axis=0, keepdims=True)
        VR[102:103, :] += jnp.sum(dh2, axis=0, keepdims=True)
        wv = dh2 * vec[5:6, :]
        dmid = CI[rows, :].astype(F32) + r2 * (
            wv - jnp.mean(wv, axis=-1, keepdims=True) - n2 * jnp.mean(wv * n2, axis=-1, keepdims=True)
        )
        EX[rows, :] = dmid
        gb = dmid.astype(BF)
        GB[rows, :] = gb
        VR[100:101, :] += jnp.sum(gb.astype(F32), axis=0, keepdims=True)
        return 0

    lax.fori_loop(0, 4, norm2_back, 0)
    left(asend)
    As[...] = jnp.zeros((4, 2, 128, 256), BF)

    def dattn(e, _):
        eh, ez = lax.div(e, 4), lax.rem(e, 4)
        da = nt(GB[:, 0:640], F[0, 0, eh, ez].reshape(160, 640)) + nt(
            GB[:, 640:1280], F[0, 1, eh, ez].reshape(160, 640)
        )
        As[lax.div(e, 2), lax.rem(e, 2), :, 0:160] = da.astype(BF)
        return 0

    lax.fori_loop(0, 8, dattn, 0)
    dos = []
    for k in range(4):
        for cc in (c, sib):
            if k == 0 and cc is c:
                continue
            dos.append(send(As.at[zs[k], cc], DOr.at[z, c], dev(h, zs[k], y, cc)))
    DOr[z, c] = As[z, c]


    def outo(e, _):
        def one(half, _):
            g = tn(A[e, :, 0:160], GB[:, pl.ds(pl.multiple_of(half * 640, 128), 640)])
            F[1, half, lax.div(e, 4), lax.rem(e, 4)] = g.astype(BF).reshape(2, 80, 640)
            return 0

        lax.fori_loop(0, 2, one, 0)
        return 0

    lax.fori_loop(0, 8, outo, 0)
    rs_a(0)

    for cp in dos:
        cp.wait_recv()
    left(kv1 + kv2 + kv3)

    def prep(zt, _):
        do = DOr[zt].reshape(256, 256).astype(F32)
        DOs[zt] = pltpu.roll(do, 32, 1).astype(BF)
        dt = jnp.transpose(do)
        dt = jnp.concatenate([dt[224:256, :], dt[0:224, :]], axis=0)
        DOT[zt] = dt.astype(BF)
        MS[zt, 1:2, :] = jnp.sum(dt * OT[zt], axis=0, keepdims=True)
        DQ[zt] = jnp.zeros((256, 256), F32)
        return 0

    lax.fori_loop(0, 4, prep, 0)

    def key_tile(kh, kz, ky):
        kt = kh * 8 + kz * 2 + ky
        zlo, zhi = pair_range(kt)
        DK[...] = jnp.zeros((256, 256), F32)
        DV[...] = jnp.zeros((256, 256), F32)
        tile = KV.at[kh, kz, ky]
        TS[...] = jnp.transpose(tile[:, 0:256].astype(F32)).astype(BF)

        def one(zq, _):
            s = nn(tile[:, 0:256], QT[zq]) * scale
            p = jnp.exp(jnp.where(allowed(kt, zq), s - MS[zq, 0:1, :], -1e30))
            dp = nn(tile[:, 128:384], DOT[zq])
            ds = (p * (dp - MS[zq, 1:2, :])).astype(BF)
            DK[...] += nn(ds, Q[zq])
            DV[...] += nn(p.astype(BF), DOs[zq])
            DQ[zq] += nn(TS[...], ds)
            return 0

        lax.fori_loop(zlo, zhi, one, 0)
        dk = DK[...] * scale
        dv = DV[...]
        KV[kh, kz, ky, :, 0:128] = dk[:, 0:128].astype(BF)
        KV[kh, kz, ky, :, 128:256] = (dk[:, 128:256] + dv[:, 0:128]).astype(BF)
        KV[kh, kz, ky, :, 256:384] = dv[:, 128:256].astype(BF)

    dk0, dk1, dk2 = {}, {}, {}
    turn = (1, 2, 3, 0)

    def far_tiles(k):
        kz = zs[k]
        key_tile(hx, kz, yx)
        dk1[k] = send(KV.at[hx, kz, yx], DKVr.at[1, kz], P2)
        key_tile(p2h, kz, p2y)
        dk0[k] = send(KV.at[p2h, kz, p2y], DKVr.at[0, kz], P2)

    def near_tile(k):
        kz = zs[k]
        key_tile(p1h, kz, p1y)
        dk1[k].wait_recv()
        KV[p1h, kz, p1y] = (KV[p1h, kz, p1y].astype(F32) + DKVr[1, kz].astype(F32)).astype(BF)
        dk2[k] = send(KV.at[p1h, kz, p1y], DKVr.at[2, kz], P1)

    def own_tile(kz, _):
        key_tile(h, kz, y)
        return 0

    rs_c(2)
    far_tiles(1)
    far_tiles(2)
    near_tile(1)
    far_tiles(3)
    near_tile(2)
    far_tiles(0)
    rs_b(1)
    near_tile(3)
    near_tile(0)
    rs_d(2)
    lax.fori_loop(0, 4, own_tile, 0)
    rs_b(0)

    def join(zt, _):
        dkv = KV[h, zt, y].astype(F32) + DKVr[0, zt].astype(F32) + DKVr[2, zt].astype(F32)
        dq = pltpu.roll(jnp.where(lane256 < 160, jnp.transpose(DQ[zt]) * scale, 0.0), 64, 1)
        DKVQ[zt, :, 0:256] = dkv[:, 0:256].astype(BF)
        DKVQ[zt, :, 256:384] = (dkv[:, 256:384] + dq[:, 0:128]).astype(BF)
        DKVQ[zt, :, 384:512] = dq[:, 128:256].astype(BF)
        return 0


    VS[...] = jnp.zeros((128, 512), F32)

    def first_grad(zt, _):
        d = DKVQ[zt]
        VS[98:99, :] += jnp.sum(d.astype(F32), axis=0, keepdims=True)

        def u_half(i, cols):
            u = nt(d, W[i].reshape(640, 512))
            VR[97:98, cols] += jnp.sum(u, axis=0, keepdims=True)
            U[zt, :, :, cols] = u.astype(BF).reshape(2, 128, 640)

        halves(u_half)

        return 0

    def gain_sum(i, _):
        zt = lax.div(i, 2)
        rows = pl.ds(pl.multiple_of(lax.rem(i, 2) * 64, 64), 64)
        n, _ = stats(T[zt, c, rows].astype(F32))
        VR[96:97, :] += jnp.sum(U[zt, c, rows].astype(F32) * n, axis=0, keepdims=True)
        return 0

    us, uz = {}, []

    def block_sum(k):
        us[k].wait_recv()
        zt = zs[k]
        U[zt, c] = (U[zt, c].astype(F32) + UR[zt].astype(F32)).astype(BF)
        if k:
            uz.append(send(U.at[zt, c], UZ.at[k - 1], dev(h, zt, y, c)))

    for i, k in enumerate(turn):
        dk0[k].wait_recv()
        dk2[k].wait_recv()
        join(zs[k], 0)
        first_grad(zs[k], 0)
        us[k] = send(U.at[zs[k], sib], UR.at[zs[k]], SIB)
        if i:
            block_sum(turn[i - 1])
        if i == 3:
            rs_c(1)
    block_sum(0)
    rs_c(0)
    lax.fori_loop(0, 8, gain_sum, 0)
    rs_e(2)
    rs_d(1)
    VS[99:100, :] = VS[98:99, :]
    vst = jnp.transpose(VS[...])
    vlane = lax.broadcasted_iota(jnp.int32, (160, 128), 1)
    colb[0:1280, :] = jnp.transpose(VR[...])
    rows = pl.ds(pl.multiple_of(t * 160, 8), 160)
    colb[rows, :] += jnp.where(vlane == 98, vst[320:480, :], 0.0) + jnp.where(
        vlane == 99, vst[160:320, :], 0.0
    )

    def head_grad(hh, _):
        g = tn(
            H[:, :, pl.ds(pl.multiple_of(hh * 640, 128), 640)].reshape(1024, 640),
            DKVQ[...].reshape(1024, 512),
        )
        DW[hh, :, :, :, 0:384] = g[:, 0:384].astype(BF).reshape(4, 2, 80, 384)
        last = g[:, 384:512] + colb[pl.ds(pl.multiple_of(hh * 640, 128), 640), :]
        DW[hh, :, :, :, 384:512] = last.astype(BF).reshape(4, 2, 80, 128)
        return 0

    lax.fori_loop(0, 2, head_grad, 0)
    dw1 = send(DW.at[hx, :, yx], DWr.at[1], P2)
    dw0 = send(DW.at[p2h, :, p2y], DWr.at[0], P2)
    rs_d(0)
    dw1.wait_recv()
    DW[p1h, :, p1y] = (DW[p1h, :, p1y].astype(F32) + DWr[1].astype(F32)).astype(BF)
    dw2 = send(DW.at[p1h, :, p1y], DWr.at[2], P1)
    dw0.wait_recv()
    dw2.wait_recv()
    left(wz)
    for k in range(4):
        DWz[k] = (
            DW[h, k, y].astype(F32) + DWr[0, k].astype(F32) + DWr[2, k].astype(F32)
        ).astype(BF)
    dwz = [send(DWz.at[zs[k]], DWh.at[z], dev(h, zs[k], y, c)) for k in range(1, 4)]
    DWh[z] = DWz[z]
    rs_e(1)
    rs_e(0)

    rx.wait_recv()
    pm = perm[pl.ds(h * 16 + b, 1), :]
    om0 = jnp.where(pm == b * 128 + i_sub, 1.0, 0.0).astype(BF)
    om1 = jnp.where(pm == (16 + b) * 128 + i_sub, 1.0, 0.0).astype(BF)

    def mix_half(i, cols):
        mixed_out[:, cols] = (tn(om0, RES[0, :, cols]) + tn(om1, RES[1, :, cols])).astype(BF)

    halves(mix_half)


    for cp in uz:
        cp.wait_recv()

    def last_rows(i, _):
        rows = pl.ds(pl.multiple_of(i * 32, 32), 32)
        u = U[z, c, rows].astype(F32)
        for k in range(3):
            u += UZ[k, rows].astype(F32)
        n, r = stats(tok[rows, :].astype(F32))
        wv = u * vec[0:1, :]
        gt = EX[rows, :] + r * (
            wv - jnp.mean(wv, axis=-1, keepdims=True) - n * jnp.mean(wv * n, axis=-1, keepdims=True)
        )
        gtok_out[rows, :] = gt.astype(BF)
        return 0

    lax.fori_loop(0, 4, last_rows, 0)

    for cp in dwz:
        cp.wait_recv()
    for k in range(4):
        wasm[k] = DWh[k].astype(F32)
    wr[...] = wasm[:, pl.ds(pl.multiple_of(sib * 40, 8), 40), :]
    wo = send(wr, WOr, SIB)
    left([wa])
    WP[c] = wasm[:, pl.ds(pl.multiple_of(c * 40, 8), 40), :]
    for w in (2, 1, 0):
        rs_f(w)
    wo.wait_recv()
    WP[sib] = WOr[...]
    total = jnp.zeros((40, 128), F32)
    for e in range(8):
        for i, dst in enumerate((gk, gv, gq)):
            dst[:, e * 160:(e + 1) * 160] = WP[e % 2, e // 2, :, i * 160:(i + 1) * 160]
        total += WP[e % 2, e // 2, :, 384:512]
    colb[0:40, :] = total
    vgo[...] = jnp.transpose(colb[0:128, :])[96:112, :]

    token_end()
    for cp in pending:
        cp.wait_send()

    assert count[0] <= NSEM, count[0]


NSEM = 192


def hand_over(*refs):
    n = len(refs) // 2
    sems = refs[-1]
    copies = [pltpu.make_async_copy(refs[i], refs[n + i], sems.at[i]) for i in range(n)]
    for cp in copies:
        cp.start()
    for cp in copies:
        cp.wait()


def fast_local(
    tokens, cotangent, permutation, seq_lengths, first_gain, first_bias, query_weight, query_bias,
    key_weight, value_weight, value_bias, output_weight, output_bias, second_gain, second_bias,
    expand_weight, expand_bias, contract_weight, contract_bias,
):
    vectors = [first_gain, first_bias, query_bias, value_bias, output_bias, second_gain, second_bias,
               expand_bias, contract_bias]
    vcol = jnp.pad(jnp.stack(vectors, axis=1).astype(F32), ((0, 0), (0, 23)))
    perm = permutation.reshape(32, 128)

    vm = pltpu.VMEM
    fshape = (2, 2, 4, 2, 80, 640)
    scratch = dict(
        WP=vm((2, 4, 40, 512), F32), FP=vm((2, 3, 40, 640), F32),
        T=vm((4, 2, 128, 1280), BF), H=vm((4, 256, 1280), BF), W=vm((2, 4, 2, 80, 512), BF),
        KV=vm((2, 4, 2, 256, 384), BF), Q=vm((4, 256, 256), BF), QT=vm((4, 256, 256), BF), OT=vm((4, 256, 256), F32),
        F=vm((3,) + fshape, BF), G=vm(fshape, BF), R0=vm((3, 2, 4, 2, 80, 640), BF),
        R1=vm((3, 2, 4, 80, 640), BF), R2=vm((3, 4, 80, 640), BF), R3=vm((3, 3, 80, 640), BF),
        FA=vm((3, 80, 640), F32), FR=vm((3, 40, 640), F32),
        wr=vm((4, 40, 512), F32), wasm=vm((4, 80, 512), F32),
        fr=vm((3, 40, 640), F32),
        colb=vm((1408, 128), F32), vec=vm((16, 1280), F32), bias=vm((8, 512), F32),
        MS=vm((4, 8, 256), F32), TS=vm((256, 256), BF),
        A=vm((8, 128, 256), BF), As=vm((4, 2, 128, 256), BF), C=vm((2, 128, 1280), BF),
        RES=vm((2, 128, 1280), BF), MID=vm((128, 1280), F32),
        EX=vm((128, 1280), F32), H2=vm((128, 1280), BF), ACT=vm((128, 1280), BF),
        CI=vm((128, 1280), BF), DE=vm((128, 1280), BF), GB=vm((128, 1280), BF),
        DOs=vm((4, 256, 256), BF), DOT=vm((4, 256, 256), BF), DOr=vm((4, 2, 128, 256), BF),
        DK=vm((256, 256), F32), DV=vm((256, 256), F32), DQ=vm((4, 256, 256), F32),
        DKVr=vm((3, 4, 256, 384), BF), DKVQ=vm((4, 256, 512), BF), U=vm((4, 2, 128, 1280), BF),
        UR=vm((4, 128, 1280), BF), UZ=vm((3, 128, 1280), BF), VR=vm((128, 1280), F32),
        VS=vm((128, 512), F32), DW=vm((2, 4, 2, 80, 512), BF),
        DWr=vm((3, 4, 80, 512), BF), DWz=vm((4, 80, 512), BF), DWh=vm((4, 80, 512), BF),
        WOr=vm((4, 40, 512), F32),
        ss=pltpu.SemaphoreType.DMA((NSEM,)), rs=pltpu.SemaphoreType.DMA((NSEM,)),
        lss=pltpu.SemaphoreType.DMA((5,)), lrs=pltpu.SemaphoreType.DMA((4,)),
    )
    vspec = pl.BlockSpec(memory_space=pltpu.VMEM)
    rows = jax.ShapeDtypeStruct((40, 1280), F32)
    tokens_out = jax.ShapeDtypeStruct((128, 1280), BF)
    mixed, gtok, gq, gk, gv, go, ge, gc, vg = pl.pallas_call(
        block_kernel,
        out_shape=(tokens_out, tokens_out) + (rows,) * 6 + (jax.ShapeDtypeStruct((16, 128), F32),),
        in_specs=[vspec, vspec, vspec, pl.BlockSpec(memory_space=pltpu.SMEM)] + [vspec] * 7,
        out_specs=(vspec,) * 9,
        scratch_shapes=list(scratch.values()),
        compiler_params=pltpu.CompilerParams(
            collective_id=0, has_side_effects=True, vmem_limit_bytes=63 * MB,
        ),
        cost_estimate=pl.CostEstimate(flops=12_000_000_000, bytes_accessed=6_000_000, transcendentals=5_000_000),
        name="block",
    )(tokens, cotangent, perm, seq_lengths, vcol, query_weight, key_weight, value_weight, output_weight,
      expand_weight, contract_weight)
    any_spec = pl.BlockSpec(memory_space=pl.ANY)
    mixed, gtok, gq, gk, gv, go, ge, gc = pl.pallas_call(
        hand_over,
        out_shape=(tokens_out, tokens_out) + (rows,) * 6,
        in_specs=[vspec] * 8,
        out_specs=(any_spec,) * 8,
        scratch_shapes=[pltpu.SemaphoreType.DMA((8,))],
        name="hand_over",
    )(mixed, gtok, gq, gk, gv, go, ge, gc)
    v = [vg[j, 0:40] for j in range(9)]
    return mixed, gtok, v[0], v[1], gq, v[2], gk, gv, v[3], go, v[4], v[5], v[6], ge, v[7], gc, v[8]


def shifted(array, axis, by):
    length = lax.axis_size(axis)
    return lax.ppermute(array, axis, [(i, (i + by) % length) for i in range(length)])


def normalize(values, gain, shift):
    centre = jnp.mean(values, axis=-1, keepdims=True)
    spread = jnp.mean((values - centre) ** 2, axis=-1, keepdims=True)
    return (values - centre) * lax.rsqrt(spread + 1e-05) * gain + shift


def exact_gelu(values):
    return jax.nn.gelu(values, approximate=False)


def layout_initial(permutation, blk_source, width, blk_count, head_count):
    rows = jnp.arange(width * head_count, dtype=jnp.int32)
    places = (rows // width * blk_count + blk_source) * width + rows % width
    return jnp.take(permutation, places)


def segment_of(initial, ends):
    return jnp.sum((initial[:, None] >= ends[None, :]).astype(jnp.int32), axis=1)


def permitted(query_orig, key_orig, ends):
    same = segment_of(query_orig, ends)[:, None] == segment_of(key_orig, ends)[None, :]
    return same & (key_orig[None, :] <= query_orig[:, None])


def outer_sum(left, right):
    return lax.dot_general(
        left, right, (((0,), (0,)), ((), ())), preferred_element_type=jnp.float32
    )


def back_product(left, right):
    return lax.dot_general(
        left, right, (((1,), (1,)), ((), ())), preferred_element_type=jnp.float32
    )


def block_terms(
    query_block,
    grad_block,
    log_block,
    agree_block,
    query_orig,
    key_block,
    value_block,
    key_orig,
    ends,
    scale,
):
    allowed = permitted(query_orig, key_orig, ends)
    scores = (
        jnp.einsum("qhd,khd->hqk", query_block, key_block, preferred_element_type=jnp.float32)
        * scale
    )
    weights = jnp.exp(jnp.where(allowed[None], scores - log_block[..., None], -1e30))
    value_term = jnp.einsum(
        "hqk,qhd->khd", weights.astype(jnp.bfloat16), grad_block, preferred_element_type=jnp.float32
    )
    product = jnp.einsum(
        "qhd,khd->hqk", grad_block, value_block, preferred_element_type=jnp.float32
    )
    score_grad = (weights * (product - agree_block[..., None])).astype(jnp.bfloat16)
    query_term = jnp.einsum(
        "hqk,khd->qhd", score_grad, key_block, preferred_element_type=jnp.float32
    )
    key_term = jnp.einsum(
        "hqk,qhd->khd", score_grad, query_block, preferred_element_type=jnp.float32
    )
    return (query_term, key_term, value_term)


def local(
    tokens,
    cotangent,
    permutation,
    seq_lengths,
    first_gain,
    first_bias,
    query_weight,
    query_bias,
    key_weight,
    value_weight,
    value_bias,
    output_weight,
    output_bias,
    second_gain,
    second_bias,
    expand_weight,
    expand_bias,
    contract_weight,
    contract_bias,
):
    width = tokens.shape[0]
    blk_count = lax.axis_size("blk")
    head_count = lax.axis_size("head")
    blk_index = lax.axis_index("blk")
    flat_index = lax.axis_index("head") * blk_count + blk_index
    count = seq_lengths.shape[0]
    before = jnp.arange(count)[None, :] <= jnp.arange(count)[:, None]
    ends = jnp.sum(jnp.where(before, seq_lengths[None, :], 0), axis=1)
    total = permutation.shape[0]
    numbers = jnp.arange(total, dtype=jnp.int32)
    inverse = jnp.zeros((total,), jnp.int32).at[permutation].set(numbers)
    local_rows = jnp.arange(width, dtype=jnp.int32)
    first_row = flat_index * width
    going = lax.dynamic_slice_in_dim(inverse, first_row, width)
    order_source = jnp.argsort(going)
    arriving = lax.dynamic_slice_in_dim(permutation, first_row, width)
    order_target = jnp.argsort(arriving // width // blk_count * width + local_rows)
    undo_target = jnp.argsort(order_target)
    undo_source = jnp.argsort(order_source)
    received = lax.all_to_all(
        jnp.take(tokens, order_source, axis=0), "head", split_axis=0, concat_axis=0, tiled=True
    )
    inputs = jnp.take(received, undo_target, axis=0).astype(jnp.float32)
    vectors = jnp.stack(
        [
            first_gain,
            first_bias,
            query_bias,
            value_bias,
            output_bias,
            second_gain,
            second_bias,
            expand_bias,
            contract_bias,
        ]
    )
    query_full, key_full, value_full, output_full, expand_full, contract_full, vector_stack = (
        lax.all_gather(query_weight, ("head", "blk"), axis=0, tiled=True),
        lax.all_gather(key_weight, ("head", "blk"), axis=0, tiled=True),
        lax.all_gather(value_weight, ("head", "blk"), axis=0, tiled=True),
        lax.all_gather(output_weight, ("head", "blk"), axis=0, tiled=True),
        lax.all_gather(expand_weight, ("head", "blk"), axis=0, tiled=True),
        lax.all_gather(contract_weight, ("head", "blk"), axis=0, tiled=True),
        lax.all_gather(vectors, ("head", "blk"), axis=1, tiled=True),
    )
    vector_full = vector_stack.astype(jnp.float32)
    first_hidden = normalize(inputs, vector_full[0], vector_full[1]).astype(jnp.bfloat16)
    queries = (
        jnp.dot(first_hidden, query_full, preferred_element_type=jnp.float32) + vector_full[2]
    ).astype(jnp.bfloat16)
    keys = jnp.dot(first_hidden, key_full, preferred_element_type=jnp.float32).astype(jnp.bfloat16)
    values = (
        jnp.dot(first_hidden, value_full, preferred_element_type=jnp.float32) + vector_full[3]
    ).astype(jnp.bfloat16)
    head_queries, head_keys, head_values = (
        lax.all_to_all(queries, "head", split_axis=1, concat_axis=0, tiled=True),
        lax.all_to_all(keys, "head", split_axis=1, concat_axis=0, tiled=True),
        lax.all_to_all(values, "head", split_axis=1, concat_axis=0, tiled=True),
    )
    rows_here = width * head_count
    feature_here = head_queries.shape[1]
    heads_here = feature_here // HEAD_DIM
    scale = HEAD_DIM ** (-0.5)
    query_initial = layout_initial(permutation, blk_index, width, blk_count, head_count)
    shaped_queries = head_queries.reshape(rows_here, heads_here, HEAD_DIM)
    shaped_keys = head_keys.reshape(rows_here, heads_here, HEAD_DIM)
    shaped_values = head_values.reshape(rows_here, heads_here, HEAD_DIM)
    start_state = (
        jnp.full((heads_here, rows_here), -1e30, jnp.float32),
        jnp.zeros((heads_here, rows_here), jnp.float32),
        jnp.zeros((heads_here, rows_here, HEAD_DIM), jnp.float32),
    )
    carry = start_state
    key_piece = lax.all_gather(head_keys, "blk", axis=0, tiled=True)
    value_piece = lax.all_gather(head_values, "blk", axis=0, tiled=True)
    pieces = key_piece.shape[0] // rows_here
    key_blocks = key_piece.reshape(pieces, rows_here, heads_here, HEAD_DIM)
    value_blocks = value_piece.reshape(pieces, rows_here, heads_here, HEAD_DIM)

    def visit(state, item):
        key_block, value_block, offset = item
        running, total_sum, gathered = state
        key_initial = layout_initial(permutation, offset, width, blk_count, head_count)
        allowed = permitted(query_initial, key_initial, ends)
        scores = (
            jnp.einsum(
                "qhd,khd->hqk", shaped_queries, key_block, preferred_element_type=jnp.float32
            )
            * scale
        )
        scores = jnp.where(allowed[None], scores, -1e30)
        newest = jnp.maximum(running, jnp.max(scores, axis=-1))
        factor = jnp.exp(running - newest)
        exponent = jnp.where(allowed[None], jnp.exp(scores - newest[..., None]), 0.0)
        total_sum = factor * total_sum + jnp.sum(exponent, axis=-1)
        gathered = factor[..., None] * gathered + jnp.einsum(
            "hqk,khd->hqd",
            exponent.astype(jnp.bfloat16),
            value_block,
            preferred_element_type=jnp.float32,
        )
        return ((newest, total_sum, gathered), None)

    carry, unused = lax.scan(
        visit, carry, (key_blocks, value_blocks, jnp.arange(pieces, dtype=jnp.int32))
    )
    running, total_sum, gathered = carry
    attended = gathered / total_sum[..., None]
    log_total = running + jnp.log(total_sum)
    attended_rows = jnp.transpose(attended, (1, 0, 2)).reshape(rows_here, feature_here)
    merged = lax.all_to_all(
        attended_rows.astype(jnp.bfloat16), "head", split_axis=0, concat_axis=1, tiled=True
    )
    middle = (
        inputs + jnp.dot(merged, output_full, preferred_element_type=jnp.float32) + vector_full[4]
    )
    second_hidden = normalize(middle, vector_full[5], vector_full[6]).astype(jnp.bfloat16)
    expanded = (
        jnp.dot(second_hidden, expand_full, preferred_element_type=jnp.float32) + vector_full[7]
    )
    activated = exact_gelu(expanded).astype(jnp.bfloat16)
    result = (
        middle
        + jnp.dot(activated, contract_full, preferred_element_type=jnp.float32)
        + vector_full[8]
    )
    grad_contract = outer_sum(activated, cotangent)
    grad_contract_bias = jnp.sum(cotangent.astype(jnp.float32), axis=0)
    grad_activated = back_product(cotangent, contract_full)
    unused_value, gelu_pull = jax.vjp(exact_gelu, expanded)
    grad_expanded = gelu_pull(grad_activated)[0].astype(jnp.bfloat16)
    grad_expand = outer_sum(second_hidden, grad_expanded)
    grad_expand_bias = jnp.sum(grad_expanded.astype(jnp.float32), axis=0)
    grad_second = back_product(grad_expanded, expand_full)
    unused_second, second_pull = jax.vjp(normalize, middle, vector_full[5], vector_full[6])
    grad_middle_norm, grad_second_gain, grad_second_bias = second_pull(grad_second)
    grad_middle = cotangent.astype(jnp.float32) + grad_middle_norm
    grad_branch = grad_middle.astype(jnp.bfloat16)
    grad_output = outer_sum(merged, grad_branch)
    grad_output_bias = jnp.sum(grad_branch.astype(jnp.float32), axis=0)
    grad_merged = back_product(grad_branch, output_full).astype(jnp.bfloat16)
    head_grad = lax.all_to_all(grad_merged, "head", split_axis=1, concat_axis=0, tiled=True)
    shaped_grad = head_grad.reshape(rows_here, heads_here, HEAD_DIM)
    agreement = jnp.einsum("qhd,hqd->hq", shaped_grad.astype(jnp.float32), attended)
    zero_rows = jnp.zeros((rows_here, heads_here, HEAD_DIM), jnp.float32)

    def key_turn(turn, state):
        moving_keys, moving_values, key_total, value_total, query_total = state
        source = (blk_index - turn) % blk_count
        key_orig = layout_initial(permutation, source, width, blk_count, head_count)
        query_term, key_term, value_term = block_terms(
            shaped_queries,
            shaped_grad,
            log_total,
            agreement,
            query_initial,
            moving_keys,
            moving_values,
            key_orig,
            ends,
            scale,
        )
        moving_keys, moving_values = shifted((moving_keys, moving_values), "blk", 1)
        key_total, value_total = (
            shifted((key_total + key_term).astype(jnp.bfloat16), "blk", 1).astype(jnp.float32),
            shifted((value_total + value_term).astype(jnp.bfloat16), "blk", 1).astype(jnp.float32),
        )
        return (moving_keys, moving_values, key_total, value_total, query_total + query_term)

    final_state = lax.fori_loop(
        0, blk_count, key_turn, (shaped_keys, shaped_values, zero_rows, zero_rows, zero_rows)
    )
    key_grad_heads = final_state[2]
    value_grad_heads = final_state[3]
    query_grad_heads = final_state[4]
    query_grad_rows = (
        (query_grad_heads * scale).astype(jnp.bfloat16).reshape(rows_here, feature_here)
    )
    key_grad_rows = (key_grad_heads * scale).astype(jnp.bfloat16).reshape(rows_here, feature_here)
    value_grad_rows = value_grad_heads.astype(jnp.bfloat16).reshape(rows_here, feature_here)
    grad_queries, grad_keys, grad_values = (
        lax.all_to_all(query_grad_rows, "head", split_axis=0, concat_axis=1, tiled=True),
        lax.all_to_all(key_grad_rows, "head", split_axis=0, concat_axis=1, tiled=True),
        lax.all_to_all(value_grad_rows, "head", split_axis=0, concat_axis=1, tiled=True),
    )
    grad_query = outer_sum(first_hidden, grad_queries)
    grad_key = outer_sum(first_hidden, grad_keys)
    grad_value = outer_sum(first_hidden, grad_values)
    grad_query_bias = jnp.sum(grad_queries.astype(jnp.float32), axis=0)
    grad_value_bias = jnp.sum(grad_values.astype(jnp.float32), axis=0)
    grad_first = (
        back_product(grad_queries, query_full)
        + back_product(grad_keys, key_full)
        + back_product(grad_values, value_full)
    )
    unused_first, first_pull = jax.vjp(normalize, inputs, vector_full[0], vector_full[1])
    grad_inputs_norm, grad_first_gain, grad_first_bias = first_pull(grad_first)
    grad_inputs = (grad_middle + grad_inputs_norm).astype(jnp.bfloat16)
    vector_grads = jnp.stack(
        [
            grad_first_gain,
            grad_first_bias,
            grad_query_bias,
            grad_value_bias,
            grad_output_bias,
            grad_second_gain,
            grad_second_bias,
            grad_expand_bias,
            grad_contract_bias,
        ]
    )
    summed = (
        lax.psum_scatter(grad_query, ("head", "blk"), scatter_dimension=0, tiled=True),
        lax.psum_scatter(grad_key, ("head", "blk"), scatter_dimension=0, tiled=True),
        lax.psum_scatter(grad_value, ("head", "blk"), scatter_dimension=0, tiled=True),
        lax.psum_scatter(grad_output, ("head", "blk"), scatter_dimension=0, tiled=True),
        lax.psum_scatter(grad_expand, ("head", "blk"), scatter_dimension=0, tiled=True),
        lax.psum_scatter(grad_contract, ("head", "blk"), scatter_dimension=0, tiled=True),
        lax.psum_scatter(vector_grads, ("head", "blk"), scatter_dimension=1, tiled=True),
    )
    vector_shares = summed[6]
    returned = lax.all_to_all(
        jnp.take(grad_inputs, order_target, axis=0), "head", split_axis=0, concat_axis=0, tiled=True
    )
    grad_tokens = jnp.take(returned, undo_source, axis=0)
    return (
        result.astype(jnp.bfloat16),
        grad_tokens,
        vector_shares[0],
        vector_shares[1],
        summed[0],
        vector_shares[2],
        summed[1],
        summed[2],
        vector_shares[3],
        summed[3],
        vector_shares[4],
        vector_shares[5],
        vector_shares[6],
        summed[4],
        vector_shares[7],
        summed[5],
        vector_shares[8],
    )


def solution(mesh):
    return jax.shard_map(
        fast_local if mesh.shape["head"] == 2 and mesh.shape["blk"] == 16 else local,
        mesh=mesh,
        in_specs=(
            P(("head", "blk"), None),
            P(("head", "blk"), None),
            P(),
            P(),
            P(("head", "blk")),
            P(("head", "blk")),
            P(("head", "blk"), None),
            P(("head", "blk")),
            P(("head", "blk"), None),
            P(("head", "blk"), None),
            P(("head", "blk")),
            P(("head", "blk"), None),
            P(("head", "blk")),
            P(("head", "blk")),
            P(("head", "blk")),
            P(("head", "blk"), None),
            P(("head", "blk")),
            P(("head", "blk"), None),
            P(("head", "blk")),
        ),
        out_specs=(
            P(("head", "blk"), None),
            P(("head", "blk"), None),
            P(("head", "blk")),
            P(("head", "blk")),
            P(("head", "blk"), None),
            P(("head", "blk")),
            P(("head", "blk"), None),
            P(("head", "blk"), None),
            P(("head", "blk")),
            P(("head", "blk"), None),
            P(("head", "blk")),
            P(("head", "blk")),
            P(("head", "blk")),
            P(("head", "blk"), None),
            P(("head", "blk")),
            P(("head", "blk"), None),
            P(("head", "blk")),
        ),
        check_vma=False,
    )
```

```python
import functools
import jax
import jax.numpy as jnp
from jax import lax
from jax.experimental import pallas as pl
from jax.experimental.pallas import tpu as pltpu
from jax.sharding import PartitionSpec as P

HEAD_DIM = 160
MESH = pl.DeviceIdType.MESH
BF = jnp.bfloat16
F32 = jnp.float32
MB = 1 << 20


def nn(a, b):
    return lax.dot_general(a, b, (((1,), (0,)), ((), ())), preferred_element_type=F32)


def nt(a, b):
    return lax.dot_general(a, b, (((1,), (1,)), ((), ())), preferred_element_type=F32)


def tn(a, b):
    return lax.dot_general(a, b, (((0,), (0,)), ((), ())), preferred_element_type=F32)


def stats(v):
    centre = jnp.mean(v, axis=-1, keepdims=True)
    off = v - centre
    spread = jnp.mean(off * off, axis=-1, keepdims=True)
    r = lax.rsqrt(spread + 1e-05)
    return off * r, r


def block_kernel(
    tok, cot, perm, lens, vcol, wq, wk, wv, wts0, wts1, wts2,
    mixed_out, gtok_out, gq, gk, gv, fo0, fo1, fo2, vgo,
    WP, FP, T, H, W, KV, Q, QT, OT, F, G, R0, R1, R2, R3, FA, FR,
    wr, wasm, fr, colb, vec, bias,
    MS, TS, A, As, C, RES, MID, EX, H2, ACT, CI, DE, GB, DOs, DOT, DOr,
    DK, DV, DQ, DKVr, DKVQ, U, UR, UZ, VR, VS, DW, DWr, DWz, DWh, WOr,
    ss, rs, lss, lrs,
):
    h = lax.axis_index("head")
    b = lax.axis_index("blk")
    z = lax.div(b, 4)
    y = lax.rem(lax.div(b, 2), 2)
    c = lax.rem(b, 2)
    sib = 1 - c
    hx = 1 - h
    yx = 1 - y
    t = z * 2 + c
    first = c == 0
    p1h = jnp.where(first, hx, h)
    p1y = jnp.where(first, y, yx)
    p2h = jnp.where(first, h, hx)
    p2y = jnp.where(first, yx, y)

    def dev(hh, zz, yy, cc):
        return (hh, zz * 4 + yy * 2 + cc)

    zs = [lax.rem(z + k, 4) for k in range(4)]
    zr = [lax.rem(z + 4 - k, 4) for k in range(4)]
    SIB = dev(h, z, y, sib)
    P1 = dev(p1h, z, p1y, c)
    P2 = dev(p2h, z, p2y, c)
    XP = dev(hx, z, y, c)
    YP = dev(h, z, yx, c)

    count = [0]

    def desc(src, dst, device):
        i = count[0]
        count[0] += 1
        return pltpu.make_async_remote_copy(
            src_ref=src, dst_ref=dst, send_sem=ss.at[i], recv_sem=rs.at[i],
            device_id=device, device_id_type=MESH,
        )

    pending = []

    def send(src, dst, device):
        cp = desc(src, dst, device)
        cp.start()
        pending.append(cp)
        return cp

    def left(cps):
        for cp in cps:
            cp.wait_send()
        keep = [cp for cp in pending if not any(cp is one for one in cps)]
        pending[:] = keep

    bar = pltpu.get_barrier_semaphore()
    for k in range(1, 4):
        pl.semaphore_signal(bar, inc=1, device_id=dev(h, zs[k], y, c), device_id_type=MESH)
        pl.semaphore_signal(bar, inc=1, device_id=dev(h, zs[k], y, sib), device_id_type=MESH)
    for peer in (SIB, XP, YP):
        pl.semaphore_signal(bar, inc=1, device_id=peer, device_id_type=MESH)

    fout = (fo0, fo1, fo2)
    for e in range(8):
        for i, src in enumerate((wk, wv, wq)):
            WP[e % 2, e // 2, :, i * 160:(i + 1) * 160] = src[:, e * 160:(e + 1) * 160].astype(F32)
        WP[e % 2, e // 2, :, 480:512] = vcol[...]
    for w, src in enumerate((wts0, wts1, wts2)):
        for half in range(2):
            FP[half, w] = src[:, half * 640:(half + 1) * 640].astype(F32)

    pl.semaphore_wait(bar, 9)

    up, down = z < 3, z > 0
    UP = dev(h, jnp.minimum(z + 1, 3), y, c)
    DOWN = dev(h, jnp.maximum(z - 1, 0), y, c)
    order = [
        z,
        jnp.where(z == 0, 1, jnp.where(z == 3, 2, jnp.where(z == 1, 0, 3))),
        jnp.where(z == 0, 2, jnp.where(z == 3, 1, jnp.where(z == 1, 2, 1))),
        jnp.where(z == 0, 3, jnp.where(z == 3, 0, jnp.where(z == 1, 3, 0))),
    ]

    def tcopy(src, zt, si, device):
        return pltpu.make_async_remote_copy(
            src_ref=src, dst_ref=T.at[zt, c], send_sem=lss.at[si], recv_sem=lrs.at[zt],
            device_id=device, device_id_type=MESH,
        )

    ts = []

    def token_start():
        pl.when(up)(tcopy(tok, z, 0, UP).start)
        pl.when(down)(tcopy(tok, z, 1, DOWN).start)
        ts.append(send(tok, T.at[z, c], SIB))

    def token_step(k):
        zt = order[k]
        here = T.at[zt, c]
        tcopy(here, zt, 0, UP).wait_recv()
        pl.when((zt < z) & up)(tcopy(here, zt, 1 + k, UP).start)
        pl.when((zt > z) & down)(tcopy(here, zt, 1 + k, DOWN).start)
        ts.append(send(here, here, SIB))

    def token_end():
        pl.when(up)(tcopy(tok, z, 0, UP).wait_send)
        pl.when(down)(tcopy(tok, z, 1, DOWN).wait_send)
        for k in range(1, 4):
            zt = order[k]
            here = T.at[zt, c]
            pl.when((zt < z) & up)(tcopy(here, zt, 1 + k, UP).wait_send)
            pl.when((zt > z) & down)(tcopy(here, zt, 1 + k, DOWN).wait_send)

    wa = send(WP.at[sib], wr, SIB)
    fa = send(FP.at[sib], fr, SIB)
    cx = send(cot, C.at[h], XP)
    T[z, c] = tok[...]
    C[h] = cot[...]

    wa.wait_recv()
    wasm[:, pl.ds(pl.multiple_of(c * 40, 8), 40), :] = WP[c]
    wasm[:, pl.ds(pl.multiple_of(sib * 40, 8), 40), :] = wr[...]
    for k in range(4):
        DWz[k] = wasm[k].astype(BF)
    W[h, z, y] = DWz[z]
    wz = [send(DWz.at[zs[k]], W.at[h, z, y], dev(h, zs[k], y, c)) for k in range(1, 4)]
    fa.wait_recv()
    FA[:, pl.ds(pl.multiple_of(c * 40, 8), 40), :] = FP[c]
    FA[:, pl.ds(pl.multiple_of(sib * 40, 8), 40), :] = fr[...]
    for w in range(3):
        F[w, c, h, z, y] = FA[w].astype(BF)

    fz = [None] * 3

    def f_line(w):
        own = F.at[w, c, h, z, y]
        fz[w] = [send(own, own, dev(h, zs[k], y, c)) for k in range(1, 4)]

    f1, f2a, f2b, fs = [None] * 3, [None] * 3, [None] * 3, []

    def f_plane(w):
        for cp in fz[w]:
            cp.wait_recv()
        own = F.at[w, c, h, :, y]
        f1[w] = send(own, own, P1)
        f2a[w] = send(own, own, P2)
        one = send(own, own, SIB)
        fs.append(one)
        fs_w[id(one)] = w

    def f_forward(w):
        f1[w].wait_recv()
        got = F.at[w, c, p1h, :, p1y]
        f2b[w] = send(got, got, P2)
        one = send(got, got, SIB)
        fs.append(one)
        fs_w[id(one)] = w

    flast = [None] * 3
    fs_w = {}

    def f_last(w):
        f2a[w].wait_recv()
        got = F.at[w, c, p2h, :, p2y]
        one = send(got, got, SIB)
        f2b[w].wait_recv()
        got = F.at[w, c, hx, :, yx]
        flast[w] = [one, send(got, got, SIB)]

    f_line(0)
    token_start()
    for cp in wz:
        cp.wait_recv()
    own = W.at[h, :, y]
    w1 = send(own, own, P1)
    w2 = send(own, own, P2)
    w1.wait_recv()
    got = W.at[p1h, :, p1y]
    w3 = send(got, got, P2)
    f_plane(0)
    w2.wait_recv()
    w3.wait_recv()

    def tcol(hh, _):
        colb[pl.ds(pl.multiple_of(hh * 640, 128), 640), :] = (
            W[hh, :, :, :, 384:512].reshape(640, 128).astype(F32)
        )
        return 0

    lax.fori_loop(0, 2, tcol, 0)
    colb[1280:1408, :] = jnp.zeros((128, 128), F32)
    vec[...] = jnp.transpose(colb[0:1280, :])[96:112, :]
    mine = jnp.transpose(colb[pl.ds(pl.multiple_of(t * 160, 8), 256), :])
    bias[...] = jnp.zeros((8, 512), F32)
    bias[0:1, 160:320] = mine[99:100, 0:160]
    bias[0:1, 320:480] = mine[98:99, 0:160]

    lane256 = lax.broadcasted_iota(jnp.int32, (256, 256), 1)

    kv1, kv2, kv3 = [], [], []

    def project(k):
        zt = order[k]
        ts[k].wait_recv()

        def norm(i, _):
            rows = pl.ds(pl.multiple_of(lax.rem(i, 2) * 64, 64), 64)
            n, _ = stats(T[zt, lax.div(i, 2), rows].astype(F32))
            H[zt, pl.ds(pl.multiple_of(i * 64, 64), 64)] = (n * vec[0:1, :] + vec[1:2, :]).astype(BF)
            return 0

        lax.fori_loop(0, 4, norm, 0)
        kvq = nn(H[zt], W[...].reshape(1280, 512)) + bias[0:1, :]
        KV[h, zt, y] = kvq[:, 0:384].astype(BF)
        qr = pltpu.roll(kvq[:, 256:512], 192, 1)
        qr = jnp.where(lane256 < 160, qr, 0.0)
        Q[zt] = qr.astype(BF)
        QT[zt] = jnp.transpose(qr).astype(BF)
        src = KV.at[h, zt, y]
        kv1.append(send(src, src, P1))
        kv2.append(send(src, src, P2))

    def kv_forward(k):
        kv1[k].wait_recv()
        got = KV.at[p1h, order[k], p1y]
        kv3.append(send(got, got, P2))

    scale = HEAD_DIM ** -0.5
    ends = []
    run = 0
    for e in range(8):
        run = run + lens[e]
        ends.append(run)

    def seg_of(pos):
        s = jnp.zeros_like(pos)
        for e in range(7):
            s = jnp.where(pos >= ends[e], ends[e], s)
        return s

    def rowpos(zt):
        return (h * 8 + zt * 2 + y) * 256

    def pair_range(kt):
        base = kt - h * 8 - y
        zlo = jnp.maximum(lax.div(base + 33, 2) - 16, 0)
        zhi = jnp.minimum(lax.div(base + 40, 2) - 16, 3) + 1
        return zlo, zhi

    def allowed(kt, zq):
        kpos = kt * 256 + lax.broadcasted_iota(jnp.int32, (256, 1), 0)
        qpos = (h * 8 + zq * 2 + y) * 256 + lax.broadcasted_iota(jnp.int32, (1, 256), 1)
        return (kpos >= seg_of(qpos)) & (kpos <= qpos)

    def absorb(gh, kz, gy):
        kt = gh * 8 + kz * 2 + gy
        zlo, zhi = pair_range(kt)
        TS[...] = jnp.transpose(KV[gh, kz, gy, :, 128:384].astype(F32)).astype(BF)
        kk = KV.at[gh, kz, gy]

        def one(zq, _):
            s = jnp.where(allowed(kt, zq), nn(kk[:, 0:256], QT[zq]) * scale, -1e30)
            m = MS[zq, 0:1, :]
            mn = jnp.maximum(m, jnp.max(s, axis=0, keepdims=True))
            f = jnp.exp(m - mn)
            p = jnp.exp(s - mn)
            MS[zq, 0:1, :] = mn
            MS[zq, 1:2, :] = MS[zq, 1:2, :] * f + jnp.sum(p, axis=0, keepdims=True)
            OT[zq] = OT[zq] * f + nn(TS[...], p.astype(BF))
            return 0

        lax.fori_loop(zlo, zhi, one, 0)
        return 0

    def group(gh, gy):
        lax.fori_loop(0, 4, lambda kz, _: absorb(gh, kz, gy), 0)

    OT[...] = jnp.zeros((4, 256, 256), F32)
    MS[:, 0:1, :] = jnp.full((4, 1, 256), -1e30, F32)
    MS[:, 1:2, :] = jnp.zeros((4, 1, 256), F32)

    def finish(zt):
        m, l = MS[zt, 0:1, :], MS[zt, 1:2, :]
        o = OT[zt] / l
        OT[zt] = o
        MS[zt, 0:1, :] = m + jnp.log(l)
        turned = jnp.concatenate([o[32:256, :], o[0:32, :]], axis=0)
        As[zt] = jnp.transpose(turned).astype(BF).reshape(2, 128, 256)

    project(0)
    token_step(1)
    f_forward(0)
    project(1)
    token_step(2)
    f_line(1)
    project(2)
    kv_forward(0)
    token_step(3)
    f_line(2)
    project(3)
    kv_forward(1)
    kv_forward(2)
    kv_forward(3)
    f_plane(1)
    group(h, y)
    f_plane(2)
    group(p1h, p1y)
    f_forward(1)
    for cp in kv2:
        cp.wait_recv()
    group(p2h, p2y)
    for cp in kv3:
        cp.wait_recv()
    group(hx, yx)
    f_forward(2)
    asend = []
    for k in (1, 2, 3, 0):
        zt = zs[k]
        finish(zt)
        for cc in (c, sib):
            if k == 0 and cc is c:
                continue
            asend.append(send(As.at[zt, cc], A.at[t], dev(h, zt, y, cc)))
    A[t] = As[z, c]

    f_last(0)
    for cp in asend:
        cp.wait_recv()

    def f_done(w):
        for cp in flast[w] + fs[2 * w:2 * w + 2]:
            cp.wait_recv()

    fs.sort(key=lambda cp: fs_w[id(cp)])
    f_done(0)
    f_last(1)

    VR[...] = jnp.zeros((128, 1280), F32)

    def halves(fn):
        def run_half(i, _):
            fn(i, pl.ds(pl.multiple_of(i * 640, 128), 640))
            return 0

        lax.fori_loop(0, 2, run_half, 0)

    def out_half(i, cols):
        acc = tok[:, cols].astype(F32) + vec[4:5, cols]
        for e in range(8):
            acc += nn(A[e, :, 0:160], F[0, i, e // 4, e % 4].reshape(160, 640))
        MID[:, cols] = acc

    halves(out_half)

    def norm2(i, _):
        rows = pl.ds(pl.multiple_of(i * 32, 32), 32)
        n2, _ = stats(MID[rows, :])
        H2[rows, :] = (n2 * vec[5:6, :] + vec[6:7, :]).astype(BF)
        return 0

    lax.fori_loop(0, 4, norm2, 0)

    def exp_half(i, cols):
        ex = nn(H2[...], F[1, i].reshape(1280, 640)) + vec[7:8, cols]
        phi = 0.5 * (1.0 + lax.erf(ex * (0.5**0.5)))
        ACT[:, cols] = (ex * phi).astype(BF)
        EX[:, cols] = phi + ex * jnp.exp(-0.5 * ex * ex) * 0.3989422804014327

    f_done(1)
    f_last(2)
    halves(exp_half)

    cx.wait_recv()
    i_sub = lax.broadcasted_iota(jnp.int32, (128, 128), 0)
    mine0 = (h * 16 + b) * 128
    pr0, pr1 = perm[pl.ds(b, 1), :], perm[pl.ds(16 + b, 1), :]
    oh0 = jnp.where(pr0 == mine0 + i_sub, 1.0, 0.0).astype(BF)
    oh1 = jnp.where(pr1 == mine0 + i_sub, 1.0, 0.0).astype(BF)

    def cot_half(i, cols):
        ci = nn(oh0, C[0, :, cols]) + nn(oh1, C[1, :, cols])
        CI[:, cols] = ci.astype(BF)
        VR[104:105, cols] = jnp.sum(ci, axis=0, keepdims=True)

    halves(cot_half)

    def outer(left, right, dst):
        def one(i, _):
            hh, half = lax.div(i, 2), lax.rem(i, 2)
            g = tn(
                left[:, pl.ds(pl.multiple_of(hh * 640, 128), 640)],
                right[:, pl.ds(pl.multiple_of(half * 640, 128), 640)],
            )
            dst[half, hh] = g.astype(BF).reshape(4, 2, 80, 640)
            return 0

        lax.fori_loop(0, 4, one, 0)

    Gw = [F.at[1], F.at[2], G]
    ra = [None] * 3

    def rs_a(w):
        ra[w] = send(Gw[w].at[sib], R0.at[w], SIB)

    r1, r2s, r3, r4 = [None] * 3, [None] * 3, [None] * 3, [None] * 3

    def rs_b(w):
        ra[w].wait_recv()
        gw = Gw[w]

        def one(i, _):
            ih, iz = lax.div(i, 4), lax.rem(i, 4)
            gw[c, ih, iz] = (gw[c, ih, iz].astype(F32) + R0[w, ih, iz].astype(F32)).astype(BF)
            return 0

        lax.fori_loop(0, 8, one, 0)
        r1[w] = [
            send(gw.at[c, hx, :, yx], R1.at[w, 1], P2),
            send(gw.at[c, p2h, :, p2y], R1.at[w, 0], P2),
        ]

    def rs_c(w):
        gw = Gw[w]
        for cp in r1[w]:
            cp.wait_recv()

        def one(i, _):
            gw[c, p1h, i, p1y] = (gw[c, p1h, i, p1y].astype(F32) + R1[w, 1, i].astype(F32)).astype(BF)
            return 0

        lax.fori_loop(0, 4, one, 0)
        r2s[w] = send(gw.at[c, p1h, :, p1y], R2.at[w], P1)

    def rs_d(w):
        gw = Gw[w]
        r2s[w].wait_recv()

        def two(i, _):
            gw[c, h, i, y] = (
                gw[c, h, i, y].astype(F32) + R1[w, 0, i].astype(F32) + R2[w, i].astype(F32)
            ).astype(BF)
            return 0

        lax.fori_loop(0, 4, two, 0)
        r3[w] = [send(gw.at[c, h, zs[k], y], R3.at[w, k - 1], dev(h, zs[k], y, c)) for k in range(1, 4)]

    def rs_e(w):
        gw = Gw[w]
        total = gw[c, h, z, y].astype(F32)
        for k in range(1, 4):
            r3[w][k - 1].wait_recv()
            total += R3[w, k - 1].astype(F32)
        FA[w] = total
        r4[w] = send(FA.at[w, pl.ds(pl.multiple_of(sib * 40, 8), 40)], FR.at[w], SIB)

    def rs_f(w):
        r4[w].wait_recv()
        fout[w][:, pl.ds(pl.multiple_of(c * 640, 128), 640)] = FA[w, pl.ds(pl.multiple_of(c * 40, 8), 40)]
        fout[w][:, pl.ds(pl.multiple_of(sib * 640, 128), 640)] = FR[w]

    outer(ACT, CI, G)
    rs_a(2)
    f_done(2)
    def con_half(i, cols):
        res = MID[:, cols] + nn(ACT[...], F[2, i].reshape(1280, 640)) + vec[8:9, cols]
        RES[h, :, cols] = res.astype(BF)

    halves(con_half)
    rx = send(RES.at[h], RES.at[h], XP)

    def act_half(i, cols):
        f0, f1w = F[2, 0, i].reshape(640, 640), F[2, 1, i].reshape(640, 640)
        dact = nt(CI[:, 0:640], f0) + nt(CI[:, 640:1280], f1w)
        de = (dact * EX[:, cols]).astype(BF)
        DE[:, cols] = de
        VR[103:104, cols] = jnp.sum(de.astype(F32), axis=0, keepdims=True)

    halves(act_half)
    def back_half(i, cols):
        f0, f1w = F[1, 0, i].reshape(640, 640), F[1, 1, i].reshape(640, 640)
        EX[:, cols] = nt(DE[:, 0:640], f0) + nt(DE[:, 640:1280], f1w)

    left([cp for row in fz + flast for cp in row] + f1 + f2a + f2b + fs)
    outer(H2, DE, F.at[2])
    rs_a(1)
    rs_b(2)
    halves(back_half)

    def norm2_back(i, _):
        rows = pl.ds(pl.multiple_of(i * 32, 32), 32)
        dh2 = EX[rows, :]
        n2, r2 = stats(MID[rows, :])
        VR[101:102, :] += jnp.sum(dh2 * n2, axis=0, keepdims=True)
        VR[102:103, :] += jnp.sum(dh2, axis=0, keepdims=True)
        wv = dh2 * vec[5:6, :]
        dmid = CI[rows, :].astype(F32) + r2 * (
            wv - jnp.mean(wv, axis=-1, keepdims=True) - n2 * jnp.mean(wv * n2, axis=-1, keepdims=True)
        )
        EX[rows, :] = dmid
        gb = dmid.astype(BF)
        GB[rows, :] = gb
        VR[100:101, :] += jnp.sum(gb.astype(F32), axis=0, keepdims=True)
        return 0

    lax.fori_loop(0, 4, norm2_back, 0)
    left(asend)
    As[...] = jnp.zeros((4, 2, 128, 256), BF)

    def dattn(e, _):
        eh, ez = lax.div(e, 4), lax.rem(e, 4)
        da = nt(GB[:, 0:640], F[0, 0, eh, ez].reshape(160, 640)) + nt(
            GB[:, 640:1280], F[0, 1, eh, ez].reshape(160, 640)
        )
        As[lax.div(e, 2), lax.rem(e, 2), :, 0:160] = da.astype(BF)
        return 0

    lax.fori_loop(0, 8, dattn, 0)
    dos = []
    for k in range(4):
        for cc in (c, sib):
            if k == 0 and cc is c:
                continue
            dos.append(send(As.at[zs[k], cc], DOr.at[z, c], dev(h, zs[k], y, cc)))
    DOr[z, c] = As[z, c]


    def outo(e, _):
        def one(half, _):
            g = tn(A[e, :, 0:160], GB[:, pl.ds(pl.multiple_of(half * 640, 128), 640)])
            F[1, half, lax.div(e, 4), lax.rem(e, 4)] = g.astype(BF).reshape(2, 80, 640)
            return 0

        lax.fori_loop(0, 2, one, 0)
        return 0

    lax.fori_loop(0, 8, outo, 0)
    rs_a(0)

    for cp in dos:
        cp.wait_recv()
    left(kv1 + kv2 + kv3)

    def prep(zt, _):
        do = DOr[zt].reshape(256, 256).astype(F32)
        DOs[zt] = pltpu.roll(do, 32, 1).astype(BF)
        dt = jnp.transpose(do)
        dt = jnp.concatenate([dt[224:256, :], dt[0:224, :]], axis=0)
        DOT[zt] = dt.astype(BF)
        MS[zt, 1:2, :] = jnp.sum(dt * OT[zt], axis=0, keepdims=True)
        DQ[zt] = jnp.zeros((256, 256), F32)
        return 0

    lax.fori_loop(0, 4, prep, 0)

    def key_tile(kh, kz, ky):
        kt = kh * 8 + kz * 2 + ky
        zlo, zhi = pair_range(kt)
        DK[...] = jnp.zeros((256, 256), F32)
        DV[...] = jnp.zeros((256, 256), F32)
        tile = KV.at[kh, kz, ky]
        TS[...] = jnp.transpose(tile[:, 0:256].astype(F32)).astype(BF)

        def one(zq, _):
            s = nn(tile[:, 0:256], QT[zq]) * scale
            p = jnp.exp(jnp.where(allowed(kt, zq), s - MS[zq, 0:1, :], -1e30))
            dp = nn(tile[:, 128:384], DOT[zq])
            ds = (p * (dp - MS[zq, 1:2, :])).astype(BF)
            DK[...] += nn(ds, Q[zq])
            DV[...] += nn(p.astype(BF), DOs[zq])
            DQ[zq] += nn(TS[...], ds)
            return 0

        lax.fori_loop(zlo, zhi, one, 0)
        dk = DK[...] * scale
        dv = DV[...]
        KV[kh, kz, ky, :, 0:128] = dk[:, 0:128].astype(BF)
        KV[kh, kz, ky, :, 128:256] = (dk[:, 128:256] + dv[:, 0:128]).astype(BF)
        KV[kh, kz, ky, :, 256:384] = dv[:, 128:256].astype(BF)

    dk0, dk1, dk2 = {}, {}, {}
    turn = (1, 2, 3, 0)

    def far_tiles(k):
        kz = zs[k]
        key_tile(hx, kz, yx)
        dk1[k] = send(KV.at[hx, kz, yx], DKVr.at[1, kz], P2)
        key_tile(p2h, kz, p2y)
        dk0[k] = send(KV.at[p2h, kz, p2y], DKVr.at[0, kz], P2)

    def near_tile(k):
        kz = zs[k]
        key_tile(p1h, kz, p1y)
        dk1[k].wait_recv()
        KV[p1h, kz, p1y] = (KV[p1h, kz, p1y].astype(F32) + DKVr[1, kz].astype(F32)).astype(BF)
        dk2[k] = send(KV.at[p1h, kz, p1y], DKVr.at[2, kz], P1)

    def own_tile(kz, _):
        key_tile(h, kz, y)
        return 0

    rs_c(2)
    far_tiles(1)
    far_tiles(2)
    near_tile(1)
    far_tiles(3)
    near_tile(2)
    far_tiles(0)
    rs_b(1)
    near_tile(3)
    near_tile(0)
    rs_d(2)
    lax.fori_loop(0, 4, own_tile, 0)
    rs_b(0)

    def join(zt, _):
        dkv = KV[h, zt, y].astype(F32) + DKVr[0, zt].astype(F32) + DKVr[2, zt].astype(F32)
        dq = pltpu.roll(jnp.where(lane256 < 160, jnp.transpose(DQ[zt]) * scale, 0.0), 64, 1)
        DKVQ[zt, :, 0:256] = dkv[:, 0:256].astype(BF)
        DKVQ[zt, :, 256:384] = (dkv[:, 256:384] + dq[:, 0:128]).astype(BF)
        DKVQ[zt, :, 384:512] = dq[:, 128:256].astype(BF)
        return 0


    VS[...] = jnp.zeros((128, 512), F32)

    def first_grad(zt, _):
        d = DKVQ[zt]
        VS[98:99, :] += jnp.sum(d.astype(F32), axis=0, keepdims=True)

        def u_half(i, cols):
            u = nt(d, W[i].reshape(640, 512))
            VR[97:98, cols] += jnp.sum(u, axis=0, keepdims=True)
            U[zt, :, :, cols] = u.astype(BF).reshape(2, 128, 640)

        halves(u_half)

        return 0

    def gain_sum(i, _):
        zt = lax.div(i, 2)
        rows = pl.ds(pl.multiple_of(lax.rem(i, 2) * 64, 64), 64)
        n, _ = stats(T[zt, c, rows].astype(F32))
        VR[96:97, :] += jnp.sum(U[zt, c, rows].astype(F32) * n, axis=0, keepdims=True)
        return 0

    us, uz = {}, []

    def block_sum(k):
        us[k].wait_recv()
        zt = zs[k]
        U[zt, c] = (U[zt, c].astype(F32) + UR[zt].astype(F32)).astype(BF)
        if k:
            uz.append(send(U.at[zt, c], UZ.at[k - 1], dev(h, zt, y, c)))

    for i, k in enumerate(turn):
        dk0[k].wait_recv()
        dk2[k].wait_recv()
        join(zs[k], 0)
        first_grad(zs[k], 0)
        us[k] = send(U.at[zs[k], sib], UR.at[zs[k]], SIB)
        if i:
            block_sum(turn[i - 1])
        if i == 3:
            rs_c(1)
    block_sum(0)
    rs_c(0)
    lax.fori_loop(0, 8, gain_sum, 0)
    rs_e(2)
    rs_d(1)
    VS[99:100, :] = VS[98:99, :]
    vst = jnp.transpose(VS[...])
    vlane = lax.broadcasted_iota(jnp.int32, (160, 128), 1)
    colb[0:1280, :] = jnp.transpose(VR[...])
    rows = pl.ds(pl.multiple_of(t * 160, 8), 160)
    colb[rows, :] += jnp.where(vlane == 98, vst[320:480, :], 0.0) + jnp.where(
        vlane == 99, vst[160:320, :], 0.0
    )

    def head_grad(hh, _):
        g = tn(
            H[:, :, pl.ds(pl.multiple_of(hh * 640, 128), 640)].reshape(1024, 640),
            DKVQ[...].reshape(1024, 512),
        )
        DW[hh, :, :, :, 0:384] = g[:, 0:384].astype(BF).reshape(4, 2, 80, 384)
        last = g[:, 384:512] + colb[pl.ds(pl.multiple_of(hh * 640, 128), 640), :]
        DW[hh, :, :, :, 384:512] = last.astype(BF).reshape(4, 2, 80, 128)
        return 0

    lax.fori_loop(0, 2, head_grad, 0)
    dw1 = send(DW.at[hx, :, yx], DWr.at[1], P2)
    dw0 = send(DW.at[p2h, :, p2y], DWr.at[0], P2)
    rs_d(0)
    dw1.wait_recv()
    DW[p1h, :, p1y] = (DW[p1h, :, p1y].astype(F32) + DWr[1].astype(F32)).astype(BF)
    dw2 = send(DW.at[p1h, :, p1y], DWr.at[2], P1)
    dw0.wait_recv()
    dw2.wait_recv()
    left(wz)
    for k in range(4):
        DWz[k] = (
            DW[h, k, y].astype(F32) + DWr[0, k].astype(F32) + DWr[2, k].astype(F32)
        ).astype(BF)
    dwz = [send(DWz.at[zs[k]], DWh.at[z], dev(h, zs[k], y, c)) for k in range(1, 4)]
    DWh[z] = DWz[z]
    rs_e(1)
    rs_e(0)

    rx.wait_recv()
    pm = perm[pl.ds(h * 16 + b, 1), :]
    om0 = jnp.where(pm == b * 128 + i_sub, 1.0, 0.0).astype(BF)
    om1 = jnp.where(pm == (16 + b) * 128 + i_sub, 1.0, 0.0).astype(BF)

    def mix_half(i, cols):
        mixed_out[:, cols] = (tn(om0, RES[0, :, cols]) + tn(om1, RES[1, :, cols])).astype(BF)

    halves(mix_half)


    for cp in uz:
        cp.wait_recv()

    def last_rows(i, _):
        rows = pl.ds(pl.multiple_of(i * 32, 32), 32)
        u = U[z, c, rows].astype(F32)
        for k in range(3):
            u += UZ[k, rows].astype(F32)
        n, r = stats(tok[rows, :].astype(F32))
        wv = u * vec[0:1, :]
        gt = EX[rows, :] + r * (
            wv - jnp.mean(wv, axis=-1, keepdims=True) - n * jnp.mean(wv * n, axis=-1, keepdims=True)
        )
        gtok_out[rows, :] = gt.astype(BF)
        return 0

    lax.fori_loop(0, 4, last_rows, 0)

    for cp in dwz:
        cp.wait_recv()
    for k in range(4):
        wasm[k] = DWh[k].astype(F32)
    wr[...] = wasm[:, pl.ds(pl.multiple_of(sib * 40, 8), 40), :]
    wo = send(wr, WOr, SIB)
    left([wa])
    WP[c] = wasm[:, pl.ds(pl.multiple_of(c * 40, 8), 40), :]
    for w in (2, 1, 0):
        rs_f(w)
    wo.wait_recv()
    WP[sib] = WOr[...]
    total = jnp.zeros((40, 128), F32)
    for e in range(8):
        for i, dst in enumerate((gk, gv, gq)):
            dst[:, e * 160:(e + 1) * 160] = WP[e % 2, e // 2, :, i * 160:(i + 1) * 160]
        total += WP[e % 2, e // 2, :, 384:512]
    colb[0:40, :] = total
    vgo[...] = jnp.transpose(colb[0:128, :])[96:112, :]

    token_end()
    for cp in pending:
        cp.wait_send()

    assert count[0] <= NSEM, count[0]


NSEM = 192


def hand_over(*refs):
    n = len(refs) // 2
    sems = refs[-1]
    copies = [pltpu.make_async_copy(refs[i], refs[n + i], sems.at[i]) for i in range(n)]
    for cp in copies:
        cp.start()
    for cp in copies:
        cp.wait()


def fast_local(
    tokens, cotangent, permutation, seq_lengths, first_gain, first_bias, query_weight, query_bias,
    key_weight, value_weight, value_bias, output_weight, output_bias, second_gain, second_bias,
    expand_weight, expand_bias, contract_weight, contract_bias,
):
    vectors = [first_gain, first_bias, query_bias, value_bias, output_bias, second_gain, second_bias,
               expand_bias, contract_bias]
    vcol = jnp.pad(jnp.stack(vectors, axis=1).astype(F32), ((0, 0), (0, 23)))
    perm = permutation.reshape(32, 128)

    vm = pltpu.VMEM
    fshape = (2, 2, 4, 2, 80, 640)
    scratch = dict(
        WP=vm((2, 4, 40, 512), F32), FP=vm((2, 3, 40, 640), F32),
        T=vm((4, 2, 128, 1280), BF), H=vm((4, 256, 1280), BF), W=vm((2, 4, 2, 80, 512), BF),
        KV=vm((2, 4, 2, 256, 384), BF), Q=vm((4, 256, 256), BF), QT=vm((4, 256, 256), BF), OT=vm((4, 256, 256), F32),
        F=vm((3,) + fshape, BF), G=vm(fshape, BF), R0=vm((3, 2, 4, 2, 80, 640), BF),
        R1=vm((3, 2, 4, 80, 640), BF), R2=vm((3, 4, 80, 640), BF), R3=vm((3, 3, 80, 640), BF),
        FA=vm((3, 80, 640), F32), FR=vm((3, 40, 640), F32),
        wr=vm((4, 40, 512), F32), wasm=vm((4, 80, 512), F32),
        fr=vm((3, 40, 640), F32),
        colb=vm((1408, 128), F32), vec=vm((16, 1280), F32), bias=vm((8, 512), F32),
        MS=vm((4, 8, 256), F32), TS=vm((256, 256), BF),
        A=vm((8, 128, 256), BF), As=vm((4, 2, 128, 256), BF), C=vm((2, 128, 1280), BF),
        RES=vm((2, 128, 1280), BF), MID=vm((128, 1280), F32),
        EX=vm((128, 1280), F32), H2=vm((128, 1280), BF), ACT=vm((128, 1280), BF),
        CI=vm((128, 1280), BF), DE=vm((128, 1280), BF), GB=vm((128, 1280), BF),
        DOs=vm((4, 256, 256), BF), DOT=vm((4, 256, 256), BF), DOr=vm((4, 2, 128, 256), BF),
        DK=vm((256, 256), F32), DV=vm((256, 256), F32), DQ=vm((4, 256, 256), F32),
        DKVr=vm((3, 4, 256, 384), BF), DKVQ=vm((4, 256, 512), BF), U=vm((4, 2, 128, 1280), BF),
        UR=vm((4, 128, 1280), BF), UZ=vm((3, 128, 1280), BF), VR=vm((128, 1280), F32),
        VS=vm((128, 512), F32), DW=vm((2, 4, 2, 80, 512), BF),
        DWr=vm((3, 4, 80, 512), BF), DWz=vm((4, 80, 512), BF), DWh=vm((4, 80, 512), BF),
        WOr=vm((4, 40, 512), F32),
        ss=pltpu.SemaphoreType.DMA((NSEM,)), rs=pltpu.SemaphoreType.DMA((NSEM,)),
        lss=pltpu.SemaphoreType.DMA((5,)), lrs=pltpu.SemaphoreType.DMA((4,)),
    )
    vspec = pl.BlockSpec(memory_space=pltpu.VMEM)
    rows = jax.ShapeDtypeStruct((40, 1280), F32)
    tokens_out = jax.ShapeDtypeStruct((128, 1280), BF)
    mixed, gtok, gq, gk, gv, go, ge, gc, vg = pl.pallas_call(
        block_kernel,
        out_shape=(tokens_out, tokens_out) + (rows,) * 6 + (jax.ShapeDtypeStruct((16, 128), F32),),
        in_specs=[vspec, vspec, vspec, pl.BlockSpec(memory_space=pltpu.SMEM)] + [vspec] * 7,
        out_specs=(vspec,) * 9,
        scratch_shapes=list(scratch.values()),
        compiler_params=pltpu.CompilerParams(
            collective_id=0, has_side_effects=True, vmem_limit_bytes=63 * MB,
        ),
        cost_estimate=pl.CostEstimate(flops=12_000_000_000, bytes_accessed=6_000_000, transcendentals=5_000_000),
        name="block",
    )(tokens, cotangent, perm, seq_lengths, vcol, query_weight, key_weight, value_weight, output_weight,
      expand_weight, contract_weight)
    any_spec = pl.BlockSpec(memory_space=pl.ANY)
    mixed, gtok, gq, gk, gv, go, ge, gc = pl.pallas_call(
        hand_over,
        out_shape=(tokens_out, tokens_out) + (rows,) * 6,
        in_specs=[vspec] * 8,
        out_specs=(any_spec,) * 8,
        scratch_shapes=[pltpu.SemaphoreType.DMA((8,))],
        name="hand_over",
    )(mixed, gtok, gq, gk, gv, go, ge, gc)
    v = [vg[j, 0:40] for j in range(9)]
    return mixed, gtok, v[0], v[1], gq, v[2], gk, gv, v[3], go, v[4], v[5], v[6], ge, v[7], gc, v[8]


def shifted(array, axis, by):
    length = lax.axis_size(axis)
    return lax.ppermute(array, axis, [(i, (i + by) % length) for i in range(length)])


def normalize(values, gain, shift):
    centre = jnp.mean(values, axis=-1, keepdims=True)
    spread = jnp.mean((values - centre) ** 2, axis=-1, keepdims=True)
    return (values - centre) * lax.rsqrt(spread + 1e-05) * gain + shift


def exact_gelu(values):
    return jax.nn.gelu(values, approximate=False)


def layout_initial(permutation, blk_source, width, blk_count, head_count):
    rows = jnp.arange(width * head_count, dtype=jnp.int32)
    places = (rows // width * blk_count + blk_source) * width + rows % width
    return jnp.take(permutation, places)


def segment_of(initial, ends):
    return jnp.sum((initial[:, None] >= ends[None, :]).astype(jnp.int32), axis=1)


def permitted(query_orig, key_orig, ends):
    same = segment_of(query_orig, ends)[:, None] == segment_of(key_orig, ends)[None, :]
    return same & (key_orig[None, :] <= query_orig[:, None])


def outer_sum(left, right):
    return lax.dot_general(
        left, right, (((0,), (0,)), ((), ())), preferred_element_type=jnp.float32
    )


def back_product(left, right):
    return lax.dot_general(
        left, right, (((1,), (1,)), ((), ())), preferred_element_type=jnp.float32
    )


def block_terms(
    query_block,
    grad_block,
    log_block,
    agree_block,
    query_orig,
    key_block,
    value_block,
    key_orig,
    ends,
    scale,
):
    allowed = permitted(query_orig, key_orig, ends)
    scores = (
        jnp.einsum("qhd,khd->hqk", query_block, key_block, preferred_element_type=jnp.float32)
        * scale
    )
    weights = jnp.exp(jnp.where(allowed[None], scores - log_block[..., None], -1e30))
    value_term = jnp.einsum(
        "hqk,qhd->khd", weights.astype(jnp.bfloat16), grad_block, preferred_element_type=jnp.float32
    )
    product = jnp.einsum(
        "qhd,khd->hqk", grad_block, value_block, preferred_element_type=jnp.float32
    )
    score_grad = (weights * (product - agree_block[..., None])).astype(jnp.bfloat16)
    query_term = jnp.einsum(
        "hqk,khd->qhd", score_grad, key_block, preferred_element_type=jnp.float32
    )
    key_term = jnp.einsum(
        "hqk,qhd->khd", score_grad, query_block, preferred_element_type=jnp.float32
    )
    return (query_term, key_term, value_term)


def local(
    tokens,
    cotangent,
    permutation,
    seq_lengths,
    first_gain,
    first_bias,
    query_weight,
    query_bias,
    key_weight,
    value_weight,
    value_bias,
    output_weight,
    output_bias,
    second_gain,
    second_bias,
    expand_weight,
    expand_bias,
    contract_weight,
    contract_bias,
):
    width = tokens.shape[0]
    blk_count = lax.axis_size("blk")
    head_count = lax.axis_size("head")
    blk_index = lax.axis_index("blk")
    flat_index = lax.axis_index("head") * blk_count + blk_index
    count = seq_lengths.shape[0]
    before = jnp.arange(count)[None, :] <= jnp.arange(count)[:, None]
    ends = jnp.sum(jnp.where(before, seq_lengths[None, :], 0), axis=1)
    total = permutation.shape[0]
    numbers = jnp.arange(total, dtype=jnp.int32)
    inverse = jnp.zeros((total,), jnp.int32).at[permutation].set(numbers)
    local_rows = jnp.arange(width, dtype=jnp.int32)
    first_row = flat_index * width
    going = lax.dynamic_slice_in_dim(inverse, first_row, width)
    order_source = jnp.argsort(going)
    arriving = lax.dynamic_slice_in_dim(permutation, first_row, width)
    order_target = jnp.argsort(arriving // width // blk_count * width + local_rows)
    undo_target = jnp.argsort(order_target)
    undo_source = jnp.argsort(order_source)
    received = lax.all_to_all(
        jnp.take(tokens, order_source, axis=0), "head", split_axis=0, concat_axis=0, tiled=True
    )
    inputs = jnp.take(received, undo_target, axis=0).astype(jnp.float32)
    vectors = jnp.stack(
        [
            first_gain,
            first_bias,
            query_bias,
            value_bias,
            output_bias,
            second_gain,
            second_bias,
            expand_bias,
            contract_bias,
        ]
    )
    query_full, key_full, value_full, output_full, expand_full, contract_full, vector_stack = (
        lax.all_gather(query_weight, ("head", "blk"), axis=0, tiled=True),
        lax.all_gather(key_weight, ("head", "blk"), axis=0, tiled=True),
        lax.all_gather(value_weight, ("head", "blk"), axis=0, tiled=True),
        lax.all_gather(output_weight, ("head", "blk"), axis=0, tiled=True),
        lax.all_gather(expand_weight, ("head", "blk"), axis=0, tiled=True),
        lax.all_gather(contract_weight, ("head", "blk"), axis=0, tiled=True),
        lax.all_gather(vectors, ("head", "blk"), axis=1, tiled=True),
    )
    vector_full = vector_stack.astype(jnp.float32)
    first_hidden = normalize(inputs, vector_full[0], vector_full[1]).astype(jnp.bfloat16)
    queries = (
        jnp.dot(first_hidden, query_full, preferred_element_type=jnp.float32) + vector_full[2]
    ).astype(jnp.bfloat16)
    keys = jnp.dot(first_hidden, key_full, preferred_element_type=jnp.float32).astype(jnp.bfloat16)
    values = (
        jnp.dot(first_hidden, value_full, preferred_element_type=jnp.float32) + vector_full[3]
    ).astype(jnp.bfloat16)
    head_queries, head_keys, head_values = (
        lax.all_to_all(queries, "head", split_axis=1, concat_axis=0, tiled=True),
        lax.all_to_all(keys, "head", split_axis=1, concat_axis=0, tiled=True),
        lax.all_to_all(values, "head", split_axis=1, concat_axis=0, tiled=True),
    )
    rows_here = width * head_count
    feature_here = head_queries.shape[1]
    heads_here = feature_here // HEAD_DIM
    scale = HEAD_DIM ** (-0.5)
    query_initial = layout_initial(permutation, blk_index, width, blk_count, head_count)
    shaped_queries = head_queries.reshape(rows_here, heads_here, HEAD_DIM)
    shaped_keys = head_keys.reshape(rows_here, heads_here, HEAD_DIM)
    shaped_values = head_values.reshape(rows_here, heads_here, HEAD_DIM)
    start_state = (
        jnp.full((heads_here, rows_here), -1e30, jnp.float32),
        jnp.zeros((heads_here, rows_here), jnp.float32),
        jnp.zeros((heads_here, rows_here, HEAD_DIM), jnp.float32),
    )
    carry = start_state
    key_piece = lax.all_gather(head_keys, "blk", axis=0, tiled=True)
    value_piece = lax.all_gather(head_values, "blk", axis=0, tiled=True)
    pieces = key_piece.shape[0] // rows_here
    key_blocks = key_piece.reshape(pieces, rows_here, heads_here, HEAD_DIM)
    value_blocks = value_piece.reshape(pieces, rows_here, heads_here, HEAD_DIM)

    def visit(state, item):
        key_block, value_block, offset = item
        running, total_sum, gathered = state
        key_initial = layout_initial(permutation, offset, width, blk_count, head_count)
        allowed = permitted(query_initial, key_initial, ends)
        scores = (
            jnp.einsum(
                "qhd,khd->hqk", shaped_queries, key_block, preferred_element_type=jnp.float32
            )
            * scale
        )
        scores = jnp.where(allowed[None], scores, -1e30)
        newest = jnp.maximum(running, jnp.max(scores, axis=-1))
        factor = jnp.exp(running - newest)
        exponent = jnp.where(allowed[None], jnp.exp(scores - newest[..., None]), 0.0)
        total_sum = factor * total_sum + jnp.sum(exponent, axis=-1)
        gathered = factor[..., None] * gathered + jnp.einsum(
            "hqk,khd->hqd",
            exponent.astype(jnp.bfloat16),
            value_block,
            preferred_element_type=jnp.float32,
        )
        return ((newest, total_sum, gathered), None)

    carry, unused = lax.scan(
        visit, carry, (key_blocks, value_blocks, jnp.arange(pieces, dtype=jnp.int32))
    )
    running, total_sum, gathered = carry
    attended = gathered / total_sum[..., None]
    log_total = running + jnp.log(total_sum)
    attended_rows = jnp.transpose(attended, (1, 0, 2)).reshape(rows_here, feature_here)
    merged = lax.all_to_all(
        attended_rows.astype(jnp.bfloat16), "head", split_axis=0, concat_axis=1, tiled=True
    )
    middle = (
        inputs + jnp.dot(merged, output_full, preferred_element_type=jnp.float32) + vector_full[4]
    )
    second_hidden = normalize(middle, vector_full[5], vector_full[6]).astype(jnp.bfloat16)
    expanded = (
        jnp.dot(second_hidden, expand_full, preferred_element_type=jnp.float32) + vector_full[7]
    )
    activated = exact_gelu(expanded).astype(jnp.bfloat16)
    result = (
        middle
        + jnp.dot(activated, contract_full, preferred_element_type=jnp.float32)
        + vector_full[8]
    )
    grad_contract = outer_sum(activated, cotangent)
    grad_contract_bias = jnp.sum(cotangent.astype(jnp.float32), axis=0)
    grad_activated = back_product(cotangent, contract_full)
    unused_value, gelu_pull = jax.vjp(exact_gelu, expanded)
    grad_expanded = gelu_pull(grad_activated)[0].astype(jnp.bfloat16)
    grad_expand = outer_sum(second_hidden, grad_expanded)
    grad_expand_bias = jnp.sum(grad_expanded.astype(jnp.float32), axis=0)
    grad_second = back_product(grad_expanded, expand_full)
    unused_second, second_pull = jax.vjp(normalize, middle, vector_full[5], vector_full[6])
    grad_middle_norm, grad_second_gain, grad_second_bias = second_pull(grad_second)
    grad_middle = cotangent.astype(jnp.float32) + grad_middle_norm
    grad_branch = grad_middle.astype(jnp.bfloat16)
    grad_output = outer_sum(merged, grad_branch)
    grad_output_bias = jnp.sum(grad_branch.astype(jnp.float32), axis=0)
    grad_merged = back_product(grad_branch, output_full).astype(jnp.bfloat16)
    head_grad = lax.all_to_all(grad_merged, "head", split_axis=1, concat_axis=0, tiled=True)
    shaped_grad = head_grad.reshape(rows_here, heads_here, HEAD_DIM)
    agreement = jnp.einsum("qhd,hqd->hq", shaped_grad.astype(jnp.float32), attended)
    zero_rows = jnp.zeros((rows_here, heads_here, HEAD_DIM), jnp.float32)

    def key_turn(turn, state):
        moving_keys, moving_values, key_total, value_total, query_total = state
        source = (blk_index - turn) % blk_count
        key_orig = layout_initial(permutation, source, width, blk_count, head_count)
        query_term, key_term, value_term = block_terms(
            shaped_queries,
            shaped_grad,
            log_total,
            agreement,
            query_initial,
            moving_keys,
            moving_values,
            key_orig,
            ends,
            scale,
        )
        moving_keys, moving_values = shifted((moving_keys, moving_values), "blk", 1)
        key_total, value_total = (
            shifted((key_total + key_term).astype(jnp.bfloat16), "blk", 1).astype(jnp.float32),
            shifted((value_total + value_term).astype(jnp.bfloat16), "blk", 1).astype(jnp.float32),
        )
        return (moving_keys, moving_values, key_total, value_total, query_total + query_term)

    final_state = lax.fori_loop(
        0, blk_count, key_turn, (shaped_keys, shaped_values, zero_rows, zero_rows, zero_rows)
    )
    key_grad_heads = final_state[2]
    value_grad_heads = final_state[3]
    query_grad_heads = final_state[4]
    query_grad_rows = (
        (query_grad_heads * scale).astype(jnp.bfloat16).reshape(rows_here, feature_here)
    )
    key_grad_rows = (key_grad_heads * scale).astype(jnp.bfloat16).reshape(rows_here, feature_here)
    value_grad_rows = value_grad_heads.astype(jnp.bfloat16).reshape(rows_here, feature_here)
    grad_queries, grad_keys, grad_values = (
        lax.all_to_all(query_grad_rows, "head", split_axis=0, concat_axis=1, tiled=True),
        lax.all_to_all(key_grad_rows, "head", split_axis=0, concat_axis=1, tiled=True),
        lax.all_to_all(value_grad_rows, "head", split_axis=0, concat_axis=1, tiled=True),
    )
    grad_query = outer_sum(first_hidden, grad_queries)
    grad_key = outer_sum(first_hidden, grad_keys)
    grad_value = outer_sum(first_hidden, grad_values)
    grad_query_bias = jnp.sum(grad_queries.astype(jnp.float32), axis=0)
    grad_value_bias = jnp.sum(grad_values.astype(jnp.float32), axis=0)
    grad_first = (
        back_product(grad_queries, query_full)
        + back_product(grad_keys, key_full)
        + back_product(grad_values, value_full)
    )
    unused_first, first_pull = jax.vjp(normalize, inputs, vector_full[0], vector_full[1])
    grad_inputs_norm, grad_first_gain, grad_first_bias = first_pull(grad_first)
    grad_inputs = (grad_middle + grad_inputs_norm).astype(jnp.bfloat16)
    vector_grads = jnp.stack(
        [
            grad_first_gain,
            grad_first_bias,
            grad_query_bias,
            grad_value_bias,
            grad_output_bias,
            grad_second_gain,
            grad_second_bias,
            grad_expand_bias,
            grad_contract_bias,
        ]
    )
    summed = (
        lax.psum_scatter(grad_query, ("head", "blk"), scatter_dimension=0, tiled=True),
        lax.psum_scatter(grad_key, ("head", "blk"), scatter_dimension=0, tiled=True),
        lax.psum_scatter(grad_value, ("head", "blk"), scatter_dimension=0, tiled=True),
        lax.psum_scatter(grad_output, ("head", "blk"), scatter_dimension=0, tiled=True),
        lax.psum_scatter(grad_expand, ("head", "blk"), scatter_dimension=0, tiled=True),
        lax.psum_scatter(grad_contract, ("head", "blk"), scatter_dimension=0, tiled=True),
        lax.psum_scatter(vector_grads, ("head", "blk"), scatter_dimension=1, tiled=True),
    )
    vector_shares = summed[6]
    returned = lax.all_to_all(
        jnp.take(grad_inputs, order_target, axis=0), "head", split_axis=0, concat_axis=0, tiled=True
    )
    grad_tokens = jnp.take(returned, undo_source, axis=0)
    return (
        result.astype(jnp.bfloat16),
        grad_tokens,
        vector_shares[0],
        vector_shares[1],
        summed[0],
        vector_shares[2],
        summed[1],
        summed[2],
        vector_shares[3],
        summed[3],
        vector_shares[4],
        vector_shares[5],
        vector_shares[6],
        summed[4],
        vector_shares[7],
        summed[5],
        vector_shares[8],
    )


def solution(mesh):
    return jax.shard_map(
        fast_local if mesh.shape["head"] == 2 and mesh.shape["blk"] == 16 else local,
        mesh=mesh,
        in_specs=(
            P(("head", "blk"), None),
            P(("head", "blk"), None),
            P(),
            P(),
            P(("head", "blk")),
            P(("head", "blk")),
            P(("head", "blk"), None),
            P(("head", "blk")),
            P(("head", "blk"), None),
            P(("head", "blk"), None),
            P(("head", "blk")),
            P(("head", "blk"), None),
            P(("head", "blk")),
            P(("head", "blk")),
            P(("head", "blk")),
            P(("head", "blk"), None),
            P(("head", "blk")),
            P(("head", "blk"), None),
            P(("head", "blk")),
        ),
        out_specs=(
            P(("head", "blk"), None),
            P(("head", "blk"), None),
            P(("head", "blk")),
            P(("head", "blk")),
            P(("head", "blk"), None),
            P(("head", "blk")),
            P(("head", "blk"), None),
            P(("head", "blk"), None),
            P(("head", "blk")),
            P(("head", "blk"), None),
            P(("head", "blk")),
            P(("head", "blk")),
            P(("head", "blk")),
            P(("head", "blk"), None),
            P(("head", "blk")),
            P(("head", "blk"), None),
            P(("head", "blk")),
        ),
        check_vma=False,
    )
```
